32 devices in a mesh: len: 8 (over y, x, core), wid: 4 (over z).
Axes of the slice: x: 2, y: 2, z: 4, core: 2. Of those that a mesh axis runs over, the one named last changes fastest.
Arguments:
- prior_heat_level: float32 [32, 1024, 1024], P(None, 'wid', 'len'), may hold values from -6 to 6
- spanwise_diffusivity_number: float32 [32, 1024], P(None, 'len'), may hold values from 30 to 8000
- planar_speed_vector: float32 [2, 32, 1024, 1024], P(None, None, 'wid', 'len'), may hold values from -4 to 4
- driving_load_vector: float32 [2, 32, 1024, 1024], P(None, None, 'wid', 'len'), may hold values from -6 to 6
- pinned_indicator: int32 [32, 1024, 1024], P(None, 'wid', 'len'), may hold values 0 or 1
Outputs:
- heated: float32 [32, 1024, 1024], P(None, 'wid', 'len')
- flow: float32 [2, 32, 1024, 1024], P(None, None, 'wid', 'len')
The draws below stay inside these ranges and needn't reach their ends.
All inputs are finite; a program needn't handle non-finite values. No bound on the sum of `pinned_indicator` on one device may be relied on, other than what follows from the above.
Results may differ from the reference program's by a relative error of at most 0.0008.
Values sent between devices are 32-bit elements; how exact they have to be, the bound alone decides.
No kernel may reach another device: no remote copies, remote signals or barrier semaphores. Data moves between devices by JAX's collectives and lax.ppermute only.
A program may use at most 192 MiB of HBM per device.

```python
import math
import jax
import jax.numpy as jnp
from jax import lax

SPANWISE_COUNT = 1024
DEPTH_COUNT = 32
DOWNSTREAM_COUNT = 1024


def draw_prior_heat_level(key, part):
    key = jax.random.fold_in(key, 11)
    key_noise = jax.random.fold_in(key, 1)
    key_span = jax.random.fold_in(key, 2)
    noise_shape = (DEPTH_COUNT, SPANWISE_COUNT + 7, DOWNSTREAM_COUNT)
    noise_draw = jax.random.normal(key_noise, noise_shape, jnp.float32)
    window_len = jax.random.randint(key_span, (DEPTH_COUNT, 1, DOWNSTREAM_COUNT), 4, 9)
    running = jnp.zeros((DEPTH_COUNT, SPANWISE_COUNT, DOWNSTREAM_COUNT), jnp.float32)
    for offset in range(8):
        inside_window = (window_len > offset).astype(jnp.float32)
        running = running + inside_window * noise_draw[:, offset:offset + SPANWISE_COUNT, :]
    heat_field = 1.5 * running / jnp.sqrt(window_len.astype(jnp.float32))
    return jnp.clip(heat_field, -6.0, 6.0)


def plant(array, key, low, top_value):
    index_at = [jax.random.randint(jax.random.fold_in(key, axis), (), 0, length) for axis, length in enumerate(array.shape)]
    main_axis = array.shape.index(max(array.shape))
    beside = index_at[:main_axis] + [(index_at[main_axis] + 1) % array.shape[main_axis]] + index_at[main_axis + 1:]
    return array.at[tuple(index_at)].set(low).at[tuple(beside)].set(top_value)


def level_of(rng, dims, shards, least, high):
    def one(position, blocks):
        heights = jax.random.uniform(jax.random.fold_in(jax.random.fold_in(rng, 6), position), (blocks,), jnp.float32, least / len(shards), high / len(shards))
        return jnp.repeat(jnp.exp(heights), dims[position] // blocks).reshape((-1,) + (1,) * (len(dims) - position - 1))

    factor_of = one(*shards[0])
    for cut in shards[1:]:
        factor_of = factor_of * one(*cut)
    return factor_of


def noise(rng, shape, deviation, bound, cuts=(), held_as=jnp.bfloat16):
    gain = level_of(rng, shape, cuts, -0.22, 0.18) if cuts else 1.0
    entries = jax.random.normal(rng, shape, jnp.float32) * deviation * gain
    return jnp.minimum(jnp.maximum(entries, -bound), bound).astype(held_as)


def setup_inputs(seed: int = 0) -> dict:
    key_of = jax.random.split(jax.random.key(seed), 6)
    prior_heat_level = draw_prior_heat_level(jax.random.fold_in(key_of[5], 71), 0)
    spanwise_diffusivity_number = jnp.clip(jnp.exp(math.log(8000.0) - 5.5859994 * jax.random.uniform(key_of[1], (DEPTH_COUNT, DOWNSTREAM_COUNT), jnp.float32) ** level_of(key_of[1], (DEPTH_COUNT, DOWNSTREAM_COUNT), ((1, 8),), -0.2, 0.2)), 30.0, 8000.0)
    planar_speed_vector = noise(key_of[2], (2, DEPTH_COUNT, SPANWISE_COUNT, DOWNSTREAM_COUNT), 0.5, 4.0, ((2, 4), (3, 8)), jnp.float32)
    driving_load_vector = noise(key_of[3], (2, DEPTH_COUNT, SPANWISE_COUNT, DOWNSTREAM_COUNT), 1.0, 6.0, ((2, 4), (3, 8)), jnp.float32)
    pinned_indicator = plant((jax.random.randint(key_of[4], (DEPTH_COUNT, SPANWISE_COUNT, DOWNSTREAM_COUNT), 0, 8) < 1).astype(jnp.int32), jax.random.fold_in(key_of[4], 1), 0, 1)
    return {"prior_heat_level": prior_heat_level, "spanwise_diffusivity_number": spanwise_diffusivity_number, "planar_speed_vector": planar_speed_vector, "driving_load_vector": driving_load_vector, "pinned_indicator": pinned_indicator}


DRAG_COEFF = 0.5
RELAX_FACTOR = 0.8

def tables(full_width):
    freq = jnp.arange(full_width, dtype=jnp.float32)
    cells = jnp.arange(full_width, dtype=jnp.float32) + 0.5
    factor = jnp.where(freq == 0, jnp.sqrt(1.0 / full_width), jnp.sqrt(2.0 / full_width)).astype(jnp.float32)
    precomputed_chart = factor[:, None] * jnp.cos(jnp.pi * freq[:, None] * cells[None, :] / full_width)
    eigen_values = 2.0 - 2.0 * jnp.cos(jnp.pi * freq / full_width)
    return (precomputed_chart, eigen_values)

def relaxation(padded, driving_load_vector, viscosity, holding):
    centre = padded[:, :, 1:-1, 1:-1]
    beside = padded[:, :, 2:, 1:-1] + padded[:, :, :-2, 1:-1] + padded[:, :, 1:-1, 2:] + padded[:, :, 1:-1, :-2]
    cross_term = 0.25 * (padded[:, :, 2:, 2:] - padded[:, :, 2:, :-2] - padded[:, :, :-2, 2:] + padded[:, :, :-2, :-2])
    cross_term = cross_term[::-1]
    target = (driving_load_vector + viscosity * (beside + cross_term)) / (DRAG_COEFF + 4.0 * viscosity)
    relaxed = centre + RELAX_FACTOR * (target - centre)
    return holding * centre + (1.0 - holding) * relaxed

def reference(prior_heat_level, spanwise_diffusivity_number, planar_speed_vector, driving_load_vector, pinned_indicator):
    precomputed_chart, eigen_values = tables(SPANWISE_COUNT)
    harmonic_eigenvalue_set = jnp.einsum('oe,qed->qod', precomputed_chart, prior_heat_level, precision=lax.Precision.HIGHEST)
    harmonic_eigenvalue_set = harmonic_eigenvalue_set / (1.0 + spanwise_diffusivity_number[:, None, :] * eigen_values[None, :, None])
    heated = jnp.einsum('kw,tkl->twl', precomputed_chart, harmonic_eigenvalue_set, precision=lax.Precision.HIGHEST)
    viscosity = jnp.exp(-0.5 * heated)
    holding = pinned_indicator.astype(jnp.float32)
    for sweep_count in range(2):
        padded = jnp.pad(planar_speed_vector, ((0, 0), (0, 0), (1, 1), (1, 1)))
        planar_speed_vector = relaxation(padded, driving_load_vector, viscosity, holding)
    return (heated, planar_speed_vector)
```

```python
import functools

import jax
import jax.numpy as jnp
from jax import lax
from jax.experimental import pallas as pl
from jax.experimental.pallas import tpu as pltpu
from jax.sharding import PartitionSpec as P

DRAG_COEFF = 0.5
RELAX_FACTOR = 0.8
F32 = jnp.float32
MIB = 1 << 20


def decay(d):
    x = 1.0 / d
    one_less = jnp.sqrt(x + 0.25 * x * x) - 0.5 * x
    r = 1.0 - one_less
    return r, (1.0 - r) / (1.0 + r)


def power(r, n):
    out = None
    while n:
        if n & 1:
            out = r if out is None else out * r
        n >>= 1
        if n:
            r = r * r
    return out


def sublane_powers(r, shape):
    s = lax.broadcasted_iota(jnp.int32, shape, 0)
    r2 = r * r
    r4 = r2 * r2
    one = jnp.ones(shape, F32)
    return (
        jnp.where((s & 1) != 0, r, one)
        * jnp.where((s & 2) != 0, r2, one)
        * jnp.where((s & 4) != 0, r4, one)
    )


def iotas():
    lane = lax.broadcasted_iota(jnp.int32, (8, 128), 1)
    sub = lax.broadcasted_iota(jnp.int32, (8, 128), 0)
    return lane, sub


def moments_kernel(tb, n, d_ref, f_ref, seg_ref, pq_ref):
    S = n // 8
    base = pl.program_id(0) * tb
    G = 4
    for g in range(tb // G):
        rs = []
        for u in range(G):
            r, _ = decay(d_ref[pl.ds(base + g * G + u, 1), :])
            rs.append(jnp.broadcast_to(r, (8, 128)))
        fwd = [None] * G
        bwd = [None] * G
        for i in range(S):
            for u in range(G):
                a = f_ref[g * G + u, pl.ds(i, 8, stride=S), :]
                b = f_ref[g * G + u, pl.ds(S - 1 - i, 8, stride=S), :]
                fwd[u] = a if i == 0 else fwd[u] * rs[u] + a
                bwd[u] = b if i == 0 else bwd[u] * rs[u] + b
        for u in range(G):
            k = g * G + u
            seg_ref[0, k] = fwd[u]
            seg_ref[1, k] = bwd[u]
            rS = power(rs[u], S)
            up = sublane_powers(rS, (8, 128))
            s = lax.broadcasted_iota(jnp.int32, (8, 128), 0)
            rS2 = rS * rS
            one = jnp.ones((8, 128), F32)
            down = (
                jnp.where((s & 1) == 0, rS, one)
                * jnp.where((s & 2) == 0, rS2, one)
                * jnp.where((s & 4) == 0, rS2 * rS2, one)
            )
            pq_ref[0, k : k + 1, :] = jnp.sum(fwd[u] * down, axis=0, keepdims=True)
            pq_ref[1, k : k + 1, :] = jnp.sum(bwd[u] * up, axis=0, keepdims=True)


def moments(d, prior):
    T, n, _ = prior.shape
    tb = 8
    return pl.pallas_call(
        functools.partial(moments_kernel, tb, n),
        grid=(T // tb,),
        in_specs=[
            pl.BlockSpec((T, 128), lambda t: (0, 0)),
            pl.BlockSpec((tb, n, 128), lambda t: (t, 0, 0)),
        ],
        out_specs=[
            pl.BlockSpec((2, tb, 8, 128), lambda t: (0, t, 0, 0)),
            pl.BlockSpec((2, tb, 128), lambda t: (0, t, 0)),
        ],
        out_shape=[
            jax.ShapeDtypeStruct((2, T, 8, 128), F32),
            jax.ShapeDtypeStruct((2, T, 128), F32),
        ],
        compiler_params=pltpu.CompilerParams(vmem_limit_bytes=16 * MIB),
        cost_estimate=pl.CostEstimate(flops=4 * T * n * 128, bytes_accessed=4 * T * n * 128, transcendentals=0),
        name="moments",
    )(d, prior)


def pack_kernel(tb, n, v_ref, f_ref, p_ref, pk_ref, lo_ref, hi_ref):
    base = pl.program_id(0) * tb
    lane = lax.broadcasted_iota(jnp.int32, (n, 128), 1)
    group = lane >> 2
    for k in range(5):
        acc = pk_ref[k]
        for u in range(tb):
            if k < 2:
                x = v_ref[k, u]
            elif k < 4:
                x = f_ref[k - 2, u]
            else:
                x = 1.0 - p_ref[u].astype(F32)
            t = base + u
            acc = jnp.where(group == t, pltpu.roll(x, (4 * t + 2) & 127, 1), acc)
        pk_ref[k] = acc
    for u in range(tb):
        for ref, a, e in ((lo_ref, 0, 0), (hi_ref, n - 2, n - 1)):
            ref[u, 0:2, :] = v_ref[0, u, a : a + 2, :]
            ref[u, 2:4, :] = v_ref[1, u, a : a + 2, :]
            ref[u, 4:5, :] = f_ref[0, u, e : e + 1, :]
            ref[u, 5:6, :] = f_ref[1, u, e : e + 1, :]
            ref[u, 6:7, :] = 1.0 - p_ref[u, e : e + 1, :].astype(F32)
            ref[u, 7:8, :] = jnp.zeros((1, 128), F32)


def pack(v, f, pinned):
    _, T, n, _ = v.shape
    tb = 4
    row = jax.ShapeDtypeStruct((T, 8, 128), F32)
    return pl.pallas_call(
        functools.partial(pack_kernel, tb, n),
        grid=(T // tb,),
        in_specs=[
            pl.BlockSpec((2, tb, n, 128), lambda t: (0, t, 0, 0)),
            pl.BlockSpec((2, tb, n, 128), lambda t: (0, t, 0, 0)),
            pl.BlockSpec((tb, n, 128), lambda t: (t, 0, 0)),
        ],
        out_specs=[
            pl.BlockSpec((5, n, 128), lambda t: (0, 0, 0)),
            pl.BlockSpec((tb, 8, 128), lambda t: (t, 0, 0)),
            pl.BlockSpec((tb, 8, 128), lambda t: (t, 0, 0)),
        ],
        out_shape=[jax.ShapeDtypeStruct((5, n, 128), F32), row, row],
        compiler_params=pltpu.CompilerParams(vmem_limit_bytes=24 * MIB),
        cost_estimate=pl.CostEstimate(flops=5 * T * n * 128, bytes_accessed=20 * T * n * 128, transcendentals=0),
        name="pack_edges",
    )(v, f, pinned)


def heat_kernel(
    J, tb, n, d_ref, all_ref, seg_ref, f_ref, pk_ref, lo7_ref, hi7_ref,
    out_ref, right_ref, left_ref, lo_ref, hi_ref, sums, pkh, ys,
):
    S = n // 8
    T = d_ref.shape[0]
    step = pl.program_id(0)
    base = step * tb

    @pl.when(step == 0)
    def _():
        j = lax.axis_index("wid")
        r, _ = decay(d_ref[...])
        rn = power(r, n)
        rN = power(rn, J)
        sp = all_ref[0, 0]
        for i in range(1, J):
            sp = sp * rn + all_ref[i, 0]
        sq = all_ref[J - 1, 1]
        for i in range(J - 2, -1, -1):
            sq = sq * rn + all_ref[i, 1]
        inv = 1.0 / (1.0 - rN * rN)
        left = (sq + rN * sp) * inv
        right = (sp + rN * sq) * inv
        for i in range(J - 1):
            left = jnp.where(i < j, rn * left + all_ref[i, 0], left)
        for i in range(J - 1, 0, -1):
            right = jnp.where(i > j, rn * right + all_ref[i, 1], right)
        sums[0] = left
        sums[1] = right

    _, sub = iotas()
    rs, gain, y, z = [], [], [], []
    for u in range(tb):
        t = base + u
        r, a0 = decay(d_ref[pl.ds(t, 1), :])
        r = jnp.broadcast_to(r, (8, 128))
        a0 = jnp.broadcast_to(a0, (8, 128))
        rS = power(r, S)
        rS2 = rS * rS
        rS4 = rS2 * rS2
        c = jnp.where(sub == 0, sums[0, pl.ds(t, 1), :], pltpu.roll(seg_ref[0, u], 1, 0))
        b = jnp.where(sub == 7, sums[1, pl.ds(t, 1), :], pltpu.roll(seg_ref[1, u], 7, 0))
        for s, q in ((1, rS), (2, rS2), (4, rS4)):
            c = c + q * jnp.where(sub >= s, pltpu.roll(c, s, 0), 0.0)
            b = b + q * jnp.where(sub < 8 - s, pltpu.roll(b, 8 - s, 0), 0.0)
        rs.append(r)
        gain.append(a0)
        y.append(c)
        z.append(b)
    for i in range(S):
        for u in range(tb):
            y[u] = y[u] * rs[u] + f_ref[u, pl.ds(i, 8, stride=S), :]
            ys[u, i] = y[u]
    for i in range(S - 1, -1, -1):
        for u in range(tb):
            zr = z[u] * rs[u]
            out_ref[u, pl.ds(i, 8, stride=S), :] = gain[u] * (ys[u, i] + zr)
            z[u] = zr + f_ref[u, pl.ds(i, 8, stride=S), :]

    lane_n = lax.broadcasted_iota(jnp.int32, (n, 128), 1)
    group = lane_n >> 2
    acc = pkh[...]
    for u in range(tb):
        t = base + u
        acc = jnp.where(group == t, pltpu.roll(out_ref[u], (4 * t + 2) & 127, 1), acc)
    pkh[...] = acc
    for u in range(tb):
        lo_ref[u] = jnp.where(sub == 7, out_ref[u, 0:1, :], lo7_ref[u])
        hi_ref[u] = jnp.where(sub == 7, out_ref[u, n - 1 : n, :], hi7_ref[u])

    @pl.when(step == pl.num_programs(0) - 1)
    def _():
        slot = lane_n & 3
        v0, v1, f0, f1, fr, he = pk_ref[0], pk_ref[1], pk_ref[2], pk_ref[3], pk_ref[4], pkh[...]

        def sel(a, b, c, d):
            return jnp.where(slot < 2, jnp.where(slot == 0, a, b), jnp.where(slot == 2, c, d))

        right_ref[0] = jnp.where(slot < 2, v0, pltpu.roll(v1, 2, 1))
        left_ref[0] = jnp.where(slot >= 2, v0, pltpu.roll(v1, 126, 1))
        right_ref[1] = sel(pltpu.roll(f0, 127, 1), f1, pltpu.roll(fr, 1, 1), pltpu.roll(he, 2, 1))
        left_ref[1] = sel(pltpu.roll(f0, 126, 1), pltpu.roll(f1, 127, 1), fr, pltpu.roll(he, 1, 1))


def heat(d, gathered, seg, prior, pk, lo7, hi7):
    T, n, _ = prior.shape
    J = gathered.shape[0]
    tb = 4
    row = jax.ShapeDtypeStruct((T + 1, 8, 128), F32)
    return pl.pallas_call(
        functools.partial(heat_kernel, J, tb, n),
        grid=(T // tb,),
        in_specs=[
            pl.BlockSpec((T, 128), lambda t: (0, 0)),
            pl.BlockSpec((J, 2, T, 128), lambda t: (0, 0, 0, 0)),
            pl.BlockSpec((2, tb, 8, 128), lambda t: (0, t, 0, 0)),
            pl.BlockSpec((tb, n, 128), lambda t: (t, 0, 0)),
            pl.BlockSpec((5, n, 128), lambda t: (0, 0, 0)),
            pl.BlockSpec((tb, 8, 128), lambda t: (t, 0, 0)),
            pl.BlockSpec((tb, 8, 128), lambda t: (t, 0, 0)),
        ],
        out_specs=[
            pl.BlockSpec((tb, n, 128), lambda t: (t, 0, 0)),
            pl.BlockSpec((2, n, 128), lambda t: (0, 0, 0)),
            pl.BlockSpec((2, n, 128), lambda t: (0, 0, 0)),
            pl.BlockSpec((tb, 8, 128), lambda t: (t, 0, 0)),
            pl.BlockSpec((tb, 8, 128), lambda t: (t, 0, 0)),
        ],
        out_shape=[
            jax.ShapeDtypeStruct((T, n, 128), F32),
            jax.ShapeDtypeStruct((2, n, 128), F32),
            jax.ShapeDtypeStruct((2, n, 128), F32),
            row,
            row,
        ],
        scratch_shapes=[
            pltpu.VMEM((2, T, 128), F32),
            pltpu.VMEM((n, 128), F32),
            pltpu.VMEM((tb, n // 8, 8, 128), F32),
        ],
        compiler_params=pltpu.CompilerParams(vmem_limit_bytes=24 * MIB),
        cost_estimate=pl.CostEstimate(flops=10 * T * n * 128, bytes_accessed=8 * T * n * 128, transcendentals=0),
        name="heat",
    )(d, gathered, seg, prior, pk, lo7, hi7)


def corner_kernel(n, fl_ref, fr_ref, lo_in, hi_in, r_ref, lo_ref, hi_ref):
    slot = lax.broadcasted_iota(jnp.int32, (n, 128), 1) & 3
    al, ar, bl, br = fl_ref[0], fr_ref[0], fl_ref[1], fr_ref[1]
    low = slot < 2
    r_ref[0] = jnp.where(low, al, ar)
    r_ref[1] = jnp.where(low, pltpu.roll(al, 126, 1), pltpu.roll(ar, 2, 1))
    for k in range(4):
        a = bl if k == 1 else pltpu.roll(bl, (1 - k) & 127, 1)
        b = br if k == 2 else pltpu.roll(br, (2 - k) & 127, 1)
        r_ref[2 + k] = jnp.where(low, a, b)
    for ref, a, e in ((lo_ref, 0, 0), (hi_ref, n - 2, n - 1)):
        ref[0, 0:2, :] = r_ref[0, a : a + 2, :]
        ref[0, 2:4, :] = r_ref[1, a : a + 2, :]
        for k in range(4):
            ref[0, 4 + k : 5 + k, :] = r_ref[2 + k, e : e + 1, :]


def corners(from_left, from_right, lo, hi):
    _, n, _ = from_left.shape
    T = lo.shape[0] - 1
    row = jax.ShapeDtypeStruct(lo.shape, F32)
    return pl.pallas_call(
        functools.partial(corner_kernel, n),
        grid=(1,),
        in_specs=[
            pl.BlockSpec((2, n, 128), lambda g: (0, 0, 0)),
            pl.BlockSpec((2, n, 128), lambda g: (0, 0, 0)),
            pl.BlockSpec(memory_space=pl.ANY),
            pl.BlockSpec(memory_space=pl.ANY),
        ],
        out_specs=[
            pl.BlockSpec((6, n, 128), lambda g: (0, 0, 0)),
            pl.BlockSpec((1, 8, 128), lambda g: (T, 0, 0)),
            pl.BlockSpec((1, 8, 128), lambda g: (T, 0, 0)),
        ],
        out_shape=[jax.ShapeDtypeStruct((6, n, 128), F32), row, row],
        input_output_aliases={2: 1, 3: 2},
        compiler_params=pltpu.CompilerParams(vmem_limit_bytes=16 * MIB),
        cost_estimate=pl.CostEstimate(flops=0, bytes_accessed=40 * n * 128, transcendentals=0),
        name="corners",
    )(from_left, from_right, lo, hi)


def coefficients(f0, f1, free, heated):
    v = jnp.exp(-0.5 * heated)
    w = RELAX_FACTOR * free
    a = w / (DRAG_COEFF + 4.0 * v)
    return 1.0 - w, a * v, a * f0, a * f1


def sweep_kernel(
    tb, n, v_ref, f_ref, p_ref, h_ref, lo_ref, hi_ref, r_ref, own_ref,
    out_ref, yh1, yh2, v1s, cos, r1s,
):
    S = n // 8
    T = lo_ref.shape[0] - 1
    step = pl.program_id(0)
    lane, sub = iotas()
    slot = lane & 3
    first, last = lane == 0, lane == 127

    def ext(load, lo_row, hi_row, i):
        if i < 0:
            return jnp.where(sub == 0, lo_row(i), pltpu.roll(load(S + i), 1, 0))
        if i >= S:
            return jnp.where(sub == 7, hi_row(i - S), pltpu.roll(load(i - S), 7, 0))
        return load(i)

    @pl.when(step == 0)
    def _():
        own_lo = jnp.zeros((8, 128), F32)
        own_hi = jnp.zeros((8, 128), F32)
        for t in range(T):
            own_lo = jnp.where(lane >> 2 == t, pltpu.roll(lo_ref[t], (4 * t + 2) & 127, 1), own_lo)
            own_hi = jnp.where(lane >> 2 == t, pltpu.roll(hi_ref[t], (4 * t + 2) & 127, 1), own_hi)
        outer = (slot == 0) | (slot == 3)
        sign = jnp.where(slot == 1, -0.25, 0.25)

        def r_at(c, i):
            return ext(
                lambda q: r_ref[c, pl.ds(q, 8, stride=S), :],
                lambda q: lo_ref[T, 2 * c + 2 + q : 2 * c + 3 + q, :],
                lambda q: hi_ref[T, 2 * c + q : 2 * c + 1 + q, :],
                i,
            )

        def o_at(c, i):
            return ext(
                lambda q: own_ref[c, pl.ds(q, 8, stride=S), :],
                lambda q: own_lo[2 * c + 2 + q : 2 * c + 3 + q, :],
                lambda q: own_hi[2 * c + q : 2 * c + 1 + q, :],
                i,
            )

        def e_at(k, i):
            return ext(
                lambda q: r_ref[k, pl.ds(q, 8, stride=S), :],
                lambda q: lo_ref[T, 2 + k : 3 + k, :],
                lambda q: hi_ref[T, 2 + k : 3 + k, :],
                i,
            )

        def both(i):
            r = [r_at(c, i) for c in range(2)]
            w = [jnp.where(outer, r[c], o_at(c, i)) for c in range(2)]
            return r, w

        prev, here = both(-2), both(-1)
        for i in range(-1, S + 1):
            after = both(i + 1)
            k, g, a0, a1 = coefficients(e_at(2, i), e_at(3, i), e_at(4, i), e_at(5, i))
            dr = [after[0][c] - prev[0][c] for c in range(2)]
            qw = [0.25 * (after[1][c] - prev[1][c]) for c in range(2)]
            for c in range(2):
                yh1[c, i + 1] = here[0][c] + sign * dr[1 - c]
                around = (
                    prev[0][c]
                    + after[0][c]
                    + pltpu.roll(here[1][c] + qw[1 - c], 127, 1)
                    + pltpu.roll(here[1][c] - qw[1 - c], 1, 1)
                )
                r1s[c, i + 1] = k * here[0][c] + (a0, a1)[c] + g * around
            prev, here = here, after
        for i in range(S):
            for c in range(2):
                yh2[c, i] = r1s[c, i + 1] + sign * (r1s[1 - c, i + 2] - r1s[1 - c, i])

    def layer(u, _):
        t = step * tb + u
        shift = (126 - 4 * t) & 127

        def update(prev, here, after, k, g, a, yh):
            q = [0.25 * (after[c] - prev[c]) for c in range(2)]
            new = []
            for c in range(2):
                edge = pltpu.roll(yh[c], shift, 1)
                up = jnp.where(first, edge, here[c] + q[1 - c])
                down = jnp.where(last, edge, here[c] - q[1 - c])
                around = prev[c] + after[c] + (pltpu.roll(up, 127, 1) + pltpu.roll(down, 1, 1))
                new.append(k * here[c] + a[c] + g * around)
            return new

        def at(i):
            return [
                ext(
                    lambda q: v_ref[c, u, pl.ds(q, 8, stride=S), :],
                    lambda q: lo_ref[t, 2 * c + 2 + q : 2 * c + 3 + q, :],
                    lambda q: hi_ref[t, 2 * c + q : 2 * c + 1 + q, :],
                    i,
                )
                for c in range(2)
            ]

        def edge_of(k, load, i):
            return ext(load, lambda q: lo_ref[t, k : k + 1, :], lambda q: hi_ref[t, k : k + 1, :], i)

        prev, here = at(-2), at(-1)
        for i in range(-1, S + 1):
            after = at(i + 1)
            co = coefficients(
                edge_of(4, lambda q: f_ref[0, u, pl.ds(q, 8, stride=S), :], i),
                edge_of(5, lambda q: f_ref[1, u, pl.ds(q, 8, stride=S), :], i),
                edge_of(6, lambda q: 1.0 - p_ref[u, pl.ds(q, 8, stride=S), :].astype(F32), i),
                edge_of(7, lambda q: h_ref[u, pl.ds(q, 8, stride=S), :], i),
            )
            if 0 <= i < S:
                for m in range(4):
                    cos[m, i] = co[m]
            new = update(prev, here, after, co[0], co[1], co[2:], [yh1[c, i + 1] for c in range(2)])
            for c in range(2):
                v1s[c, i + 1] = new[c]
            prev, here = here, after
        for i in range(S):
            new = update(
                [v1s[c, i] for c in range(2)],
                [v1s[c, i + 1] for c in range(2)],
                [v1s[c, i + 2] for c in range(2)],
                cos[0, i],
                cos[1, i],
                [cos[2, i], cos[3, i]],
                [yh2[c, i] for c in range(2)],
            )
            for c in range(2):
                out_ref[c, u, pl.ds(i, 8, stride=S), :] = new[c]
        return 0

    lax.fori_loop(0, tb, layer, 0)


def sweeps(v, f, pinned, heated, lo, hi, r, pk):
    _, T, n, _ = v.shape
    S = n // 8
    tb = 2
    return pl.pallas_call(
        functools.partial(sweep_kernel, tb, n),
        grid=(T // tb,),
        in_specs=[
            pl.BlockSpec((2, tb, n, 128), lambda t: (0, t, 0, 0)),
            pl.BlockSpec((2, tb, n, 128), lambda t: (0, t, 0, 0)),
            pl.BlockSpec((tb, n, 128), lambda t: (t, 0, 0)),
            pl.BlockSpec((tb, n, 128), lambda t: (t, 0, 0)),
            pl.BlockSpec((T + 1, 8, 128), lambda t: (0, 0, 0)),
            pl.BlockSpec((T + 1, 8, 128), lambda t: (0, 0, 0)),
            pl.BlockSpec((6, n, 128), lambda t: (0, 0, 0)),
            pl.BlockSpec((2, n, 128), lambda t: (0, 0, 0)),
        ],
        out_specs=pl.BlockSpec((2, tb, n, 128), lambda t: (0, t, 0, 0)),
        out_shape=jax.ShapeDtypeStruct((2, T, n, 128), F32),
        scratch_shapes=[
            pltpu.VMEM((2, S + 2, 8, 128), F32),
            pltpu.VMEM((2, S, 8, 128), F32),
            pltpu.VMEM((2, S + 2, 8, 128), F32),
            pltpu.VMEM((4, S, 8, 128), F32),
            pltpu.VMEM((2, S + 2, 8, 128), F32),
        ],
        compiler_params=pltpu.CompilerParams(vmem_limit_bytes=32 * MIB),
        cost_estimate=pl.CostEstimate(flops=60 * T * n * 128, bytes_accessed=32 * T * n * 128, transcendentals=T * n * 128),
        name="sweeps",
    )(v, f, pinned, heated, lo, hi, r, pk)


def shifted(up_going, down_going, axis):
    count = lax.axis_size(axis)
    up = [(i, i + 1) for i in range(count - 1)]
    down = [(j, i) for i, j in up]
    return lax.ppermute(up_going, axis, up), lax.ppermute(down_going, axis, down)


def local(prior, d, v, f, pinned):
    seg, pq = moments(d, prior)
    gathered = lax.all_gather(pq, "wid")
    pk, lo7, hi7 = pack(v, f, pinned)
    heated, right, left, lo, hi = heat(d, gathered, seg, prior, pk, lo7, hi7)
    from_left, from_right = shifted(right, left, "len")
    r, lo, hi = corners(from_left, from_right, lo, hi)
    from_below, from_above = shifted(hi, lo, "wid")
    flow = sweeps(v, f, pinned, heated, from_below, from_above, r, pk)
    return heated, flow


def solution(mesh):
    in_specs = (
        P(None, "wid", "len"),
        P(None, "len"),
        P(None, None, "wid", "len"),
        P(None, None, "wid", "len"),
        P(None, "wid", "len"),
    )
    out_specs = (P(None, "wid", "len"), P(None, None, "wid", "len"))
    return jax.shard_map(local, mesh=mesh, in_specs=in_specs, out_specs=out_specs, check_vma=False)
```

```python
import functools

import jax
import jax.numpy as jnp
from jax import lax
from jax.experimental import pallas as pl
from jax.experimental.pallas import tpu as pltpu
from jax.sharding import PartitionSpec as P

DRAG_COEFF = 0.5
RELAX_FACTOR = 0.8
F32 = jnp.float32
MIB = 1 << 20


def decay(d):
    x = 1.0 / d
    one_less = jnp.sqrt(x + 0.25 * x * x) - 0.5 * x
    r = 1.0 - one_less
    return r, (1.0 - r) / (1.0 + r)


def power(r, n):
    out = None
    while n:
        if n & 1:
            out = r if out is None else out * r
        n >>= 1
        if n:
            r = r * r
    return out


def sublane_powers(r, shape):
    s = lax.broadcasted_iota(jnp.int32, shape, 0)
    r2 = r * r
    r4 = r2 * r2
    one = jnp.ones(shape, F32)
    return (
        jnp.where((s & 1) != 0, r, one)
        * jnp.where((s & 2) != 0, r2, one)
        * jnp.where((s & 4) != 0, r4, one)
    )


def reciprocal(x):
    y = pl.reciprocal(x, approx=True)
    return y * (2.0 - x * y)


def batches(lo, hi, most=11):
    parts = -(-(hi - lo) // most)
    cuts = [lo + (hi - lo) * k // parts for k in range(parts + 1)]
    return [range(a, b) for a, b in zip(cuts, cuts[1:])]


def iotas():
    lane = lax.broadcasted_iota(jnp.int32, (8, 128), 1)
    sub = lax.broadcasted_iota(jnp.int32, (8, 128), 0)
    return lane, sub


def moments_kernel(tb, n, d_ref, f_ref, seg_ref, pq_ref):
    S = n // 8
    base = pl.program_id(0) * tb
    G = 4
    for g in range(tb // G):
        rs = []
        for u in range(G):
            r, _ = decay(d_ref[pl.ds(base + g * G + u, 1), :])
            rs.append(jnp.broadcast_to(r, (8, 128)))
        fwd = [None] * G
        bwd = [None] * G
        for i in range(S):
            for u in range(G):
                a = f_ref[g * G + u, pl.ds(i, 8, stride=S), :]
                b = f_ref[g * G + u, pl.ds(S - 1 - i, 8, stride=S), :]
                fwd[u] = a if i == 0 else fwd[u] * rs[u] + a
                bwd[u] = b if i == 0 else bwd[u] * rs[u] + b
        for u in range(G):
            k = g * G + u
            seg_ref[0, k] = fwd[u]
            seg_ref[1, k] = bwd[u]
            rS = power(rs[u], S)
            up = sublane_powers(rS, (8, 128))
            s = lax.broadcasted_iota(jnp.int32, (8, 128), 0)
            rS2 = rS * rS
            one = jnp.ones((8, 128), F32)
            down = (
                jnp.where((s & 1) == 0, rS, one)
                * jnp.where((s & 2) == 0, rS2, one)
                * jnp.where((s & 4) == 0, rS2 * rS2, one)
            )
            pq_ref[0, k : k + 1, :] = jnp.sum(fwd[u] * down, axis=0, keepdims=True)
            pq_ref[1, k : k + 1, :] = jnp.sum(bwd[u] * up, axis=0, keepdims=True)


def moments(d, prior):
    T, n, _ = prior.shape
    tb = 8
    return pl.pallas_call(
        functools.partial(moments_kernel, tb, n),
        grid=(T // tb,),
        in_specs=[
            pl.BlockSpec((T, 128), lambda t: (0, 0)),
            pl.BlockSpec((tb, n, 128), lambda t: (t, 0, 0)),
        ],
        out_specs=[
            pl.BlockSpec((2, tb, 8, 128), lambda t: (0, t, 0, 0)),
            pl.BlockSpec((2, tb, 128), lambda t: (0, t, 0)),
        ],
        out_shape=[
            jax.ShapeDtypeStruct((2, T, 8, 128), F32),
            jax.ShapeDtypeStruct((2, T, 128), F32),
        ],
        compiler_params=pltpu.CompilerParams(vmem_limit_bytes=60 * MIB),
        cost_estimate=pl.CostEstimate(flops=4 * T * n * 128, bytes_accessed=4 * T * n * 128, transcendentals=0),
        name="moments",
    )(d, prior)


def pack_kernel(tb, n, v_ref, f_ref, p_ref, pk_ref, lo_ref, hi_ref):
    base = pl.program_id(0) * tb
    lane = lax.broadcasted_iota(jnp.int32, (n, 128), 1)
    group = lane >> 2
    for k in range(5):
        acc = pk_ref[k]
        for u in range(tb):
            if k < 2:
                x = v_ref[k, u]
            elif k < 4:
                x = f_ref[k - 2, u]
            else:
                x = 1.0 - p_ref[u].astype(F32)
            t = base + u
            acc = jnp.where(group == t, pltpu.roll(x, (4 * t + 2) & 127, 1), acc)
        pk_ref[k] = acc
    _, sub = iotas()

    def stack(v0, v1, f0, f1, fr):
        out = jnp.where(sub < 2, v0, v1)
        out = jnp.where(sub >= 4, f0, out)
        out = jnp.where(sub >= 5, f1, out)
        return jnp.where(sub >= 6, fr, out)

    tiles = []
    for u in range(tb):
        for top, at, shifts in ((True, 0, (0, 2, 4, 5, 6)), (False, n - 8, (2, 4, 5, 6, 7))):
            rows = pl.ds(at, 8)
            raw = [v_ref[0, u, rows, :], v_ref[1, u, rows, :], f_ref[0, u, rows, :], f_ref[1, u, rows, :]]
            raw.append(1.0 - p_ref[u, rows, :].astype(F32))
            tiles.append((u, top, stack(*[pltpu.roll(x, q, 0) if q else x for x, q in zip(raw, shifts)])))
    for u, top, tile in tiles:
        (lo_ref if top else hi_ref)[u] = tile


def pack(v, f, pinned):
    _, T, n, _ = v.shape
    tb = 4
    row = jax.ShapeDtypeStruct((T, 8, 128), F32)
    return pl.pallas_call(
        functools.partial(pack_kernel, tb, n),
        grid=(T // tb,),
        in_specs=[
            pl.BlockSpec((2, tb, n, 128), lambda t: (0, t, 0, 0)),
            pl.BlockSpec((2, tb, n, 128), lambda t: (0, t, 0, 0)),
            pl.BlockSpec((tb, n, 128), lambda t: (t, 0, 0)),
        ],
        out_specs=[
            pl.BlockSpec((5, n, 128), lambda t: (0, 0, 0)),
            pl.BlockSpec((tb, 8, 128), lambda t: (t, 0, 0)),
            pl.BlockSpec((tb, 8, 128), lambda t: (t, 0, 0)),
        ],
        out_shape=[jax.ShapeDtypeStruct((5, n, 128), F32), row, row],
        compiler_params=pltpu.CompilerParams(vmem_limit_bytes=60 * MIB),
        cost_estimate=pl.CostEstimate(flops=5 * T * n * 128, bytes_accessed=20 * T * n * 128, transcendentals=0),
        name="pack_edges",
    )(v, f, pinned)


def heat_kernel(J, tb, n, *refs):
    d_ref, *pq_refs = refs[: J + 1]
    (
        seg_ref, f_ref, pk_ref, lo7_ref, hi7_ref,
        out_ref, right_ref, left_ref, lo_ref, hi_ref, alls, sums, pkh, ys,
    ) = refs[J + 1 :]
    S = n // 8
    step = pl.program_id(0)
    base = step * tb

    @pl.when(step == 0)
    def _():
        j = lax.axis_index("wid")
        for s in range(J):
            alls[lax.rem(j - s + J, J)] = pq_refs[s][...]
        r, _ = decay(d_ref[...])
        rn = power(r, n)
        rN = power(rn, J)
        sp = alls[0, 0]
        for i in range(1, J):
            sp = sp * rn + alls[i, 0]
        sq = alls[J - 1, 1]
        for i in range(J - 2, -1, -1):
            sq = sq * rn + alls[i, 1]
        inv = 1.0 / (1.0 - rN * rN)
        left = (sq + rN * sp) * inv
        right = (sp + rN * sq) * inv
        for i in range(J - 1):
            left = jnp.where(i < j, rn * left + alls[i, 0], left)
        for i in range(J - 1, 0, -1):
            right = jnp.where(i > j, rn * right + alls[i, 1], right)
        sums[0] = left
        sums[1] = right

    _, sub = iotas()
    rs, gain, y, z = [], [], [], []
    for u in range(tb):
        t = base + u
        r, a0 = decay(d_ref[pl.ds(t, 1), :])
        r = jnp.broadcast_to(r, (8, 128))
        a0 = jnp.broadcast_to(a0, (8, 128))
        rS = power(r, S)
        rS2 = rS * rS
        rS4 = rS2 * rS2
        c = jnp.where(sub == 0, sums[0, pl.ds(t, 1), :], pltpu.roll(seg_ref[0, u], 1, 0))
        b = jnp.where(sub == 7, sums[1, pl.ds(t, 1), :], pltpu.roll(seg_ref[1, u], 7, 0))
        for s, q in ((1, rS), (2, rS2), (4, rS4)):
            c = c + q * jnp.where(sub >= s, pltpu.roll(c, s, 0), 0.0)
            b = b + q * jnp.where(sub < 8 - s, pltpu.roll(b, 8 - s, 0), 0.0)
        rs.append(r)
        gain.append(a0)
        y.append(c)
        z.append(b)
    for rows in batches(0, S, 8):
        done = []
        for i in rows:
            for u in range(tb):
                y[u] = y[u] * rs[u] + f_ref[u, pl.ds(i, 8, stride=S), :]
                done.append((u, i, y[u]))
        for u, i, value in done:
            ys[u, i] = value
    for rows in batches(0, S, 8)[::-1]:
        done = []
        for i in rows[::-1]:
            for u in range(tb):
                zr = z[u] * rs[u]
                done.append((u, i, gain[u] * (ys[u, i] + zr)))
                z[u] = zr + f_ref[u, pl.ds(i, 8, stride=S), :]
        for u, i, value in done:
            out_ref[u, pl.ds(i, 8, stride=S), :] = value

    lane_n = lax.broadcasted_iota(jnp.int32, (n, 128), 1)
    group = lane_n >> 2
    acc = pkh[...]
    for u in range(tb):
        t = base + u
        acc = jnp.where(group == t, pltpu.roll(out_ref[u], (4 * t + 2) & 127, 1), acc)
    pkh[...] = acc
    lows = [jnp.where(sub == 7, out_ref[u, 0:1, :], lo7_ref[u]) for u in range(tb)]
    highs = [jnp.where(sub == 7, out_ref[u, n - 1 : n, :], hi7_ref[u]) for u in range(tb)]
    for u in range(tb):
        lo_ref[u] = lows[u]
        hi_ref[u] = highs[u]

    @pl.when(step == pl.num_programs(0) - 1)
    def _():
        slot = lane_n & 3
        v0, v1, f0, f1, fr, he = pk_ref[0], pk_ref[1], pk_ref[2], pk_ref[3], pk_ref[4], pkh[...]

        def sel(a, b, c, d):
            return jnp.where(slot < 2, jnp.where(slot == 0, a, b), jnp.where(slot == 2, c, d))

        right_ref[0] = jnp.where(slot < 2, v0, pltpu.roll(v1, 2, 1))
        left_ref[0] = jnp.where(slot >= 2, v0, pltpu.roll(v1, 126, 1))
        right_ref[1] = sel(pltpu.roll(f0, 127, 1), f1, pltpu.roll(fr, 1, 1), pltpu.roll(he, 2, 1))
        left_ref[1] = sel(pltpu.roll(f0, 126, 1), pltpu.roll(f1, 127, 1), fr, pltpu.roll(he, 1, 1))


def heat(d, pqs, seg, prior, pk, lo7, hi7):
    T, n, _ = prior.shape
    J = len(pqs)
    tb = 4
    row = jax.ShapeDtypeStruct((T + 1, 8, 128), F32)
    return pl.pallas_call(
        functools.partial(heat_kernel, J, tb, n),
        grid=(T // tb,),
        in_specs=[
            pl.BlockSpec((T, 128), lambda t: (0, 0)),
            *[pl.BlockSpec((2, T, 128), lambda t: (0, 0, 0)) for _ in range(J)],
            pl.BlockSpec((2, tb, 8, 128), lambda t: (0, t, 0, 0)),
            pl.BlockSpec((tb, n, 128), lambda t: (t, 0, 0)),
            pl.BlockSpec((5, n, 128), lambda t: (0, 0, 0)),
            pl.BlockSpec((tb, 8, 128), lambda t: (t, 0, 0)),
            pl.BlockSpec((tb, 8, 128), lambda t: (t, 0, 0)),
        ],
        out_specs=[
            pl.BlockSpec((tb, n, 128), lambda t: (t, 0, 0)),
            pl.BlockSpec((2, n, 128), lambda t: (0, 0, 0)),
            pl.BlockSpec((2, n, 128), lambda t: (0, 0, 0)),
            pl.BlockSpec((tb, 8, 128), lambda t: (t, 0, 0)),
            pl.BlockSpec((tb, 8, 128), lambda t: (t, 0, 0)),
        ],
        out_shape=[
            jax.ShapeDtypeStruct((T, n, 128), F32),
            jax.ShapeDtypeStruct((2, n, 128), F32),
            jax.ShapeDtypeStruct((2, n, 128), F32),
            row,
            row,
        ],
        scratch_shapes=[
            pltpu.VMEM((J, 2, T, 128), F32),
            pltpu.VMEM((2, T, 128), F32),
            pltpu.VMEM((n, 128), F32),
            pltpu.VMEM((tb, n // 8, 8, 128), F32),
        ],
        compiler_params=pltpu.CompilerParams(vmem_limit_bytes=24 * MIB),
        cost_estimate=pl.CostEstimate(flops=10 * T * n * 128, bytes_accessed=8 * T * n * 128, transcendentals=0),
        name="heat",
    )(d, *pqs, seg, prior, pk, lo7, hi7)


def corner_kernel(n, fl_ref, fr_ref, lo_in, hi_in, r_ref, lo_ref, hi_ref):
    slot = lax.broadcasted_iota(jnp.int32, (n, 128), 1) & 3
    al, ar, bl, br = fl_ref[0], fr_ref[0], fl_ref[1], fr_ref[1]
    low = slot < 2
    r_ref[0] = jnp.where(low, al, ar)
    r_ref[1] = jnp.where(low, pltpu.roll(al, 126, 1), pltpu.roll(ar, 2, 1))
    for k in range(4):
        a = bl if k == 1 else pltpu.roll(bl, (1 - k) & 127, 1)
        b = br if k == 2 else pltpu.roll(br, (2 - k) & 127, 1)
        r_ref[2 + k] = jnp.where(low, a, b)
    for ref, a, e in ((lo_ref, 0, 0), (hi_ref, n - 2, n - 1)):
        ref[0, 0:2, :] = r_ref[0, a : a + 2, :]
        ref[0, 2:4, :] = r_ref[1, a : a + 2, :]
        for k in range(4):
            ref[0, 4 + k : 5 + k, :] = r_ref[2 + k, e : e + 1, :]


def corners(from_left, from_right, lo, hi):
    _, n, _ = from_left.shape
    T = lo.shape[0] - 1
    row = jax.ShapeDtypeStruct(lo.shape, F32)
    return pl.pallas_call(
        functools.partial(corner_kernel, n),
        grid=(1,),
        in_specs=[
            pl.BlockSpec((2, n, 128), lambda g: (0, 0, 0)),
            pl.BlockSpec((2, n, 128), lambda g: (0, 0, 0)),
            pl.BlockSpec(memory_space=pl.ANY),
            pl.BlockSpec(memory_space=pl.ANY),
        ],
        out_specs=[
            pl.BlockSpec((6, n, 128), lambda g: (0, 0, 0)),
            pl.BlockSpec((1, 8, 128), lambda g: (T, 0, 0)),
            pl.BlockSpec((1, 8, 128), lambda g: (T, 0, 0)),
        ],
        out_shape=[jax.ShapeDtypeStruct((6, n, 128), F32), row, row],
        input_output_aliases={2: 1, 3: 2},
        compiler_params=pltpu.CompilerParams(vmem_limit_bytes=16 * MIB),
        cost_estimate=pl.CostEstimate(flops=0, bytes_accessed=40 * n * 128, transcendentals=0),
        name="corners",
    )(from_left, from_right, lo, hi)


def coefficients(f0, f1, free, heated):
    v = jnp.exp(-0.5 * heated)
    w = RELAX_FACTOR * free
    a = w * reciprocal(DRAG_COEFF + 4.0 * v)
    return 1.0 - w, a * v, a * f0, a * f1


def sweep_kernel(
    tb, n, v_ref, f_ref, p_ref, h_ref, lo_ref, hi_ref, r_ref, own_ref,
    out_ref, yh1, yh2, v1s, cos, r1s,
):
    S = n // 8
    T = lo_ref.shape[0] - 1
    step = pl.program_id(0)
    lane, sub = iotas()
    slot = lane & 3
    first, last = lane == 0, lane == 127

    def ext(load, lo_row, hi_row, i):
        if i < 0:
            return jnp.where(sub == 0, lo_row(i), pltpu.roll(load(S + i), 1, 0))
        if i >= S:
            return jnp.where(sub == 7, hi_row(i - S), pltpu.roll(load(i - S), 7, 0))
        return load(i)

    @pl.when(step == 0)
    def _():
        own_lo = jnp.zeros((8, 128), F32)
        own_hi = jnp.zeros((8, 128), F32)
        for t in range(T):
            own_lo = jnp.where(lane >> 2 == t, pltpu.roll(lo_ref[t], (4 * t + 2) & 127, 1), own_lo)
            own_hi = jnp.where(lane >> 2 == t, pltpu.roll(hi_ref[t], (4 * t + 2) & 127, 1), own_hi)
        outer = (slot == 0) | (slot == 3)
        sign = jnp.where(slot == 1, -0.25, 0.25)

        def r_at(c, i):
            return ext(
                lambda q: r_ref[c, pl.ds(q, 8, stride=S), :],
                lambda q: lo_ref[T, 2 * c + 2 + q : 2 * c + 3 + q, :],
                lambda q: hi_ref[T, 2 * c + q : 2 * c + 1 + q, :],
                i,
            )

        def o_at(c, i):
            return ext(
                lambda q: own_ref[c, pl.ds(q, 8, stride=S), :],
                lambda q: own_lo[2 * c + 2 + q : 2 * c + 3 + q, :],
                lambda q: own_hi[2 * c + q : 2 * c + 1 + q, :],
                i,
            )

        def e_at(k, i):
            return ext(
                lambda q: r_ref[k, pl.ds(q, 8, stride=S), :],
                lambda q: lo_ref[T, 2 + k : 3 + k, :],
                lambda q: hi_ref[T, 2 + k : 3 + k, :],
                i,
            )

        def both(i):
            r = [r_at(c, i) for c in range(2)]
            w = [jnp.where(outer, r[c], o_at(c, i)) for c in range(2)]
            return r, w

        for rows in batches(-1, S + 1):
            both_at = {i: both(i) for i in range(rows[0] - 1, rows[-1] + 2)}
            done = []
            for i in rows:
                prev, here, after = both_at[i - 1], both_at[i], both_at[i + 1]
                k, g, a0, a1 = coefficients(e_at(2, i), e_at(3, i), e_at(4, i), e_at(5, i))
                dr = [after[0][c] - prev[0][c] for c in range(2)]
                qw = [0.25 * (after[1][c] - prev[1][c]) for c in range(2)]
                for c in range(2):
                    around = (
                        prev[0][c]
                        + after[0][c]
                        + pltpu.roll(here[1][c] + qw[1 - c], 127, 1)
                        + pltpu.roll(here[1][c] - qw[1 - c], 1, 1)
                    )
                    done.append((c, i, here[0][c] + sign * dr[1 - c], k * here[0][c] + (a0, a1)[c] + g * around))
            for c, i, edge, new in done:
                yh1[c, i + 1] = edge
                r1s[c, i + 1] = new
        for rows in batches(0, S):
            done = [
                (c, i, r1s[c, i + 1] + sign * (r1s[1 - c, i + 2] - r1s[1 - c, i])) for i in rows for c in range(2)
            ]
            for c, i, edge in done:
                yh2[c, i] = edge

    def layer(u, _):
        t = step * tb + u
        shift = (126 - 4 * t) & 127

        def update(prev, here, after, k, g, a, yh):
            q = [0.25 * (after[c] - prev[c]) for c in range(2)]
            new = []
            for c in range(2):
                edge = pltpu.roll(yh[c], shift, 1)
                up = jnp.where(first, edge, here[c] + q[1 - c])
                down = jnp.where(last, edge, here[c] - q[1 - c])
                around = prev[c] + after[c] + (pltpu.roll(up, 127, 1) + pltpu.roll(down, 1, 1))
                new.append(k * here[c] + a[c] + g * around)
            return new

        def at(i):
            return [
                ext(
                    lambda q: v_ref[c, u, pl.ds(q, 8, stride=S), :],
                    lambda q: lo_ref[t, 2 * c + 2 + q : 2 * c + 3 + q, :],
                    lambda q: hi_ref[t, 2 * c + q : 2 * c + 1 + q, :],
                    i,
                )
                for c in range(2)
            ]

        def edge_of(k, load, i):
            return ext(load, lambda q: lo_ref[t, k : k + 1, :], lambda q: hi_ref[t, k : k + 1, :], i)

        for rows in batches(-1, S + 1):
            done = [
                (
                    i,
                    coefficients(
                        edge_of(4, lambda q: f_ref[0, u, pl.ds(q, 8, stride=S), :], i),
                        edge_of(5, lambda q: f_ref[1, u, pl.ds(q, 8, stride=S), :], i),
                        edge_of(6, lambda q: 1.0 - p_ref[u, pl.ds(q, 8, stride=S), :].astype(F32), i),
                        edge_of(7, lambda q: h_ref[u, pl.ds(q, 8, stride=S), :], i),
                    ),
                )
                for i in rows
            ]
            for i, co in done:
                for m in range(4):
                    cos[m, i + 1] = co[m]
        for rows in batches(-1, S + 1):
            x = {i: at(i) for i in range(rows[0] - 1, rows[-1] + 2)}
            done = [
                (
                    i,
                    update(
                        x[i - 1], x[i], x[i + 1], cos[0, i + 1], cos[1, i + 1],
                        [cos[2, i + 1], cos[3, i + 1]], [yh1[c, i + 1] for c in range(2)],
                    ),
                )
                for i in rows
            ]
            for i, new in done:
                for c in range(2):
                    v1s[c, i + 1] = new[c]
        for rows in batches(0, S):
            x = {i: [v1s[c, i + 1] for c in range(2)] for i in range(rows[0] - 1, rows[-1] + 2)}
            done = [
                (
                    i,
                    update(
                        x[i - 1], x[i], x[i + 1], cos[0, i + 1], cos[1, i + 1],
                        [cos[2, i + 1], cos[3, i + 1]], [yh2[c, i] for c in range(2)],
                    ),
                )
                for i in rows
            ]
            for i, new in done:
                for c in range(2):
                    out_ref[c, u, pl.ds(i, 8, stride=S), :] = new[c]
        return 0

    lax.fori_loop(0, tb, layer, 0)


def sweeps(v, f, pinned, heated, lo, hi, r, pk):
    _, T, n, _ = v.shape
    S = n // 8
    tb = 2
    return pl.pallas_call(
        functools.partial(sweep_kernel, tb, n),
        grid=(T // tb,),
        in_specs=[
            pl.BlockSpec((2, tb, n, 128), lambda t: (0, t, 0, 0)),
            pl.BlockSpec((2, tb, n, 128), lambda t: (0, t, 0, 0)),
            pl.BlockSpec((tb, n, 128), lambda t: (t, 0, 0)),
            pl.BlockSpec((tb, n, 128), lambda t: (t, 0, 0)),
            pl.BlockSpec((T + 1, 8, 128), lambda t: (0, 0, 0)),
            pl.BlockSpec((T + 1, 8, 128), lambda t: (0, 0, 0)),
            pl.BlockSpec((6, n, 128), lambda t: (0, 0, 0)),
            pl.BlockSpec((2, n, 128), lambda t: (0, 0, 0)),
        ],
        out_specs=pl.BlockSpec((2, tb, n, 128), lambda t: (0, t, 0, 0)),
        out_shape=jax.ShapeDtypeStruct((2, T, n, 128), F32),
        scratch_shapes=[
            pltpu.VMEM((2, S + 2, 8, 128), F32),
            pltpu.VMEM((2, S, 8, 128), F32),
            pltpu.VMEM((2, S + 2, 8, 128), F32),
            pltpu.VMEM((4, S + 2, 8, 128), F32),
            pltpu.VMEM((2, S + 2, 8, 128), F32),
        ],
        compiler_params=pltpu.CompilerParams(vmem_limit_bytes=32 * MIB),
        cost_estimate=pl.CostEstimate(flops=60 * T * n * 128, bytes_accessed=32 * T * n * 128, transcendentals=T * n * 128),
        name="sweeps",
    )(v, f, pinned, heated, lo, hi, r, pk)


def shifted(up_going, down_going, axis):
    count = lax.axis_size(axis)
    up = [(i, i + 1) for i in range(count - 1)]
    down = [(j, i) for i, j in up]
    return lax.ppermute(up_going, axis, up), lax.ppermute(down_going, axis, down)


def local(prior, d, v, f, pinned):
    seg, pq = moments(d, prior)
    J = lax.axis_size("wid")
    pqs = [pq] + [lax.ppermute(pq, "wid", [(i, (i + s) % J) for i in range(J)]) for s in range(1, J)]
    pk, lo7, hi7 = pack(v, f, pinned)
    heated, right, left, lo, hi = heat(d, pqs, seg, prior, pk, lo7, hi7)
    from_left, from_right = shifted(right, left, "len")
    r, lo, hi = corners(from_left, from_right, lo, hi)
    from_below, from_above = shifted(hi, lo, "wid")
    flow = sweeps(v, f, pinned, heated, from_below, from_above, r, pk)
    return heated, flow


def solution(mesh):
    in_specs = (
        P(None, "wid", "len"),
        P(None, "len"),
        P(None, None, "wid", "len"),
        P(None, None, "wid", "len"),
        P(None, "wid", "len"),
    )
    out_specs = (P(None, "wid", "len"), P(None, None, "wid", "len"))
    return jax.shard_map(local, mesh=mesh, in_specs=in_specs, out_specs=out_specs, check_vma=False)
```

```python
import functools

import jax
import jax.numpy as jnp
from jax import lax
from jax.experimental import pallas as pl
from jax.experimental.pallas import tpu as pltpu
from jax.sharding import PartitionSpec as P

DRAG_COEFF = 0.5
RELAX_FACTOR = 0.8
F32 = jnp.float32
MIB = 1 << 20


def decay(d):
    x = 1.0 / d
    one_less = jnp.sqrt(x + 0.25 * x * x) - 0.5 * x
    r = 1.0 - one_less
    return r, (1.0 - r) / (1.0 + r)


def power(r, n):
    out = None
    while n:
        if n & 1:
            out = r if out is None else out * r
        n >>= 1
        if n:
            r = r * r
    return out


def sublane_powers(r, shape):
    s = lax.broadcasted_iota(jnp.int32, shape, 0)
    r2 = r * r
    r4 = r2 * r2
    one = jnp.ones(shape, F32)
    return (
        jnp.where((s & 1) != 0, r, one)
        * jnp.where((s & 2) != 0, r2, one)
        * jnp.where((s & 4) != 0, r4, one)
    )


def reciprocal(x):
    y = pl.reciprocal(x, approx=True)
    return y * (2.0 - x * y)


def over_rows(count, body, init=0, backward=False, most=8):
    most = min(most, count)
    parts = count // most

    def step(k, carry):
        start = (parts - 1 - k if backward else k) * most
        rows = [start + i for i in range(most)]
        return body(rows[::-1] if backward else rows, carry)

    return lax.fori_loop(0, parts, step, init)


def iotas():
    lane = lax.broadcasted_iota(jnp.int32, (8, 128), 1)
    sub = lax.broadcasted_iota(jnp.int32, (8, 128), 0)
    return lane, sub


def moments_kernel(tb, n, d_ref, f_ref, seg_ref, pq_ref):
    S = n // 8
    base = pl.program_id(0) * tb
    G = 4
    for g in range(tb // G):
        rs = []
        for u in range(G):
            r, _ = decay(d_ref[pl.ds(base + g * G + u, 1), :])
            rs.append(jnp.broadcast_to(r, (8, 128)))
        zero = jnp.zeros((8, 128), F32)

        def body(rows, carry):
            fwd, bwd = list(carry[:G]), list(carry[G:])
            for i in rows:
                for u in range(G):
                    fwd[u] = fwd[u] * rs[u] + f_ref[g * G + u, pl.ds(i, 8, stride=S), :]
                    bwd[u] = bwd[u] * rs[u] + f_ref[g * G + u, pl.ds(S - 1 - i, 8, stride=S), :]
            return (*fwd, *bwd)

        carry = over_rows(S, body, (zero,) * (2 * G))
        fwd, bwd = carry[:G], carry[G:]
        for u in range(G):
            k = g * G + u
            seg_ref[0, k] = fwd[u]
            seg_ref[1, k] = bwd[u]
            rS = power(rs[u], S)
            up = sublane_powers(rS, (8, 128))
            s = lax.broadcasted_iota(jnp.int32, (8, 128), 0)
            rS2 = rS * rS
            one = jnp.ones((8, 128), F32)
            down = (
                jnp.where((s & 1) == 0, rS, one)
                * jnp.where((s & 2) == 0, rS2, one)
                * jnp.where((s & 4) == 0, rS2 * rS2, one)
            )
            pq_ref[0, k : k + 1, :] = jnp.sum(fwd[u] * down, axis=0, keepdims=True)
            pq_ref[1, k : k + 1, :] = jnp.sum(bwd[u] * up, axis=0, keepdims=True)


def moments(d, prior):
    T, n, _ = prior.shape
    tb = 8
    return pl.pallas_call(
        functools.partial(moments_kernel, tb, n),
        grid=(T // tb,),
        in_specs=[
            pl.BlockSpec((T, 128), lambda t: (0, 0)),
            pl.BlockSpec((tb, n, 128), lambda t: (t, 0, 0)),
        ],
        out_specs=[
            pl.BlockSpec((2, tb, 8, 128), lambda t: (0, t, 0, 0)),
            pl.BlockSpec((2, tb, 128), lambda t: (0, t, 0)),
        ],
        out_shape=[
            jax.ShapeDtypeStruct((2, T, 8, 128), F32),
            jax.ShapeDtypeStruct((2, T, 128), F32),
        ],
        compiler_params=pltpu.CompilerParams(vmem_limit_bytes=60 * MIB),
        cost_estimate=pl.CostEstimate(flops=4 * T * n * 128, bytes_accessed=4 * T * n * 128, transcendentals=0),
        name="moments",
    )(d, prior)


def pack_kernel(tb, n, v_ref, f_ref, p_ref, pk_ref, lo_ref, hi_ref):
    base = pl.program_id(0) * tb
    chunk = min(64, n)
    group = lax.broadcasted_iota(jnp.int32, (chunk, 128), 1) >> 2

    def body(m, _):
        rows = pl.ds(pl.multiple_of(m * chunk, chunk), chunk)
        packed = []
        for k in range(5):
            acc = pk_ref[k, rows, :]
            for u in range(tb):
                if k < 2:
                    x = v_ref[k, u, rows, :]
                elif k < 4:
                    x = f_ref[k - 2, u, rows, :]
                else:
                    x = 1.0 - p_ref[u, rows, :].astype(F32)
                t = base + u
                acc = jnp.where(group == t, pltpu.roll(x, (4 * t + 2) & 127, 1), acc)
            packed.append(acc)
        for k in range(5):
            pk_ref[k, rows, :] = packed[k]
        return 0

    lax.fori_loop(0, n // chunk, body, 0)
    _, sub = iotas()

    def stack(v0, v1, f0, f1, fr):
        out = jnp.where(sub < 2, v0, v1)
        out = jnp.where(sub >= 4, f0, out)
        out = jnp.where(sub >= 5, f1, out)
        return jnp.where(sub >= 6, fr, out)

    tiles = []
    for u in range(tb):
        for top, at, shifts in ((True, 0, (0, 2, 4, 5, 6)), (False, n - 8, (2, 4, 5, 6, 7))):
            rows = pl.ds(at, 8)
            raw = [v_ref[0, u, rows, :], v_ref[1, u, rows, :], f_ref[0, u, rows, :], f_ref[1, u, rows, :]]
            raw.append(1.0 - p_ref[u, rows, :].astype(F32))
            tiles.append((u, top, stack(*[pltpu.roll(x, q, 0) if q else x for x, q in zip(raw, shifts)])))
    for u, top, tile in tiles:
        (lo_ref if top else hi_ref)[u] = tile


def pack(v, f, pinned):
    _, T, n, _ = v.shape
    tb = 4
    row = jax.ShapeDtypeStruct((T, 8, 128), F32)
    return pl.pallas_call(
        functools.partial(pack_kernel, tb, n),
        grid=(T // tb,),
        in_specs=[
            pl.BlockSpec((2, tb, n, 128), lambda t: (0, t, 0, 0)),
            pl.BlockSpec((2, tb, n, 128), lambda t: (0, t, 0, 0)),
            pl.BlockSpec((tb, n, 128), lambda t: (t, 0, 0)),
        ],
        out_specs=[
            pl.BlockSpec((5, n, 128), lambda t: (0, 0, 0)),
            pl.BlockSpec((tb, 8, 128), lambda t: (t, 0, 0)),
            pl.BlockSpec((tb, 8, 128), lambda t: (t, 0, 0)),
        ],
        out_shape=[jax.ShapeDtypeStruct((5, n, 128), F32), row, row],
        compiler_params=pltpu.CompilerParams(vmem_limit_bytes=60 * MIB),
        cost_estimate=pl.CostEstimate(flops=5 * T * n * 128, bytes_accessed=20 * T * n * 128, transcendentals=0),
        name="pack_edges",
    )(v, f, pinned)


def heat_kernel(J, tb, n, *refs):
    d_ref, *pq_refs = refs[: J + 1]
    (
        seg_ref, f_ref, pk_ref, lo7_ref, hi7_ref,
        out_ref, right_ref, left_ref, lo_ref, hi_ref, alls, sums, pkh, ys,
    ) = refs[J + 1 :]
    S = n // 8
    step = pl.program_id(0)
    base = step * tb

    @pl.when(step == 0)
    def _():
        j = lax.axis_index("wid")
        for s in range(J):
            alls[lax.rem(j - s + J, J)] = pq_refs[s][...]
        r, _ = decay(d_ref[...])
        rn = power(r, n)
        rN = power(rn, J)
        sp = alls[0, 0]
        for i in range(1, J):
            sp = sp * rn + alls[i, 0]
        sq = alls[J - 1, 1]
        for i in range(J - 2, -1, -1):
            sq = sq * rn + alls[i, 1]
        inv = 1.0 / (1.0 - rN * rN)
        left = (sq + rN * sp) * inv
        right = (sp + rN * sq) * inv
        for i in range(J - 1):
            left = jnp.where(i < j, rn * left + alls[i, 0], left)
        for i in range(J - 1, 0, -1):
            right = jnp.where(i > j, rn * right + alls[i, 1], right)
        sums[0] = left
        sums[1] = right

    _, sub = iotas()
    rs, gain, y, z = [], [], [], []
    for u in range(tb):
        t = base + u
        r, a0 = decay(d_ref[pl.ds(t, 1), :])
        r = jnp.broadcast_to(r, (8, 128))
        a0 = jnp.broadcast_to(a0, (8, 128))
        rS = power(r, S)
        rS2 = rS * rS
        rS4 = rS2 * rS2
        c = jnp.where(sub == 0, sums[0, pl.ds(t, 1), :], pltpu.roll(seg_ref[0, u], 1, 0))
        b = jnp.where(sub == 7, sums[1, pl.ds(t, 1), :], pltpu.roll(seg_ref[1, u], 7, 0))
        for s, q in ((1, rS), (2, rS2), (4, rS4)):
            c = c + q * jnp.where(sub >= s, pltpu.roll(c, s, 0), 0.0)
            b = b + q * jnp.where(sub < 8 - s, pltpu.roll(b, 8 - s, 0), 0.0)
        rs.append(r)
        gain.append(a0)
        y.append(c)
        z.append(b)
    def forward(rows, y):
        y, done = list(y), []
        for i in rows:
            for u in range(tb):
                y[u] = y[u] * rs[u] + f_ref[u, pl.ds(i, 8, stride=S), :]
                done.append((u, i, y[u]))
        for u, i, value in done:
            ys[u, i] = value
        return tuple(y)

    def backward(rows, z):
        z, done = list(z), []
        for i in rows:
            for u in range(tb):
                zr = z[u] * rs[u]
                done.append((u, i, gain[u] * (ys[u, i] + zr)))
                z[u] = zr + f_ref[u, pl.ds(i, 8, stride=S), :]
        for u, i, value in done:
            out_ref[u, pl.ds(i, 8, stride=S), :] = value
        return tuple(z)

    over_rows(S, forward, tuple(y))
    over_rows(S, backward, tuple(z), backward=True)

    lane_n = lax.broadcasted_iota(jnp.int32, (n, 128), 1)
    group = lane_n >> 2
    acc = pkh[...]
    for u in range(tb):
        t = base + u
        acc = jnp.where(group == t, pltpu.roll(out_ref[u], (4 * t + 2) & 127, 1), acc)
    pkh[...] = acc
    lows = [jnp.where(sub == 7, out_ref[u, 0:1, :], lo7_ref[u]) for u in range(tb)]
    highs = [jnp.where(sub == 7, out_ref[u, n - 1 : n, :], hi7_ref[u]) for u in range(tb)]
    for u in range(tb):
        lo_ref[u] = lows[u]
        hi_ref[u] = highs[u]

    @pl.when(step == pl.num_programs(0) - 1)
    def _():
        slot = lane_n & 3
        v0, v1, f0, f1, fr, he = pk_ref[0], pk_ref[1], pk_ref[2], pk_ref[3], pk_ref[4], pkh[...]

        def sel(a, b, c, d):
            return jnp.where(slot < 2, jnp.where(slot == 0, a, b), jnp.where(slot == 2, c, d))

        right_ref[0] = jnp.where(slot < 2, v0, pltpu.roll(v1, 2, 1))
        left_ref[0] = jnp.where(slot >= 2, v0, pltpu.roll(v1, 126, 1))
        right_ref[1] = sel(pltpu.roll(f0, 127, 1), f1, pltpu.roll(fr, 1, 1), pltpu.roll(he, 2, 1))
        left_ref[1] = sel(pltpu.roll(f0, 126, 1), pltpu.roll(f1, 127, 1), fr, pltpu.roll(he, 1, 1))


def heat(d, pqs, seg, prior, pk, lo7, hi7):
    T, n, _ = prior.shape
    J = len(pqs)
    tb = 4
    row = jax.ShapeDtypeStruct((T + 1, 8, 128), F32)
    return pl.pallas_call(
        functools.partial(heat_kernel, J, tb, n),
        grid=(T // tb,),
        in_specs=[
            pl.BlockSpec((T, 128), lambda t: (0, 0)),
            *[pl.BlockSpec((2, T, 128), lambda t: (0, 0, 0)) for _ in range(J)],
            pl.BlockSpec((2, tb, 8, 128), lambda t: (0, t, 0, 0)),
            pl.BlockSpec((tb, n, 128), lambda t: (t, 0, 0)),
            pl.BlockSpec((5, n, 128), lambda t: (0, 0, 0)),
            pl.BlockSpec((tb, 8, 128), lambda t: (t, 0, 0)),
            pl.BlockSpec((tb, 8, 128), lambda t: (t, 0, 0)),
        ],
        out_specs=[
            pl.BlockSpec((tb, n, 128), lambda t: (t, 0, 0)),
            pl.BlockSpec((2, n, 128), lambda t: (0, 0, 0)),
            pl.BlockSpec((2, n, 128), lambda t: (0, 0, 0)),
            pl.BlockSpec((tb, 8, 128), lambda t: (t, 0, 0)),
            pl.BlockSpec((tb, 8, 128), lambda t: (t, 0, 0)),
        ],
        out_shape=[
            jax.ShapeDtypeStruct((T, n, 128), F32),
            jax.ShapeDtypeStruct((2, n, 128), F32),
            jax.ShapeDtypeStruct((2, n, 128), F32),
            row,
            row,
        ],
        scratch_shapes=[
            pltpu.VMEM((J, 2, T, 128), F32),
            pltpu.VMEM((2, T, 128), F32),
            pltpu.VMEM((n, 128), F32),
            pltpu.VMEM((tb, n // 8, 8, 128), F32),
        ],
        compiler_params=pltpu.CompilerParams(vmem_limit_bytes=24 * MIB),
        cost_estimate=pl.CostEstimate(flops=10 * T * n * 128, bytes_accessed=8 * T * n * 128, transcendentals=0),
        name="heat",
    )(d, *pqs, seg, prior, pk, lo7, hi7)


def corner_kernel(n, fl_ref, fr_ref, lo_in, hi_in, r_ref, lo_ref, hi_ref):
    slot = lax.broadcasted_iota(jnp.int32, (n, 128), 1) & 3
    al, ar, bl, br = fl_ref[0], fr_ref[0], fl_ref[1], fr_ref[1]
    low = slot < 2
    r_ref[0] = jnp.where(low, al, ar)
    r_ref[1] = jnp.where(low, pltpu.roll(al, 126, 1), pltpu.roll(ar, 2, 1))
    for k in range(4):
        a = bl if k == 1 else pltpu.roll(bl, (1 - k) & 127, 1)
        b = br if k == 2 else pltpu.roll(br, (2 - k) & 127, 1)
        r_ref[2 + k] = jnp.where(low, a, b)
    for ref, a, e in ((lo_ref, 0, 0), (hi_ref, n - 2, n - 1)):
        ref[0, 0:2, :] = r_ref[0, a : a + 2, :]
        ref[0, 2:4, :] = r_ref[1, a : a + 2, :]
        for k in range(4):
            ref[0, 4 + k : 5 + k, :] = r_ref[2 + k, e : e + 1, :]


def corners(from_left, from_right, lo, hi):
    _, n, _ = from_left.shape
    T = lo.shape[0] - 1
    row = jax.ShapeDtypeStruct(lo.shape, F32)
    return pl.pallas_call(
        functools.partial(corner_kernel, n),
        grid=(1,),
        in_specs=[
            pl.BlockSpec((2, n, 128), lambda g: (0, 0, 0)),
            pl.BlockSpec((2, n, 128), lambda g: (0, 0, 0)),
            pl.BlockSpec(memory_space=pl.ANY),
            pl.BlockSpec(memory_space=pl.ANY),
        ],
        out_specs=[
            pl.BlockSpec((6, n, 128), lambda g: (0, 0, 0)),
            pl.BlockSpec((1, 8, 128), lambda g: (T, 0, 0)),
            pl.BlockSpec((1, 8, 128), lambda g: (T, 0, 0)),
        ],
        out_shape=[jax.ShapeDtypeStruct((6, n, 128), F32), row, row],
        input_output_aliases={2: 1, 3: 2},
        compiler_params=pltpu.CompilerParams(vmem_limit_bytes=16 * MIB),
        cost_estimate=pl.CostEstimate(flops=0, bytes_accessed=40 * n * 128, transcendentals=0),
        name="corners",
    )(from_left, from_right, lo, hi)


def coefficients(f0, f1, free, heated):
    v = jnp.exp(-0.5 * heated)
    w = RELAX_FACTOR * free
    a = w * reciprocal(DRAG_COEFF + 4.0 * v)
    return 1.0 - w, a * v, a * f0, a * f1


def sweep_kernel(
    tb, n, v_ref, f_ref, p_ref, h_ref, lo_ref, hi_ref, r_ref, own_ref,
    out_ref, yh1, yh2, xs, ws, v1s, cos,
):
    S = n // 8
    T = lo_ref.shape[0] - 1
    step = pl.program_id(0)
    lane, sub = iotas()
    slot = lane & 3
    first, last = lane == 0, lane == 127

    def under(row, last_vector):
        return jnp.where(sub == 0, row, pltpu.roll(last_vector, 1, 0))

    def over(row, first_vector):
        return jnp.where(sub == 7, row, pltpu.roll(first_vector, 7, 0))

    def put(todo):
        for ref, c, i, value in todo:
            ref[c, i] = value

    def halo_rows(ref, low, high):
        todo = []
        for c in range(2):
            for q in range(2):
                todo.append((ref, c, q, under(low(2 * c + q), ref[c, S + q])))
                todo.append((ref, c, S + 2 + q, over(high(2 * c + q), ref[c, q + 2])))
        put(todo)

    def halo_coefficients(low, high, get):
        below = coefficients(*[under(low(4 + m), get(m, S - 1)) for m in range(4)])
        above = coefficients(*[over(high(4 + m), get(m, 0)) for m in range(4)])
        put([(cos, m, 0, below[m]) for m in range(4)] + [(cos, m, S + 1, above[m]) for m in range(4)])

    @pl.when(step == 0)
    def _():
        outer = (slot == 0) | (slot == 3)
        sign = jnp.where(slot == 1, -0.25, 0.25)

        def get(m, i):
            return r_ref[2 + m, pl.ds(i, 8, stride=S), :]

        def collect(t, carry):
            own = lane >> 2 == t
            return [
                jnp.where(own, pltpu.roll(ref[t], (4 * t + 2) & 127, 1), acc)
                for ref, acc in zip((lo_ref, hi_ref), carry)
            ]

        zero = jnp.zeros((8, 128), F32)
        own_lo, own_hi = lax.fori_loop(0, T, collect, [zero, zero])
        both_lo = jnp.where(outer, lo_ref[T], own_lo)
        both_hi = jnp.where(outer, hi_ref[T], own_hi)

        def load(rows, _):
            todo = []
            for i in rows:
                for c in range(2):
                    r = r_ref[c, pl.ds(i, 8, stride=S), :]
                    todo.append((xs, c, i + 2, r))
                    todo.append((ws, c, i + 2, jnp.where(outer, r, own_ref[c, pl.ds(i, 8, stride=S), :])))
                co = coefficients(*[get(m, i) for m in range(4)])
                todo += [(cos, m, i + 1, co[m]) for m in range(4)]
            put(todo)
            return 0

        over_rows(S, load, most=4)
        halo_rows(xs, lambda k: lo_ref[T, k : k + 1, :], lambda k: hi_ref[T, k : k + 1, :])
        halo_rows(ws, lambda k: both_lo[k : k + 1, :], lambda k: both_hi[k : k + 1, :])
        halo_coefficients(lambda k: lo_ref[T, k : k + 1, :], lambda k: hi_ref[T, k : k + 1, :], get)

        def relax(rows, _):
            todo = []
            for i in rows:
                r = [[xs[c, i + d] for c in range(2)] for d in (1, 2, 3)]
                w = [[ws[c, i + d] for c in range(2)] for d in (1, 2, 3)]
                for c in range(2):
                    q = 0.25 * (w[2][1 - c] - w[0][1 - c])
                    around = (
                        r[0][c] + r[2][c] + pltpu.roll(w[1][c] + q, 127, 1) + pltpu.roll(w[1][c] - q, 1, 1)
                    )
                    todo.append((yh1, c, i + 1, r[1][c] + sign * (r[2][1 - c] - r[0][1 - c])))
                    new = cos[0, i + 1] * r[1][c] + cos[2 + c, i + 1] + cos[1, i + 1] * around
                    todo.append((v1s, c, i + 1, new))
            put(todo)
            return 0

        over_rows(S, relax, most=4)
        relax([-1, S], 0)

        def edges(rows, _):
            put(
                [
                    (yh2, c, i, v1s[c, i + 1] + sign * (v1s[1 - c, i + 2] - v1s[1 - c, i]))
                    for i in rows
                    for c in range(2)
                ]
            )
            return 0

        over_rows(S, edges)

    def layer(u, _):
        t = step * tb + u
        shift = (126 - 4 * t) & 127

        def update(prev, here, after, i, yh):
            q = [0.25 * (after[c] - prev[c]) for c in range(2)]
            new = []
            for c in range(2):
                edge = pltpu.roll(yh[c], shift, 1)
                up = jnp.where(first, edge, here[c] + q[1 - c])
                down = jnp.where(last, edge, here[c] - q[1 - c])
                around = prev[c] + after[c] + (pltpu.roll(up, 127, 1) + pltpu.roll(down, 1, 1))
                new.append(cos[0, i + 1] * here[c] + cos[2 + c, i + 1] + cos[1, i + 1] * around)
            return new

        def get(m, i):
            rows = pl.ds(i, 8, stride=S)
            if m < 2:
                return f_ref[m, u, rows, :]
            return 1.0 - p_ref[u, rows, :].astype(F32) if m == 2 else h_ref[u, rows, :]

        def load(rows, _):
            todo = []
            for i in rows:
                todo += [(xs, c, i + 2, v_ref[c, u, pl.ds(i, 8, stride=S), :]) for c in range(2)]
                co = coefficients(*[get(m, i) for m in range(4)])
                todo += [(cos, m, i + 1, co[m]) for m in range(4)]
            put(todo)
            return 0

        over_rows(S, load)
        halo_rows(xs, lambda k: lo_ref[t, k : k + 1, :], lambda k: hi_ref[t, k : k + 1, :])
        halo_coefficients(lambda k: lo_ref[t, k : k + 1, :], lambda k: hi_ref[t, k : k + 1, :], get)

        def first_sweep(rows, _):
            todo = []
            for i in rows:
                x = [[xs[c, i + d] for c in range(2)] for d in (1, 2, 3)]
                new = update(*x, i, [yh1[c, i + 1] for c in range(2)])
                todo += [(v1s, c, i + 1, new[c]) for c in range(2)]
            put(todo)
            return 0

        over_rows(S, first_sweep)
        first_sweep([-1, S], 0)

        def second_sweep(rows, _):
            todo = []
            for i in rows:
                x = [[v1s[c, i + d] for c in range(2)] for d in (0, 1, 2)]
                new = update(*x, i, [yh2[c, i] for c in range(2)])
                todo += [(c, i, new[c]) for c in range(2)]
            for c, i, value in todo:
                out_ref[c, u, pl.ds(i, 8, stride=S), :] = value
            return 0

        over_rows(S, second_sweep)
        return 0

    lax.fori_loop(0, tb, layer, 0)


def sweeps(v, f, pinned, heated, lo, hi, r, pk):
    _, T, n, _ = v.shape
    S = n // 8
    tb = 2
    return pl.pallas_call(
        functools.partial(sweep_kernel, tb, n),
        grid=(T // tb,),
        in_specs=[
            pl.BlockSpec((2, tb, n, 128), lambda t: (0, t, 0, 0)),
            pl.BlockSpec((2, tb, n, 128), lambda t: (0, t, 0, 0)),
            pl.BlockSpec((tb, n, 128), lambda t: (t, 0, 0)),
            pl.BlockSpec((tb, n, 128), lambda t: (t, 0, 0)),
            pl.BlockSpec((T + 1, 8, 128), lambda t: (0, 0, 0)),
            pl.BlockSpec((T + 1, 8, 128), lambda t: (0, 0, 0)),
            pl.BlockSpec((6, n, 128), lambda t: (0, 0, 0)),
            pl.BlockSpec((2, n, 128), lambda t: (0, 0, 0)),
        ],
        out_specs=pl.BlockSpec((2, tb, n, 128), lambda t: (0, t, 0, 0)),
        out_shape=jax.ShapeDtypeStruct((2, T, n, 128), F32),
        scratch_shapes=[
            pltpu.VMEM((2, S + 2, 8, 128), F32),
            pltpu.VMEM((2, S, 8, 128), F32),
            pltpu.VMEM((2, S + 4, 8, 128), F32),
            pltpu.VMEM((2, S + 4, 8, 128), F32),
            pltpu.VMEM((2, S + 2, 8, 128), F32),
            pltpu.VMEM((4, S + 2, 8, 128), F32),
        ],
        compiler_params=pltpu.CompilerParams(vmem_limit_bytes=32 * MIB),
        cost_estimate=pl.CostEstimate(flops=60 * T * n * 128, bytes_accessed=32 * T * n * 128, transcendentals=T * n * 128),
        name="sweeps",
    )(v, f, pinned, heated, lo, hi, r, pk)


def shifted(up_going, down_going, axis):
    count = lax.axis_size(axis)
    up = [(i, i + 1) for i in range(count - 1)]
    down = [(j, i) for i, j in up]
    return lax.ppermute(up_going, axis, up), lax.ppermute(down_going, axis, down)


def local(prior, d, v, f, pinned):
    seg, pq = moments(d, prior)
    J = lax.axis_size("wid")
    pqs = [pq] + [lax.ppermute(pq, "wid", [(i, (i + s) % J) for i in range(J)]) for s in range(1, J)]
    pk, lo7, hi7 = pack(v, f, pinned)
    heated, right, left, lo, hi = heat(d, pqs, seg, prior, pk, lo7, hi7)
    from_left, from_right = shifted(right, left, "len")
    r, lo, hi = corners(from_left, from_right, lo, hi)
    from_below, from_above = shifted(hi, lo, "wid")
    flow = sweeps(v, f, pinned, heated, from_below, from_above, r, pk)
    return heated, flow


def solution(mesh):
    in_specs = (
        P(None, "wid", "len"),
        P(None, "len"),
        P(None, None, "wid", "len"),
        P(None, None, "wid", "len"),
        P(None, "wid", "len"),
    )
    out_specs = (P(None, "wid", "len"), P(None, None, "wid", "len"))
    return jax.shard_map(local, mesh=mesh, in_specs=in_specs, out_specs=out_specs, check_vma=False)
```

```python
import functools

import jax
import jax.numpy as jnp
from jax import lax
from jax.experimental import pallas as pl
from jax.experimental.pallas import tpu as pltpu
from jax.sharding import PartitionSpec as P

DRAG_COEFF = 0.5
RELAX_FACTOR = 0.8
F32 = jnp.float32
MIB = 1 << 20


def decay(d):
    x = 1.0 / d
    one_less = jnp.sqrt(x + 0.25 * x * x) - 0.5 * x
    r = 1.0 - one_less
    return r, (1.0 - r) / (1.0 + r)


def power(r, n):
    out = None
    while n:
        if n & 1:
            out = r if out is None else out * r
        n >>= 1
        if n:
            r = r * r
    return out


def sublane_powers(r, shape):
    s = lax.broadcasted_iota(jnp.int32, shape, 0)
    r2 = r * r
    r4 = r2 * r2
    one = jnp.ones(shape, F32)
    return (
        jnp.where((s & 1) != 0, r, one)
        * jnp.where((s & 2) != 0, r2, one)
        * jnp.where((s & 4) != 0, r4, one)
    )


def reciprocal(x):
    y = pl.reciprocal(x, approx=True)
    return y * (2.0 - x * y)


def batches(lo, hi, most=11):
    parts = -(-(hi - lo) // most)
    cuts = [lo + (hi - lo) * k // parts for k in range(parts + 1)]
    return [range(a, b) for a, b in zip(cuts, cuts[1:])]


def over_rows(count, body, most=8):
    most = min(most, count)

    def step(k, _):
        body(k * most, most)
        return 0

    lax.fori_loop(0, count // most, step, 0)


def iotas():
    lane = lax.broadcasted_iota(jnp.int32, (8, 128), 1)
    sub = lax.broadcasted_iota(jnp.int32, (8, 128), 0)
    return lane, sub


def moments_kernel(tb, n, d_ref, f_ref, seg_ref, pq_ref):
    S = n // 8
    base = pl.program_id(0) * tb
    G = 4
    for g in range(tb // G):
        rs = []
        for u in range(G):
            r, _ = decay(d_ref[pl.ds(base + g * G + u, 1), :])
            rs.append(jnp.broadcast_to(r, (8, 128)))
        fwd = [f_ref[g * G + u, pl.ds(0, 8, stride=S), :] for u in range(G)]
        bwd, weight = list(fwd), list(rs)
        for i in range(1, S):
            for u in range(G):
                x = f_ref[g * G + u, pl.ds(i, 8, stride=S), :]
                fwd[u] = fwd[u] * rs[u] + x
                bwd[u] = bwd[u] + weight[u] * x
                weight[u] = weight[u] * rs[u]
        for u in range(G):
            k = g * G + u
            seg_ref[0, k] = fwd[u]
            seg_ref[1, k] = bwd[u]
            rS = power(rs[u], S)
            up = sublane_powers(rS, (8, 128))
            s = lax.broadcasted_iota(jnp.int32, (8, 128), 0)
            rS2 = rS * rS
            one = jnp.ones((8, 128), F32)
            down = (
                jnp.where((s & 1) == 0, rS, one)
                * jnp.where((s & 2) == 0, rS2, one)
                * jnp.where((s & 4) == 0, rS2 * rS2, one)
            )
            pq_ref[0, k : k + 1, :] = jnp.sum(fwd[u] * down, axis=0, keepdims=True)
            pq_ref[1, k : k + 1, :] = jnp.sum(bwd[u] * up, axis=0, keepdims=True)


def moments(d, prior):
    T, n, _ = prior.shape
    tb = 8
    return pl.pallas_call(
        functools.partial(moments_kernel, tb, n),
        grid=(T // tb,),
        in_specs=[
            pl.BlockSpec((T, 128), lambda t: (0, 0)),
            pl.BlockSpec((tb, n, 128), lambda t: (t, 0, 0)),
        ],
        out_specs=[
            pl.BlockSpec((2, tb, 8, 128), lambda t: (0, t, 0, 0)),
            pl.BlockSpec((2, tb, 128), lambda t: (0, t, 0)),
        ],
        out_shape=[
            jax.ShapeDtypeStruct((2, T, 8, 128), F32),
            jax.ShapeDtypeStruct((2, T, 128), F32),
        ],
        compiler_params=pltpu.CompilerParams(vmem_limit_bytes=60 * MIB),
        cost_estimate=pl.CostEstimate(flops=4 * T * n * 128, bytes_accessed=4 * T * n * 128, transcendentals=0),
        name="moments",
    )(d, prior)


def pack_kernel(tb, n, v_ref, f_ref, p_ref, pk_ref, lo_ref, hi_ref):
    base = pl.program_id(0) * tb
    chunk = min(64, n)
    group = lax.broadcasted_iota(jnp.int32, (chunk, 128), 1) >> 2

    def body(m, _):
        rows = pl.ds(pl.multiple_of(m * chunk, chunk), chunk)
        packed = []
        for k in range(5):
            acc = pk_ref[k, rows, :]
            for u in range(tb):
                if k < 2:
                    x = v_ref[k, u, rows, :]
                elif k < 4:
                    x = f_ref[k - 2, u, rows, :]
                else:
                    x = 1.0 - p_ref[u, rows, :].astype(F32)
                t = base + u
                acc = jnp.where(group == t, pltpu.roll(x, (4 * t + 2) & 127, 1), acc)
            packed.append(acc)
        for k in range(5):
            pk_ref[k, rows, :] = packed[k]
        return 0

    lax.fori_loop(0, n // chunk, body, 0)
    _, sub = iotas()

    def stack(v0, v1, f0, f1, fr):
        out = jnp.where(sub < 2, v0, v1)
        out = jnp.where(sub >= 4, f0, out)
        out = jnp.where(sub >= 5, f1, out)
        return jnp.where(sub >= 6, fr, out)

    tiles = []
    for u in range(tb):
        for top, at, shifts in ((True, 0, (0, 2, 4, 5, 6)), (False, n - 8, (2, 4, 5, 6, 7))):
            rows = pl.ds(at, 8)
            raw = [v_ref[0, u, rows, :], v_ref[1, u, rows, :], f_ref[0, u, rows, :], f_ref[1, u, rows, :]]
            raw.append(1.0 - p_ref[u, rows, :].astype(F32))
            tiles.append((u, top, stack(*[pltpu.roll(x, q, 0) if q else x for x, q in zip(raw, shifts)])))
    for u, top, tile in tiles:
        (lo_ref if top else hi_ref)[u] = tile


def pack(v, f, pinned):
    _, T, n, _ = v.shape
    tb = 4
    row = jax.ShapeDtypeStruct((T, 8, 128), F32)
    return pl.pallas_call(
        functools.partial(pack_kernel, tb, n),
        grid=(T // tb,),
        in_specs=[
            pl.BlockSpec((2, tb, n, 128), lambda t: (0, t, 0, 0)),
            pl.BlockSpec((2, tb, n, 128), lambda t: (0, t, 0, 0)),
            pl.BlockSpec((tb, n, 128), lambda t: (t, 0, 0)),
        ],
        out_specs=[
            pl.BlockSpec((5, n, 128), lambda t: (0, 0, 0)),
            pl.BlockSpec((tb, 8, 128), lambda t: (t, 0, 0)),
            pl.BlockSpec((tb, 8, 128), lambda t: (t, 0, 0)),
        ],
        out_shape=[jax.ShapeDtypeStruct((5, n, 128), F32), row, row],
        compiler_params=pltpu.CompilerParams(vmem_limit_bytes=60 * MIB),
        cost_estimate=pl.CostEstimate(flops=5 * T * n * 128, bytes_accessed=20 * T * n * 128, transcendentals=0),
        name="pack_edges",
    )(v, f, pinned)


def heat_kernel(J, tb, n, *refs):
    d_ref, *pq_refs = refs[: J + 1]
    (
        seg_ref, f_ref, pk_ref, lo7_ref, hi7_ref,
        out_ref, right_ref, left_ref, lo_ref, hi_ref, alls, sums, pkh, ys,
    ) = refs[J + 1 :]
    S = n // 8
    step = pl.program_id(0)
    base = step * tb

    @pl.when(step == 0)
    def _():
        j = lax.axis_index("wid")
        for s in range(J):
            alls[lax.rem(j - s + J, J)] = pq_refs[s][...]
        r, _ = decay(d_ref[...])
        rn = power(r, n)
        rN = power(rn, J)
        sp = alls[0, 0]
        for i in range(1, J):
            sp = sp * rn + alls[i, 0]
        sq = alls[J - 1, 1]
        for i in range(J - 2, -1, -1):
            sq = sq * rn + alls[i, 1]
        inv = 1.0 / (1.0 - rN * rN)
        left = (sq + rN * sp) * inv
        right = (sp + rN * sq) * inv
        for i in range(J - 1):
            left = jnp.where(i < j, rn * left + alls[i, 0], left)
        for i in range(J - 1, 0, -1):
            right = jnp.where(i > j, rn * right + alls[i, 1], right)
        sums[0] = left
        sums[1] = right

    _, sub = iotas()
    rs, gain, y, z = [], [], [], []
    for u in range(tb):
        t = base + u
        r, a0 = decay(d_ref[pl.ds(t, 1), :])
        r = jnp.broadcast_to(r, (8, 128))
        a0 = jnp.broadcast_to(a0, (8, 128))
        rS = power(r, S)
        rS2 = rS * rS
        rS4 = rS2 * rS2
        c = jnp.where(sub == 0, sums[0, pl.ds(t, 1), :], pltpu.roll(seg_ref[0, u], 1, 0))
        b = jnp.where(sub == 7, sums[1, pl.ds(t, 1), :], pltpu.roll(seg_ref[1, u], 7, 0))
        for s, q in ((1, rS), (2, rS2), (4, rS4)):
            c = c + q * jnp.where(sub >= s, pltpu.roll(c, s, 0), 0.0)
            b = b + q * jnp.where(sub < 8 - s, pltpu.roll(b, 8 - s, 0), 0.0)
        rs.append(r)
        gain.append(a0)
        y.append(c)
        z.append(b)
    for rows in batches(0, S, 8):
        done = []
        for i in rows:
            for u in range(tb):
                y[u] = y[u] * rs[u] + f_ref[u, pl.ds(i, 8, stride=S), :]
                done.append((u, i, y[u]))
        for u, i, value in done:
            ys[u, i] = value
    for rows in batches(0, S, 8)[::-1]:
        done = []
        for i in rows[::-1]:
            for u in range(tb):
                zr = z[u] * rs[u]
                done.append((u, i, gain[u] * (ys[u, i] + zr)))
                z[u] = zr + f_ref[u, pl.ds(i, 8, stride=S), :]
        for u, i, value in done:
            out_ref[u, pl.ds(i, 8, stride=S), :] = value

    lane_n = lax.broadcasted_iota(jnp.int32, (n, 128), 1)
    group = lane_n >> 2
    acc = pkh[...]
    for u in range(tb):
        t = base + u
        acc = jnp.where(group == t, pltpu.roll(out_ref[u], (4 * t + 2) & 127, 1), acc)
    pkh[...] = acc
    lows = [jnp.where(sub == 7, out_ref[u, 0:1, :], lo7_ref[u]) for u in range(tb)]
    highs = [jnp.where(sub == 7, out_ref[u, n - 1 : n, :], hi7_ref[u]) for u in range(tb)]
    for u in range(tb):
        lo_ref[u] = lows[u]
        hi_ref[u] = highs[u]

    @pl.when(step == pl.num_programs(0) - 1)
    def _():
        slot = lane_n & 3
        v0, v1, f0, f1, fr, he = pk_ref[0], pk_ref[1], pk_ref[2], pk_ref[3], pk_ref[4], pkh[...]

        def sel(a, b, c, d):
            return jnp.where(slot < 2, jnp.where(slot == 0, a, b), jnp.where(slot == 2, c, d))

        right_ref[0] = jnp.where(slot < 2, v0, pltpu.roll(v1, 2, 1))
        left_ref[0] = jnp.where(slot >= 2, v0, pltpu.roll(v1, 126, 1))
        right_ref[1] = sel(pltpu.roll(f0, 127, 1), f1, pltpu.roll(fr, 1, 1), pltpu.roll(he, 2, 1))
        left_ref[1] = sel(pltpu.roll(f0, 126, 1), pltpu.roll(f1, 127, 1), fr, pltpu.roll(he, 1, 1))


def heat(d, pqs, seg, prior, pk, lo7, hi7):
    T, n, _ = prior.shape
    J = len(pqs)
    tb = 4
    row = jax.ShapeDtypeStruct((T + 1, 8, 128), F32)
    return pl.pallas_call(
        functools.partial(heat_kernel, J, tb, n),
        grid=(T // tb,),
        in_specs=[
            pl.BlockSpec((T, 128), lambda t: (0, 0)),
            *[pl.BlockSpec((2, T, 128), lambda t: (0, 0, 0)) for _ in range(J)],
            pl.BlockSpec((2, tb, 8, 128), lambda t: (0, t, 0, 0)),
            pl.BlockSpec((tb, n, 128), lambda t: (t, 0, 0)),
            pl.BlockSpec((5, n, 128), lambda t: (0, 0, 0)),
            pl.BlockSpec((tb, 8, 128), lambda t: (t, 0, 0)),
            pl.BlockSpec((tb, 8, 128), lambda t: (t, 0, 0)),
        ],
        out_specs=[
            pl.BlockSpec((tb, n, 128), lambda t: (t, 0, 0)),
            pl.BlockSpec((2, n, 128), lambda t: (0, 0, 0)),
            pl.BlockSpec((2, n, 128), lambda t: (0, 0, 0)),
            pl.BlockSpec((tb, 8, 128), lambda t: (t, 0, 0)),
            pl.BlockSpec((tb, 8, 128), lambda t: (t, 0, 0)),
        ],
        out_shape=[
            jax.ShapeDtypeStruct((T, n, 128), F32),
            jax.ShapeDtypeStruct((2, n, 128), F32),
            jax.ShapeDtypeStruct((2, n, 128), F32),
            row,
            row,
        ],
        scratch_shapes=[
            pltpu.VMEM((J, 2, T, 128), F32),
            pltpu.VMEM((2, T, 128), F32),
            pltpu.VMEM((n, 128), F32),
            pltpu.VMEM((tb, n // 8, 8, 128), F32),
        ],
        compiler_params=pltpu.CompilerParams(vmem_limit_bytes=60 * MIB),
        cost_estimate=pl.CostEstimate(flops=10 * T * n * 128, bytes_accessed=8 * T * n * 128, transcendentals=0),
        name="heat",
    )(d, *pqs, seg, prior, pk, lo7, hi7)


def corner_kernel(n, fl_ref, fr_ref, lo_in, hi_in, r_ref, lo_ref, hi_ref):
    slot = lax.broadcasted_iota(jnp.int32, (n, 128), 1) & 3
    al, ar, bl, br = fl_ref[0], fr_ref[0], fl_ref[1], fr_ref[1]
    low = slot < 2
    r_ref[0] = jnp.where(low, al, ar)
    r_ref[1] = jnp.where(low, pltpu.roll(al, 126, 1), pltpu.roll(ar, 2, 1))
    for k in range(4):
        a = bl if k == 1 else pltpu.roll(bl, (1 - k) & 127, 1)
        b = br if k == 2 else pltpu.roll(br, (2 - k) & 127, 1)
        r_ref[2 + k] = jnp.where(low, a, b)
    for ref, a, e in ((lo_ref, 0, 0), (hi_ref, n - 2, n - 1)):
        ref[0, 0:2, :] = r_ref[0, a : a + 2, :]
        ref[0, 2:4, :] = r_ref[1, a : a + 2, :]
        for k in range(4):
            ref[0, 4 + k : 5 + k, :] = r_ref[2 + k, e : e + 1, :]


def corners(from_left, from_right, lo, hi):
    _, n, _ = from_left.shape
    T = lo.shape[0] - 1
    row = jax.ShapeDtypeStruct(lo.shape, F32)
    return pl.pallas_call(
        functools.partial(corner_kernel, n),
        grid=(1,),
        in_specs=[
            pl.BlockSpec((2, n, 128), lambda g: (0, 0, 0)),
            pl.BlockSpec((2, n, 128), lambda g: (0, 0, 0)),
            pl.BlockSpec(memory_space=pl.ANY),
            pl.BlockSpec(memory_space=pl.ANY),
        ],
        out_specs=[
            pl.BlockSpec((6, n, 128), lambda g: (0, 0, 0)),
            pl.BlockSpec((1, 8, 128), lambda g: (T, 0, 0)),
            pl.BlockSpec((1, 8, 128), lambda g: (T, 0, 0)),
        ],
        out_shape=[jax.ShapeDtypeStruct((6, n, 128), F32), row, row],
        input_output_aliases={2: 1, 3: 2},
        compiler_params=pltpu.CompilerParams(vmem_limit_bytes=60 * MIB),
        cost_estimate=pl.CostEstimate(flops=0, bytes_accessed=40 * n * 128, transcendentals=0),
        name="corners",
    )(from_left, from_right, lo, hi)


def coefficients(f0, f1, free, heated):
    v = jnp.exp(-0.5 * heated)
    w = RELAX_FACTOR * free
    a = w * reciprocal(DRAG_COEFF + 4.0 * v)
    return 1.0 - w, a * v, a * f0, a * f1


def under(row, last_vector):
    _, sub = iotas()
    return jnp.where(sub == 0, row, pltpu.roll(last_vector, 1, 0))


def over(row, first_vector):
    _, sub = iotas()
    return jnp.where(sub == 7, row, pltpu.roll(first_vector, 7, 0))


def put(todo):
    for ref, c, i, value in todo:
        ref[c, i] = value


def halo_rows(ref, S, low, high):
    todo = []
    for c in range(2):
        for q in range(2):
            todo.append((ref, c, q, under(low(2 * c + q), ref[c, S + q])))
            todo.append((ref, c, S + 2 + q, over(high(2 * c + q), ref[c, q + 2])))
    put(todo)


def halo_coefficients(cos, S, low, high, get):
    below = coefficients(*[under(low(4 + m), get(m, S - 1)) for m in range(4)])
    above = coefficients(*[over(high(4 + m), get(m, 0)) for m in range(4)])
    put([(cos, m, 0, below[m]) for m in range(4)] + [(cos, m, S + 1, above[m]) for m in range(4)])


def strip_kernel(n, lo_ref, hi_ref, r_ref, own_ref, yh1, yh2, xs, ws, r1s, cos):
    S = n // 8
    T = lo_ref.shape[0] - 1
    lane, _ = iotas()
    slot = lane & 3
    outer = (slot == 0) | (slot == 3)
    sign = jnp.where(slot == 1, -0.25, 0.25)

    def low(k):
        return lo_ref[T, k : k + 1, :]

    def high(k):
        return hi_ref[T, k : k + 1, :]

    def get(m, i):
        return r_ref[2 + m, pl.ds(i, 8, stride=S), :]

    def collect(t, carry):
        own = lane >> 2 == t
        return [
            jnp.where(own, pltpu.roll(ref[t], (4 * t + 2) & 127, 1), acc)
            for ref, acc in zip((lo_ref, hi_ref), carry)
        ]

    zero = jnp.zeros((8, 128), F32)
    own_lo, own_hi = lax.fori_loop(0, T, collect, [zero, zero])
    both_lo = jnp.where(outer, lo_ref[T], own_lo)
    both_hi = jnp.where(outer, hi_ref[T], own_hi)

    def load(start, m):
        todo = []
        for i in [start + j for j in range(m)]:
            for c in range(2):
                r = r_ref[c, pl.ds(i, 8, stride=S), :]
                todo.append((xs, c, i + 2, r))
                todo.append((ws, c, i + 2, jnp.where(outer, r, own_ref[c, pl.ds(i, 8, stride=S), :])))
            co = coefficients(*[get(q, i) for q in range(4)])
            todo += [(cos, q, i + 1, co[q]) for q in range(4)]
        put(todo)

    over_rows(S, load)
    halo_rows(xs, S, low, high)
    halo_rows(ws, S, lambda k: both_lo[k : k + 1, :], lambda k: both_hi[k : k + 1, :])
    halo_coefficients(cos, S, low, high, get)

    def relax(start, m):
        r = [[xs[c, start + 1 + j] for c in range(2)] for j in range(m + 2)]
        w = [[ws[c, start + 1 + j] for c in range(2)] for j in range(m + 2)]
        todo = []
        for j in range(m):
            i = start + j
            for c in range(2):
                q = 0.25 * (w[j + 2][1 - c] - w[j][1 - c])
                around = (
                    r[j][c] + r[j + 2][c] + pltpu.roll(w[j + 1][c] + q, 127, 1) + pltpu.roll(w[j + 1][c] - q, 1, 1)
                )
                todo.append((yh1, c, i + 1, r[j + 1][c] + sign * (r[j + 2][1 - c] - r[j][1 - c])))
                new = cos[0, i + 1] * r[j + 1][c] + cos[2 + c, i + 1] + cos[1, i + 1] * around
                todo.append((r1s, c, i + 1, new))
        put(todo)

    over_rows(S, relax)
    relax(-1, 1)
    relax(S, 1)

    def edges(start, m):
        r = [[r1s[c, start + j] for c in range(2)] for j in range(m + 2)]
        put(
            [
                (yh2, c, start + j, r[j + 1][c] + sign * (r[j + 2][1 - c] - r[j][1 - c]))
                for j in range(m)
                for c in range(2)
            ]
        )

    over_rows(S, edges)


def strips(lo, hi, r, pk):
    n = r.shape[1]
    S = n // 8
    whole = lambda shape: pl.BlockSpec(shape, lambda g: (0,) * len(shape))
    return pl.pallas_call(
        functools.partial(strip_kernel, n),
        grid=(1,),
        in_specs=[whole(lo.shape), whole(hi.shape), whole(r.shape), whole((2, n, 128))],
        out_specs=[whole((2, S + 2, 8, 128)), whole((2, S, 8, 128))],
        out_shape=[
            jax.ShapeDtypeStruct((2, S + 2, 8, 128), F32),
            jax.ShapeDtypeStruct((2, S, 8, 128), F32),
        ],
        scratch_shapes=[
            pltpu.VMEM((2, S + 4, 8, 128), F32),
            pltpu.VMEM((2, S + 4, 8, 128), F32),
            pltpu.VMEM((2, S + 2, 8, 128), F32),
            pltpu.VMEM((4, S + 2, 8, 128), F32),
        ],
        compiler_params=pltpu.CompilerParams(vmem_limit_bytes=60 * MIB),
        cost_estimate=pl.CostEstimate(flops=60 * n * 128, bytes_accessed=60 * n * 128, transcendentals=n * 128),
        name="strips",
    )(lo, hi, r, pk)


def sweep_kernel(tb, n, v_ref, f_ref, p_ref, h_ref, lo_ref, hi_ref, yh1, yh2, out_ref, xs, v1s, cos):
    S = n // 8
    step = pl.program_id(0)
    lane, _ = iotas()
    first, last = lane == 0, lane == 127

    def layer(u, _):
        t = step * tb + u
        shift = (126 - 4 * t) & 127

        def low(k):
            return lo_ref[t, k : k + 1, :]

        def high(k):
            return hi_ref[t, k : k + 1, :]

        def get(m, i):
            rows = pl.ds(i, 8, stride=S)
            if m < 2:
                return f_ref[m, u, rows, :]
            return 1.0 - p_ref[u, rows, :].astype(F32) if m == 2 else h_ref[u, rows, :]

        def load(start, m):
            todo = []
            for i in [start + j for j in range(m)]:
                todo += [(xs, c, i + 2, v_ref[c, u, pl.ds(i, 8, stride=S), :]) for c in range(2)]
                co = coefficients(*[get(q, i) for q in range(4)])
                todo += [(cos, q, i + 1, co[q]) for q in range(4)]
            put(todo)

        def sweep(src, off, yh, start, m):
            x = [[src[c, start + off + j] for c in range(2)] for j in range(m + 2)]
            done = []
            for j in range(m):
                i = start + j
                prev, here, after = x[j], x[j + 1], x[j + 2]
                q = [0.25 * (after[c] - prev[c]) for c in range(2)]
                k, g = cos[0, i + 1], cos[1, i + 1]
                for c in range(2):
                    edge = pltpu.roll(yh[c, i + off], shift, 1)
                    up = jnp.where(first, edge, here[c] + q[1 - c])
                    down = jnp.where(last, edge, here[c] - q[1 - c])
                    around = prev[c] + after[c] + (pltpu.roll(up, 127, 1) + pltpu.roll(down, 1, 1))
                    done.append((c, i, k * here[c] + cos[2 + c, i + 1] + g * around))
            return done

        def first_sweep(start, m):
            put([(v1s, c, i + 1, value) for c, i, value in sweep(xs, 1, yh1, start, m)])

        def second_sweep(start, m):
            for c, i, value in sweep(v1s, 0, yh2, start, m):
                out_ref[c, u, pl.ds(i, 8, stride=S), :] = value

        over_rows(S, load, 16)
        halo_rows(xs, S, low, high)
        halo_coefficients(cos, S, low, high, get)
        over_rows(S, first_sweep, 16)
        first_sweep(-1, 1)
        first_sweep(S, 1)
        over_rows(S, second_sweep, 16)
        return 0

    lax.fori_loop(0, tb, layer, 0)


def sweeps(v, f, pinned, heated, lo, hi, yh1, yh2):
    _, T, n, _ = v.shape
    S = n // 8
    tb = 2
    whole = lambda shape: pl.BlockSpec(shape, lambda t: (0,) * len(shape))
    return pl.pallas_call(
        functools.partial(sweep_kernel, tb, n),
        grid=(T // tb,),
        in_specs=[
            pl.BlockSpec((2, tb, n, 128), lambda t: (0, t, 0, 0)),
            pl.BlockSpec((2, tb, n, 128), lambda t: (0, t, 0, 0)),
            pl.BlockSpec((tb, n, 128), lambda t: (t, 0, 0)),
            pl.BlockSpec((tb, n, 128), lambda t: (t, 0, 0)),
            whole((T + 1, 8, 128)),
            whole((T + 1, 8, 128)),
            whole((2, S + 2, 8, 128)),
            whole((2, S, 8, 128)),
        ],
        out_specs=pl.BlockSpec((2, tb, n, 128), lambda t: (0, t, 0, 0)),
        out_shape=jax.ShapeDtypeStruct((2, T, n, 128), F32),
        scratch_shapes=[
            pltpu.VMEM((2, S + 4, 8, 128), F32),
            pltpu.VMEM((2, S + 2, 8, 128), F32),
            pltpu.VMEM((4, S + 2, 8, 128), F32),
        ],
        compiler_params=pltpu.CompilerParams(vmem_limit_bytes=60 * MIB),
        cost_estimate=pl.CostEstimate(
            flops=60 * T * n * 128, bytes_accessed=32 * T * n * 128, transcendentals=T * n * 128
        ),
        name="sweeps",
    )(v, f, pinned, heated, lo, hi, yh1, yh2)


def shifted(up_going, down_going, axis):
    count = lax.axis_size(axis)
    up = [(i, i + 1) for i in range(count - 1)]
    down = [(j, i) for i, j in up]
    return lax.ppermute(up_going, axis, up), lax.ppermute(down_going, axis, down)


def local(prior, d, v, f, pinned):
    seg, pq = moments(d, prior)
    J = lax.axis_size("wid")
    pqs = [pq] + [lax.ppermute(pq, "wid", [(i, (i + s) % J) for i in range(J)]) for s in range(1, J)]
    pk, lo7, hi7 = pack(v, f, pinned)
    heated, right, left, lo, hi = heat(d, pqs, seg, prior, pk, lo7, hi7)
    from_left, from_right = shifted(right, left, "len")
    r, lo, hi = corners(from_left, from_right, lo, hi)
    from_below, from_above = shifted(hi, lo, "wid")
    yh1, yh2 = strips(from_below, from_above, r, pk)
    flow = sweeps(v, f, pinned, heated, from_below, from_above, yh1, yh2)
    return heated, flow


def solution(mesh):
    in_specs = (
        P(None, "wid", "len"),
        P(None, "len"),
        P(None, None, "wid", "len"),
        P(None, None, "wid", "len"),
        P(None, "wid", "len"),
    )
    out_specs = (P(None, "wid", "len"), P(None, None, "wid", "len"))
    return jax.shard_map(local, mesh=mesh, in_specs=in_specs, out_specs=out_specs, check_vma=False)
```

```python
import functools

import jax
import jax.numpy as jnp
from jax import lax
from jax.experimental import pallas as pl
from jax.experimental.pallas import tpu as pltpu
from jax.sharding import PartitionSpec as P

DRAG_COEFF = 0.5
RELAX_FACTOR = 0.8
F32 = jnp.float32
MIB = 1 << 20


def decay(d):
    x = 1.0 / d
    one_less = jnp.sqrt(x + 0.25 * x * x) - 0.5 * x
    r = 1.0 - one_less
    return r, (1.0 - r) / (1.0 + r)


def power(r, n):
    out = None
    while n:
        if n & 1:
            out = r if out is None else out * r
        n >>= 1
        if n:
            r = r * r
    return out


def sublane_powers(r, shape):
    s = lax.broadcasted_iota(jnp.int32, shape, 0)
    r2 = r * r
    r4 = r2 * r2
    one = jnp.ones(shape, F32)
    return (
        jnp.where((s & 1) != 0, r, one)
        * jnp.where((s & 2) != 0, r2, one)
        * jnp.where((s & 4) != 0, r4, one)
    )


def reciprocal(x):
    y = pl.reciprocal(x, approx=True)
    return y * (2.0 - x * y)


def batches(lo, hi, most=11):
    parts = -(-(hi - lo) // most)
    cuts = [lo + (hi - lo) * k // parts for k in range(parts + 1)]
    return [range(a, b) for a, b in zip(cuts, cuts[1:])]


def over_rows(first, stop, body, most=8):
    count = stop - first
    m = max(k for k in range(1, most + 1) if count % k == 0)

    def step(k, _):
        body(first + k * m, m)
        return 0

    lax.fori_loop(0, count // m, step, 0)


def iotas():
    lane = lax.broadcasted_iota(jnp.int32, (8, 128), 1)
    sub = lax.broadcasted_iota(jnp.int32, (8, 128), 0)
    return lane, sub


def moments_kernel(tb, n, d_ref, f_ref, seg_ref, pq_ref):
    S = n // 8
    base = pl.program_id(0) * tb
    G = 4
    for g in range(tb // G):
        rs = []
        for u in range(G):
            r, _ = decay(d_ref[pl.ds(base + g * G + u, 1), :])
            rs.append(jnp.broadcast_to(r, (8, 128)))
        fwd = [f_ref[g * G + u, pl.ds(0, 8, stride=S), :] for u in range(G)]
        bwd, weight = list(fwd), list(rs)
        for i in range(1, S):
            for u in range(G):
                x = f_ref[g * G + u, pl.ds(i, 8, stride=S), :]
                fwd[u] = fwd[u] * rs[u] + x
                bwd[u] = bwd[u] + weight[u] * x
                weight[u] = weight[u] * rs[u]
        for u in range(G):
            k = g * G + u
            seg_ref[0, k] = fwd[u]
            seg_ref[1, k] = bwd[u]
            rS = power(rs[u], S)
            up = sublane_powers(rS, (8, 128))
            s = lax.broadcasted_iota(jnp.int32, (8, 128), 0)
            rS2 = rS * rS
            one = jnp.ones((8, 128), F32)
            down = (
                jnp.where((s & 1) == 0, rS, one)
                * jnp.where((s & 2) == 0, rS2, one)
                * jnp.where((s & 4) == 0, rS2 * rS2, one)
            )
            pq_ref[0, k : k + 1, :] = jnp.sum(fwd[u] * down, axis=0, keepdims=True)
            pq_ref[1, k : k + 1, :] = jnp.sum(bwd[u] * up, axis=0, keepdims=True)


def moments(d, prior):
    T, n, _ = prior.shape
    tb = 8
    return pl.pallas_call(
        functools.partial(moments_kernel, tb, n),
        grid=(T // tb,),
        in_specs=[
            pl.BlockSpec((T, 128), lambda t: (0, 0)),
            pl.BlockSpec((tb, n, 128), lambda t: (t, 0, 0)),
        ],
        out_specs=[
            pl.BlockSpec((2, tb, 8, 128), lambda t: (0, t, 0, 0)),
            pl.BlockSpec((2, tb, 128), lambda t: (0, t, 0)),
        ],
        out_shape=[
            jax.ShapeDtypeStruct((2, T, 8, 128), F32),
            jax.ShapeDtypeStruct((2, T, 128), F32),
        ],
        compiler_params=pltpu.CompilerParams(vmem_limit_bytes=60 * MIB),
        cost_estimate=pl.CostEstimate(flops=4 * T * n * 128, bytes_accessed=4 * T * n * 128, transcendentals=0),
        name="moments",
    )(d, prior)


def pack_kernel(tb, n, v_ref, f_ref, p_ref, pk_ref, lo_ref, hi_ref):
    base = pl.program_id(0) * tb
    lane = lax.broadcasted_iota(jnp.int32, (n, 128), 1)
    group = lane >> 2
    for k in range(5):
        acc = pk_ref[k]
        for u in range(tb):
            if k < 2:
                x = v_ref[k, u]
            elif k < 4:
                x = f_ref[k - 2, u]
            else:
                x = 1.0 - p_ref[u].astype(F32)
            t = base + u
            acc = jnp.where(group == t, pltpu.roll(x, (4 * t + 2) & 127, 1), acc)
        pk_ref[k] = acc
    _, sub = iotas()

    def stack(v0, v1, f0, f1, fr):
        out = jnp.where(sub < 2, v0, v1)
        out = jnp.where(sub >= 4, f0, out)
        out = jnp.where(sub >= 5, f1, out)
        return jnp.where(sub >= 6, fr, out)

    tiles = []
    for u in range(tb):
        for top, at, shifts in ((True, 0, (0, 2, 4, 5, 6)), (False, n - 8, (2, 4, 5, 6, 7))):
            rows = pl.ds(at, 8)
            raw = [v_ref[0, u, rows, :], v_ref[1, u, rows, :], f_ref[0, u, rows, :], f_ref[1, u, rows, :]]
            raw.append(1.0 - p_ref[u, rows, :].astype(F32))
            tiles.append((u, top, stack(*[pltpu.roll(x, q, 0) if q else x for x, q in zip(raw, shifts)])))
    for u, top, tile in tiles:
        (lo_ref if top else hi_ref)[u] = tile


def pack(v, f, pinned):
    _, T, n, _ = v.shape
    tb = 4
    row = jax.ShapeDtypeStruct((T, 8, 128), F32)
    return pl.pallas_call(
        functools.partial(pack_kernel, tb, n),
        grid=(T // tb,),
        in_specs=[
            pl.BlockSpec((2, tb, n, 128), lambda t: (0, t, 0, 0)),
            pl.BlockSpec((2, tb, n, 128), lambda t: (0, t, 0, 0)),
            pl.BlockSpec((tb, n, 128), lambda t: (t, 0, 0)),
        ],
        out_specs=[
            pl.BlockSpec((5, n, 128), lambda t: (0, 0, 0)),
            pl.BlockSpec((tb, 8, 128), lambda t: (t, 0, 0)),
            pl.BlockSpec((tb, 8, 128), lambda t: (t, 0, 0)),
        ],
        out_shape=[jax.ShapeDtypeStruct((5, n, 128), F32), row, row],
        compiler_params=pltpu.CompilerParams(vmem_limit_bytes=60 * MIB),
        cost_estimate=pl.CostEstimate(flops=5 * T * n * 128, bytes_accessed=20 * T * n * 128, transcendentals=0),
        name="pack_edges",
    )(v, f, pinned)


def heat_kernel(J, tb, n, *refs):
    d_ref, *pq_refs = refs[: J + 1]
    (
        seg_ref, f_ref, pk_ref, lo7_ref, hi7_ref,
        out_ref, right_ref, left_ref, lo_ref, hi_ref, alls, sums, pkh, ys,
    ) = refs[J + 1 :]
    S = n // 8
    step = pl.program_id(0)
    base = step * tb

    @pl.when(step == 0)
    def _():
        j = lax.axis_index("wid")
        for s in range(J):
            alls[lax.rem(j - s + J, J)] = pq_refs[s][...]
        r, _ = decay(d_ref[...])
        rn = power(r, n)
        rN = power(rn, J)
        sp = alls[0, 0]
        for i in range(1, J):
            sp = sp * rn + alls[i, 0]
        sq = alls[J - 1, 1]
        for i in range(J - 2, -1, -1):
            sq = sq * rn + alls[i, 1]
        inv = 1.0 / (1.0 - rN * rN)
        left = (sq + rN * sp) * inv
        right = (sp + rN * sq) * inv
        for i in range(J - 1):
            left = jnp.where(i < j, rn * left + alls[i, 0], left)
        for i in range(J - 1, 0, -1):
            right = jnp.where(i > j, rn * right + alls[i, 1], right)
        sums[0] = left
        sums[1] = right

    _, sub = iotas()
    rs, gain, y, z = [], [], [], []
    for u in range(tb):
        t = base + u
        r, a0 = decay(d_ref[pl.ds(t, 1), :])
        r = jnp.broadcast_to(r, (8, 128))
        a0 = jnp.broadcast_to(a0, (8, 128))
        rS = power(r, S)
        rS2 = rS * rS
        rS4 = rS2 * rS2
        c = jnp.where(sub == 0, sums[0, pl.ds(t, 1), :], pltpu.roll(seg_ref[0, u], 1, 0))
        b = jnp.where(sub == 7, sums[1, pl.ds(t, 1), :], pltpu.roll(seg_ref[1, u], 7, 0))
        for s, q in ((1, rS), (2, rS2), (4, rS4)):
            c = c + q * jnp.where(sub >= s, pltpu.roll(c, s, 0), 0.0)
            b = b + q * jnp.where(sub < 8 - s, pltpu.roll(b, 8 - s, 0), 0.0)
        rs.append(r)
        gain.append(a0)
        y.append(c)
        z.append(b)
    for rows in batches(0, S, 8):
        done = []
        for i in rows:
            for u in range(tb):
                y[u] = y[u] * rs[u] + f_ref[u, pl.ds(i, 8, stride=S), :]
                done.append((u, i, y[u]))
        for u, i, value in done:
            ys[u, i] = value
    for rows in batches(0, S, 8)[::-1]:
        done = []
        for i in rows[::-1]:
            for u in range(tb):
                zr = z[u] * rs[u]
                done.append((u, i, gain[u] * (ys[u, i] + zr)))
                z[u] = zr + f_ref[u, pl.ds(i, 8, stride=S), :]
        for u, i, value in done:
            out_ref[u, pl.ds(i, 8, stride=S), :] = value

    lane_n = lax.broadcasted_iota(jnp.int32, (n, 128), 1)
    group = lane_n >> 2
    acc = pkh[...]
    for u in range(tb):
        t = base + u
        acc = jnp.where(group == t, pltpu.roll(out_ref[u], (4 * t + 2) & 127, 1), acc)
    pkh[...] = acc
    lows = [jnp.where(sub == 7, out_ref[u, 0:1, :], lo7_ref[u]) for u in range(tb)]
    highs = [jnp.where(sub == 7, out_ref[u, n - 1 : n, :], hi7_ref[u]) for u in range(tb)]
    for u in range(tb):
        lo_ref[u] = lows[u]
        hi_ref[u] = highs[u]

    @pl.when(step == pl.num_programs(0) - 1)
    def _():
        slot = lane_n & 3
        v0, v1, f0, f1, fr, he = pk_ref[0], pk_ref[1], pk_ref[2], pk_ref[3], pk_ref[4], pkh[...]

        def sel(a, b, c, d):
            return jnp.where(slot < 2, jnp.where(slot == 0, a, b), jnp.where(slot == 2, c, d))

        right_ref[0] = jnp.where(slot < 2, v0, pltpu.roll(v1, 2, 1))
        left_ref[0] = jnp.where(slot >= 2, v0, pltpu.roll(v1, 126, 1))
        right_ref[1] = sel(pltpu.roll(f0, 127, 1), f1, pltpu.roll(fr, 1, 1), pltpu.roll(he, 2, 1))
        left_ref[1] = sel(pltpu.roll(f0, 126, 1), pltpu.roll(f1, 127, 1), fr, pltpu.roll(he, 1, 1))


def heat(d, pqs, seg, prior, pk, lo7, hi7):
    T, n, _ = prior.shape
    J = len(pqs)
    tb = 4
    row = jax.ShapeDtypeStruct((T + 1, 8, 128), F32)
    return pl.pallas_call(
        functools.partial(heat_kernel, J, tb, n),
        grid=(T // tb,),
        in_specs=[
            pl.BlockSpec((T, 128), lambda t: (0, 0)),
            *[pl.BlockSpec((2, T, 128), lambda t: (0, 0, 0)) for _ in range(J)],
            pl.BlockSpec((2, tb, 8, 128), lambda t: (0, t, 0, 0)),
            pl.BlockSpec((tb, n, 128), lambda t: (t, 0, 0)),
            pl.BlockSpec((5, n, 128), lambda t: (0, 0, 0)),
            pl.BlockSpec((tb, 8, 128), lambda t: (t, 0, 0)),
            pl.BlockSpec((tb, 8, 128), lambda t: (t, 0, 0)),
        ],
        out_specs=[
            pl.BlockSpec((tb, n, 128), lambda t: (t, 0, 0)),
            pl.BlockSpec((2, n, 128), lambda t: (0, 0, 0)),
            pl.BlockSpec((2, n, 128), lambda t: (0, 0, 0)),
            pl.BlockSpec((tb, 8, 128), lambda t: (t, 0, 0)),
            pl.BlockSpec((tb, 8, 128), lambda t: (t, 0, 0)),
        ],
        out_shape=[
            jax.ShapeDtypeStruct((T, n, 128), F32),
            jax.ShapeDtypeStruct((2, n, 128), F32),
            jax.ShapeDtypeStruct((2, n, 128), F32),
            row,
            row,
        ],
        scratch_shapes=[
            pltpu.VMEM((J, 2, T, 128), F32),
            pltpu.VMEM((2, T, 128), F32),
            pltpu.VMEM((n, 128), F32),
            pltpu.VMEM((tb, n // 8, 8, 128), F32),
        ],
        compiler_params=pltpu.CompilerParams(vmem_limit_bytes=60 * MIB),
        cost_estimate=pl.CostEstimate(flops=10 * T * n * 128, bytes_accessed=8 * T * n * 128, transcendentals=0),
        name="heat",
    )(d, *pqs, seg, prior, pk, lo7, hi7)


def corner_kernel(n, fl_ref, fr_ref, lo_in, hi_in, r_ref, lo_ref, hi_ref):
    slot = lax.broadcasted_iota(jnp.int32, (n, 128), 1) & 3
    al, ar, bl, br = fl_ref[0], fr_ref[0], fl_ref[1], fr_ref[1]
    low = slot < 2
    r_ref[0] = jnp.where(low, al, ar)
    r_ref[1] = jnp.where(low, pltpu.roll(al, 126, 1), pltpu.roll(ar, 2, 1))
    for k in range(4):
        a = bl if k == 1 else pltpu.roll(bl, (1 - k) & 127, 1)
        b = br if k == 2 else pltpu.roll(br, (2 - k) & 127, 1)
        r_ref[2 + k] = jnp.where(low, a, b)
    for ref, a, e in ((lo_ref, 0, 0), (hi_ref, n - 2, n - 1)):
        ref[0, 0:2, :] = r_ref[0, a : a + 2, :]
        ref[0, 2:4, :] = r_ref[1, a : a + 2, :]
        for k in range(4):
            ref[0, 4 + k : 5 + k, :] = r_ref[2 + k, e : e + 1, :]


def corners(from_left, from_right, lo, hi):
    _, n, _ = from_left.shape
    T = lo.shape[0] - 1
    row = jax.ShapeDtypeStruct(lo.shape, F32)
    return pl.pallas_call(
        functools.partial(corner_kernel, n),
        grid=(1,),
        in_specs=[
            pl.BlockSpec((2, n, 128), lambda g: (0, 0, 0)),
            pl.BlockSpec((2, n, 128), lambda g: (0, 0, 0)),
            pl.BlockSpec(memory_space=pl.ANY),
            pl.BlockSpec(memory_space=pl.ANY),
        ],
        out_specs=[
            pl.BlockSpec((6, n, 128), lambda g: (0, 0, 0)),
            pl.BlockSpec((1, 8, 128), lambda g: (T, 0, 0)),
            pl.BlockSpec((1, 8, 128), lambda g: (T, 0, 0)),
        ],
        out_shape=[jax.ShapeDtypeStruct((6, n, 128), F32), row, row],
        input_output_aliases={2: 1, 3: 2},
        compiler_params=pltpu.CompilerParams(vmem_limit_bytes=8 * MIB),
        cost_estimate=pl.CostEstimate(flops=0, bytes_accessed=40 * n * 128, transcendentals=0),
        name="corners",
    )(from_left, from_right, lo, hi)


def coefficients(f0, f1, free, heated):
    v = jnp.exp(-0.5 * heated)
    w = RELAX_FACTOR * free
    a = w * reciprocal(DRAG_COEFF + 4.0 * v)
    return 1.0 - w, a * v, a * f0, a * f1


def under(row, last_vector):
    _, sub = iotas()
    return jnp.where(sub == 0, row, pltpu.roll(last_vector, 1, 0))


def over(row, first_vector):
    _, sub = iotas()
    return jnp.where(sub == 7, row, pltpu.roll(first_vector, 7, 0))


def put(todo):
    for ref, c, i, value in todo:
        ref[c, i] = value


def halo_rows(ref, S, low, high, get):
    todo = []
    for c in range(2):
        for q in range(2):
            todo.append((ref, c, q, under(low(2 * c + q), get(c, S - 2 + q))))
            todo.append((ref, c, S + 2 + q, over(high(2 * c + q), get(c, q))))
    return todo


def halo_coefficients(cos, S, low, high, get):
    below = coefficients(*[under(low(4 + m), get(m, S - 1)) for m in range(4)])
    above = coefficients(*[over(high(4 + m), get(m, 0)) for m in range(4)])
    return [(cos, m, 0, below[m]) for m in range(4)] + [(cos, m, S + 1, above[m]) for m in range(4)]


def strip_kernel(n, lo_ref, hi_ref, r_ref, own_ref, yh1, yh2, xs, ws, r1s, cos):
    S = n // 8
    T = lo_ref.shape[0] - 1
    lane, _ = iotas()
    slot = lane & 3
    outer = (slot == 0) | (slot == 3)
    sign = jnp.where(slot == 1, -0.25, 0.25)

    def low(k):
        return lo_ref[T, k : k + 1, :]

    def high(k):
        return hi_ref[T, k : k + 1, :]

    def get(m, i):
        return r_ref[2 + m, pl.ds(i, 8, stride=S), :]

    def collect(ref):
        parts = [
            jnp.where(lane >> 2 == t, pltpu.roll(ref[t], (4 * t + 2) & 127, 1), 0.0) for t in range(T)
        ]
        while len(parts) > 1:
            parts = [p + q for p, q in zip(parts[::2], parts[1::2])]
        return parts[0]

    own_lo, own_hi = collect(lo_ref), collect(hi_ref)
    both_lo = jnp.where(outer, lo_ref[T], own_lo)
    both_hi = jnp.where(outer, hi_ref[T], own_hi)

    def load(start, m):
        todo = []
        for i in [start + j for j in range(m)]:
            for c in range(2):
                r = r_ref[c, pl.ds(i, 8, stride=S), :]
                todo.append((xs, c, i + 2, r))
                todo.append((ws, c, i + 2, jnp.where(outer, r, own_ref[c, pl.ds(i, 8, stride=S), :])))
            co = coefficients(*[get(q, i) for q in range(4)])
            todo += [(cos, q, i + 1, co[q]) for q in range(4)]
        put(todo)

    over_rows(0, S, load)
    def row_low(k):
        return both_lo[k : k + 1, :]

    def row_high(k):
        return both_hi[k : k + 1, :]

    def get_r(c, i):
        return r_ref[c, pl.ds(i, 8, stride=S), :]

    def get_w(c, i):
        return jnp.where(outer, get_r(c, i), own_ref[c, pl.ds(i, 8, stride=S), :])

    put(
        halo_rows(xs, S, low, high, get_r)
        + halo_rows(ws, S, row_low, row_high, get_w)
        + halo_coefficients(cos, S, low, high, get)
    )

    def relax(start, m):
        r = [[xs[c, start + 1 + j] for c in range(2)] for j in range(m + 2)]
        w = [[ws[c, start + 1 + j] for c in range(2)] for j in range(m + 2)]
        todo = []
        for j in range(m):
            i = start + j
            for c in range(2):
                q = 0.25 * (w[j + 2][1 - c] - w[j][1 - c])
                around = (
                    r[j][c] + r[j + 2][c] + pltpu.roll(w[j + 1][c] + q, 127, 1) + pltpu.roll(w[j + 1][c] - q, 1, 1)
                )
                todo.append((yh1, c, i + 1, r[j + 1][c] + sign * (r[j + 2][1 - c] - r[j][1 - c])))
                new = cos[0, i + 1] * r[j + 1][c] + cos[2 + c, i + 1] + cos[1, i + 1] * around
                todo.append((r1s, c, i + 1, new))
        put(todo)

    over_rows(-1, S + 1, relax, 17)

    def edges(start, m):
        r = [[r1s[c, start + j] for c in range(2)] for j in range(m + 2)]
        put(
            [
                (yh2, c, start + j, r[j + 1][c] + sign * (r[j + 2][1 - c] - r[j][1 - c]))
                for j in range(m)
                for c in range(2)
            ]
        )

    over_rows(0, S, edges, 16)


def strips(lo, hi, r, pk):
    n = r.shape[1]
    S = n // 8
    whole = lambda shape: pl.BlockSpec(shape, lambda g: (0,) * len(shape))
    return pl.pallas_call(
        functools.partial(strip_kernel, n),
        grid=(1,),
        in_specs=[whole(lo.shape), whole(hi.shape), whole(r.shape), whole((2, n, 128))],
        out_specs=[whole((2, S + 2, 8, 128)), whole((2, S, 8, 128))],
        out_shape=[
            jax.ShapeDtypeStruct((2, S + 2, 8, 128), F32),
            jax.ShapeDtypeStruct((2, S, 8, 128), F32),
        ],
        scratch_shapes=[
            pltpu.VMEM((2, S + 4, 8, 128), F32),
            pltpu.VMEM((2, S + 4, 8, 128), F32),
            pltpu.VMEM((2, S + 2, 8, 128), F32),
            pltpu.VMEM((4, S + 2, 8, 128), F32),
        ],
        compiler_params=pltpu.CompilerParams(vmem_limit_bytes=8 * MIB),
        cost_estimate=pl.CostEstimate(flops=60 * n * 128, bytes_accessed=60 * n * 128, transcendentals=n * 128),
        name="strips",
    )(lo, hi, r, pk)


def sweep_kernel(tb, n, v_ref, f_ref, p_ref, h_ref, lo_ref, hi_ref, yh1, yh2, out_ref, xs, v1s, cos):
    S = n // 8
    step = pl.program_id(0)
    lane, _ = iotas()
    first, last = lane == 0, lane == 127

    def layer(u, _):
        t = step * tb + u
        shift = (126 - 4 * t) & 127

        def low(k):
            return lo_ref[t, k : k + 1, :]

        def high(k):
            return hi_ref[t, k : k + 1, :]

        def get(m, i):
            rows = pl.ds(i, 8, stride=S)
            if m < 2:
                return f_ref[m, u, rows, :]
            return 1.0 - p_ref[u, rows, :].astype(F32) if m == 2 else h_ref[u, rows, :]

        def load(start, m):
            todo = []
            for i in [start + j for j in range(m)]:
                todo += [(xs, c, i + 2, v_ref[c, u, pl.ds(i, 8, stride=S), :]) for c in range(2)]
                co = coefficients(*[get(q, i) for q in range(4)])
                todo += [(cos, q, i + 1, co[q]) for q in range(4)]
            put(todo)

        def sweep(src, off, yh, start, m):
            x = [[src[c, start + off + j] for c in range(2)] for j in range(m + 2)]
            done = []
            for j in range(m):
                i = start + j
                prev, here, after = x[j], x[j + 1], x[j + 2]
                q = [0.25 * (after[c] - prev[c]) for c in range(2)]
                k, g = cos[0, i + 1], cos[1, i + 1]
                for c in range(2):
                    edge = pltpu.roll(yh[c, i + off], shift, 1)
                    up = jnp.where(first, edge, here[c] + q[1 - c])
                    down = jnp.where(last, edge, here[c] - q[1 - c])
                    around = prev[c] + after[c] + (pltpu.roll(up, 127, 1) + pltpu.roll(down, 1, 1))
                    done.append((c, i, k * here[c] + cos[2 + c, i + 1] + g * around))
            return done

        def first_sweep(start, m):
            put([(v1s, c, i + 1, value) for c, i, value in sweep(xs, 1, yh1, start, m)])

        def second_sweep(start, m):
            for c, i, value in sweep(v1s, 0, yh2, start, m):
                out_ref[c, u, pl.ds(i, 8, stride=S), :] = value

        put(
            halo_rows(xs, S, low, high, lambda c, i: v_ref[c, u, pl.ds(i, 8, stride=S), :])
            + halo_coefficients(cos, S, low, high, get)
        )
        over_rows(0, S, load, 16)
        over_rows(-1, S + 1, first_sweep, 17)
        over_rows(0, S, second_sweep, 16)
        return 0

    lax.fori_loop(0, tb, layer, 0)


def sweeps(v, f, pinned, heated, lo, hi, yh1, yh2):
    _, T, n, _ = v.shape
    S = n // 8
    tb = 2
    whole = lambda shape: pl.BlockSpec(shape, lambda t: (0,) * len(shape))
    return pl.pallas_call(
        functools.partial(sweep_kernel, tb, n),
        grid=(T // tb,),
        in_specs=[
            pl.BlockSpec((2, tb, n, 128), lambda t: (0, t, 0, 0)),
            pl.BlockSpec((2, tb, n, 128), lambda t: (0, t, 0, 0)),
            pl.BlockSpec((tb, n, 128), lambda t: (t, 0, 0)),
            pl.BlockSpec((tb, n, 128), lambda t: (t, 0, 0)),
            whole((T + 1, 8, 128)),
            whole((T + 1, 8, 128)),
            whole((2, S + 2, 8, 128)),
            whole((2, S, 8, 128)),
        ],
        out_specs=pl.BlockSpec((2, tb, n, 128), lambda t: (0, t, 0, 0)),
        out_shape=jax.ShapeDtypeStruct((2, T, n, 128), F32),
        scratch_shapes=[
            pltpu.VMEM((2, S + 4, 8, 128), F32),
            pltpu.VMEM((2, S + 2, 8, 128), F32),
            pltpu.VMEM((4, S + 2, 8, 128), F32),
        ],
        compiler_params=pltpu.CompilerParams(vmem_limit_bytes=60 * MIB),
        cost_estimate=pl.CostEstimate(
            flops=60 * T * n * 128, bytes_accessed=32 * T * n * 128, transcendentals=T * n * 128
        ),
        name="sweeps",
    )(v, f, pinned, heated, lo, hi, yh1, yh2)


def shifted(up_going, down_going, axis):
    count = lax.axis_size(axis)
    up = [(i, i + 1) for i in range(count - 1)]
    down = [(j, i) for i, j in up]
    return lax.ppermute(up_going, axis, up), lax.ppermute(down_going, axis, down)


def local(prior, d, v, f, pinned):
    seg, pq = moments(d, prior)
    J = lax.axis_size("wid")
    pqs = [pq] + [lax.ppermute(pq, "wid", [(i, (i + s) % J) for i in range(J)]) for s in range(1, J)]
    pk, lo7, hi7 = pack(v, f, pinned)
    heated, right, left, lo, hi = heat(d, pqs, seg, prior, pk, lo7, hi7)
    from_left, from_right = shifted(right, left, "len")
    r, lo, hi = corners(from_left, from_right, lo, hi)
    from_below, from_above = shifted(hi, lo, "wid")
    yh1, yh2 = strips(from_below, from_above, r, pk)
    flow = sweeps(v, f, pinned, heated, from_below, from_above, yh1, yh2)
    return heated, flow


def solution(mesh):
    in_specs = (
        P(None, "wid", "len"),
        P(None, "len"),
        P(None, None, "wid", "len"),
        P(None, None, "wid", "len"),
        P(None, "wid", "len"),
    )
    out_specs = (P(None, "wid", "len"), P(None, None, "wid", "len"))
    return jax.shard_map(local, mesh=mesh, in_specs=in_specs, out_specs=out_specs, check_vma=False)
```

```python
import functools

import jax
import jax.numpy as jnp
from jax import lax
from jax.experimental import pallas as pl
from jax.experimental.pallas import tpu as pltpu
from jax.sharding import PartitionSpec as P

DRAG_COEFF = 0.5
RELAX_FACTOR = 0.8
HALF_LOG2E = -0.7213475204444817
F32 = jnp.float32
MIB = 1 << 20


def decay(d):
    x = 1.0 / d
    one_less = jnp.sqrt(x + 0.25 * x * x) - 0.5 * x
    r = 1.0 - one_less
    return r, (1.0 - r) / (1.0 + r)


def power(r, n):
    out = None
    while n:
        if n & 1:
            out = r if out is None else out * r
        n >>= 1
        if n:
            r = r * r
    return out


def sublane_powers(r, shape):
    s = lax.broadcasted_iota(jnp.int32, shape, 0)
    r2 = r * r
    r4 = r2 * r2
    one = jnp.ones(shape, F32)
    return (
        jnp.where((s & 1) != 0, r, one)
        * jnp.where((s & 2) != 0, r2, one)
        * jnp.where((s & 4) != 0, r4, one)
    )


def reciprocal(x):
    y = pl.reciprocal(x, approx=True)
    return y * (2.0 - x * y)


def batches(lo, hi, most=11):
    parts = -(-(hi - lo) // most)
    cuts = [lo + (hi - lo) * k // parts for k in range(parts + 1)]
    return [range(a, b) for a, b in zip(cuts, cuts[1:])]


def over_rows(first, stop, body, most=8):
    count = stop - first
    m = max(k for k in range(1, most + 1) if count % k == 0)

    def step(k, _):
        body(first + k * m, m)
        return 0

    lax.fori_loop(0, count // m, step, 0)


def iotas():
    lane = lax.broadcasted_iota(jnp.int32, (8, 128), 1)
    sub = lax.broadcasted_iota(jnp.int32, (8, 128), 0)
    return lane, sub


def moments_kernel(tb, n, d_ref, f_ref, seg_ref, pq_ref):
    S = n // 8
    base = pl.program_id(0) * tb
    G = 4
    for g in range(tb // G):
        rs = []
        for u in range(G):
            r, _ = decay(d_ref[pl.ds(base + g * G + u, 1), :])
            rs.append(jnp.broadcast_to(r, (8, 128)))
        fwd = [f_ref[g * G + u, pl.ds(0, 8, stride=S), :] for u in range(G)]
        bwd, weight = list(fwd), list(rs)
        for i in range(1, S):
            for u in range(G):
                x = f_ref[g * G + u, pl.ds(i, 8, stride=S), :]
                fwd[u] = fwd[u] * rs[u] + x
                bwd[u] = bwd[u] + weight[u] * x
                weight[u] = weight[u] * rs[u]
        for u in range(G):
            k = g * G + u
            seg_ref[0, k] = fwd[u]
            seg_ref[1, k] = bwd[u]
            rS = power(rs[u], S)
            up = sublane_powers(rS, (8, 128))
            s = lax.broadcasted_iota(jnp.int32, (8, 128), 0)
            rS2 = rS * rS
            one = jnp.ones((8, 128), F32)
            down = (
                jnp.where((s & 1) == 0, rS, one)
                * jnp.where((s & 2) == 0, rS2, one)
                * jnp.where((s & 4) == 0, rS2 * rS2, one)
            )
            pq_ref[0, k : k + 1, :] = jnp.sum(fwd[u] * down, axis=0, keepdims=True)
            pq_ref[1, k : k + 1, :] = jnp.sum(bwd[u] * up, axis=0, keepdims=True)


def moments(d, prior):
    T, n, _ = prior.shape
    tb = 8
    return pl.pallas_call(
        functools.partial(moments_kernel, tb, n),
        grid=(T // tb,),
        in_specs=[
            pl.BlockSpec((T, 128), lambda t: (0, 0)),
            pl.BlockSpec((tb, n, 128), lambda t: (t, 0, 0)),
        ],
        out_specs=[
            pl.BlockSpec((2, tb, 8, 128), lambda t: (0, t, 0, 0)),
            pl.BlockSpec((2, tb, 128), lambda t: (0, t, 0)),
        ],
        out_shape=[
            jax.ShapeDtypeStruct((2, T, 8, 128), F32),
            jax.ShapeDtypeStruct((2, T, 128), F32),
        ],
        compiler_params=pltpu.CompilerParams(vmem_limit_bytes=57 * MIB),
        cost_estimate=pl.CostEstimate(flops=4 * T * n * 128, bytes_accessed=4 * T * n * 128, transcendentals=0),
        name="moments",
    )(d, prior)


def pack_kernel(tb, n, v_ref, f_ref, p_ref, pk_ref, lo_ref, hi_ref):
    base = pl.program_id(0) * tb
    lane = lax.broadcasted_iota(jnp.int32, (n, 128), 1)
    group = lane >> 2
    for k in range(5):
        acc = pk_ref[k]
        for u in range(tb):
            if k < 2:
                x = v_ref[k, u]
            elif k < 4:
                x = f_ref[k - 2, u]
            else:
                x = 1.0 - p_ref[u].astype(F32)
            t = base + u
            acc = jnp.where(group == t, pltpu.roll(x, (4 * t + 2) & 127, 1), acc)
        pk_ref[k] = acc
    _, sub = iotas()

    def stack(v0, v1, f0, f1, fr):
        out = jnp.where(sub < 2, v0, v1)
        out = jnp.where(sub >= 4, f0, out)
        out = jnp.where(sub >= 5, f1, out)
        return jnp.where(sub >= 6, fr, out)

    tiles = []
    for u in range(tb):
        for top, at, shifts in ((True, 0, (0, 2, 4, 5, 6)), (False, n - 8, (2, 4, 5, 6, 7))):
            rows = pl.ds(at, 8)
            raw = [v_ref[0, u, rows, :], v_ref[1, u, rows, :], f_ref[0, u, rows, :], f_ref[1, u, rows, :]]
            raw.append(1.0 - p_ref[u, rows, :].astype(F32))
            tiles.append((u, top, stack(*[pltpu.roll(x, q, 0) if q else x for x, q in zip(raw, shifts)])))
    for u, top, tile in tiles:
        (lo_ref if top else hi_ref)[u] = tile


def pack(v, f, pinned):
    _, T, n, _ = v.shape
    tb = 4
    row = jax.ShapeDtypeStruct((T, 8, 128), F32)
    return pl.pallas_call(
        functools.partial(pack_kernel, tb, n),
        grid=(T // tb,),
        in_specs=[
            pl.BlockSpec((2, tb, n, 128), lambda t: (0, t, 0, 0)),
            pl.BlockSpec((2, tb, n, 128), lambda t: (0, t, 0, 0)),
            pl.BlockSpec((tb, n, 128), lambda t: (t, 0, 0)),
        ],
        out_specs=[
            pl.BlockSpec((5, n, 128), lambda t: (0, 0, 0)),
            pl.BlockSpec((tb, 8, 128), lambda t: (t, 0, 0)),
            pl.BlockSpec((tb, 8, 128), lambda t: (t, 0, 0)),
        ],
        out_shape=[jax.ShapeDtypeStruct((5, n, 128), F32), row, row],
        compiler_params=pltpu.CompilerParams(vmem_limit_bytes=57 * MIB),
        cost_estimate=pl.CostEstimate(flops=5 * T * n * 128, bytes_accessed=20 * T * n * 128, transcendentals=0),
        name="pack_edges",
    )(v, f, pinned)


def heat_kernel(J, tb, n, *refs):
    d_ref, *pq_refs = refs[: J + 1]
    (
        seg_ref, f_ref, pk_ref, lo7_ref, hi7_ref,
        out_ref, right_ref, left_ref, lo_ref, hi_ref, alls, sums, pkh, ys,
    ) = refs[J + 1 :]
    S = n // 8
    step = pl.program_id(0)
    base = step * tb

    @pl.when(step == 0)
    def _():
        j = lax.axis_index("wid")
        for s in range(J):
            alls[lax.rem(j - s + J, J)] = pq_refs[s][...]
        r, _ = decay(d_ref[...])
        rn = power(r, n)
        rN = power(rn, J)
        sp = alls[0, 0]
        for i in range(1, J):
            sp = sp * rn + alls[i, 0]
        sq = alls[J - 1, 1]
        for i in range(J - 2, -1, -1):
            sq = sq * rn + alls[i, 1]
        inv = 1.0 / (1.0 - rN * rN)
        left = (sq + rN * sp) * inv
        right = (sp + rN * sq) * inv
        for i in range(J - 1):
            left = jnp.where(i < j, rn * left + alls[i, 0], left)
        for i in range(J - 1, 0, -1):
            right = jnp.where(i > j, rn * right + alls[i, 1], right)
        sums[0] = left
        sums[1] = right

    _, sub = iotas()
    rs, gain, y, z = [], [], [], []
    for u in range(tb):
        t = base + u
        r, a0 = decay(d_ref[pl.ds(t, 1), :])
        r = jnp.broadcast_to(r, (8, 128))
        a0 = jnp.broadcast_to(a0, (8, 128))
        rS = power(r, S)
        rS2 = rS * rS
        rS4 = rS2 * rS2
        c = jnp.where(sub == 0, sums[0, pl.ds(t, 1), :], pltpu.roll(seg_ref[0, u], 1, 0))
        b = jnp.where(sub == 7, sums[1, pl.ds(t, 1), :], pltpu.roll(seg_ref[1, u], 7, 0))
        for s, q in ((1, rS), (2, rS2), (4, rS4)):
            c = c + q * jnp.where(sub >= s, pltpu.roll(c, s, 0), 0.0)
            b = b + q * jnp.where(sub < 8 - s, pltpu.roll(b, 8 - s, 0), 0.0)
        rs.append(r)
        gain.append(a0)
        y.append(c)
        z.append(b)
    for rows in batches(0, S, 8):
        done = []
        for i in rows:
            for u in range(tb):
                y[u] = y[u] * rs[u] + f_ref[u, pl.ds(i, 8, stride=S), :]
                done.append((u, i, y[u]))
        for u, i, value in done:
            ys[u, i] = value
    for rows in batches(0, S, 8)[::-1]:
        done = []
        for i in rows[::-1]:
            for u in range(tb):
                zr = z[u] * rs[u]
                done.append((u, i, gain[u] * (ys[u, i] + zr)))
                z[u] = zr + f_ref[u, pl.ds(i, 8, stride=S), :]
        for u, i, value in done:
            out_ref[u, pl.ds(i, 8, stride=S), :] = value

    lane_n = lax.broadcasted_iota(jnp.int32, (n, 128), 1)
    group = lane_n >> 2
    acc = pkh[...]
    for u in range(tb):
        t = base + u
        acc = jnp.where(group == t, pltpu.roll(out_ref[u], (4 * t + 2) & 127, 1), acc)
    pkh[...] = acc
    lows = [jnp.where(sub == 7, out_ref[u, 0:1, :], lo7_ref[u]) for u in range(tb)]
    highs = [jnp.where(sub == 7, out_ref[u, n - 1 : n, :], hi7_ref[u]) for u in range(tb)]
    for u in range(tb):
        lo_ref[u] = lows[u]
        hi_ref[u] = highs[u]

    @pl.when(step == pl.num_programs(0) - 1)
    def _():
        slot = lane_n & 3
        v0, v1, f0, f1, fr, he = pk_ref[0], pk_ref[1], pk_ref[2], pk_ref[3], pk_ref[4], pkh[...]

        def sel(a, b, c, d):
            return jnp.where(slot < 2, jnp.where(slot == 0, a, b), jnp.where(slot == 2, c, d))

        right_ref[0] = jnp.where(slot < 2, v0, pltpu.roll(v1, 2, 1))
        left_ref[0] = jnp.where(slot >= 2, v0, pltpu.roll(v1, 126, 1))
        right_ref[1] = sel(pltpu.roll(f0, 127, 1), f1, pltpu.roll(fr, 1, 1), pltpu.roll(he, 2, 1))
        left_ref[1] = sel(pltpu.roll(f0, 126, 1), pltpu.roll(f1, 127, 1), fr, pltpu.roll(he, 1, 1))


def heat(d, pqs, seg, prior, pk, lo7, hi7):
    T, n, _ = prior.shape
    J = len(pqs)
    tb = 4
    row = jax.ShapeDtypeStruct((T + 1, 8, 128), F32)
    return pl.pallas_call(
        functools.partial(heat_kernel, J, tb, n),
        grid=(T // tb,),
        in_specs=[
            pl.BlockSpec((T, 128), lambda t: (0, 0)),
            *[pl.BlockSpec((2, T, 128), lambda t: (0, 0, 0)) for _ in range(J)],
            pl.BlockSpec((2, tb, 8, 128), lambda t: (0, t, 0, 0)),
            pl.BlockSpec((tb, n, 128), lambda t: (t, 0, 0)),
            pl.BlockSpec((5, n, 128), lambda t: (0, 0, 0)),
            pl.BlockSpec((tb, 8, 128), lambda t: (t, 0, 0)),
            pl.BlockSpec((tb, 8, 128), lambda t: (t, 0, 0)),
        ],
        out_specs=[
            pl.BlockSpec((tb, n, 128), lambda t: (t, 0, 0)),
            pl.BlockSpec((2, n, 128), lambda t: (0, 0, 0)),
            pl.BlockSpec((2, n, 128), lambda t: (0, 0, 0)),
            pl.BlockSpec((tb, 8, 128), lambda t: (t, 0, 0)),
            pl.BlockSpec((tb, 8, 128), lambda t: (t, 0, 0)),
        ],
        out_shape=[
            jax.ShapeDtypeStruct((T, n, 128), F32),
            jax.ShapeDtypeStruct((2, n, 128), F32),
            jax.ShapeDtypeStruct((2, n, 128), F32),
            row,
            row,
        ],
        scratch_shapes=[
            pltpu.VMEM((J, 2, T, 128), F32),
            pltpu.VMEM((2, T, 128), F32),
            pltpu.VMEM((n, 128), F32),
            pltpu.VMEM((tb, n // 8, 8, 128), F32),
        ],
        compiler_params=pltpu.CompilerParams(vmem_limit_bytes=57 * MIB),
        cost_estimate=pl.CostEstimate(flops=10 * T * n * 128, bytes_accessed=8 * T * n * 128, transcendentals=0),
        name="heat",
    )(d, *pqs, seg, prior, pk, lo7, hi7)


def corner_kernel(n, fl_ref, fr_ref, lo_in, hi_in, r_ref, lo_ref, hi_ref):
    slot = lax.broadcasted_iota(jnp.int32, (n, 128), 1) & 3
    al, ar, bl, br = fl_ref[0], fr_ref[0], fl_ref[1], fr_ref[1]
    low = slot < 2
    r_ref[0] = jnp.where(low, al, ar)
    r_ref[1] = jnp.where(low, pltpu.roll(al, 126, 1), pltpu.roll(ar, 2, 1))
    for k in range(4):
        a = bl if k == 1 else pltpu.roll(bl, (1 - k) & 127, 1)
        b = br if k == 2 else pltpu.roll(br, (2 - k) & 127, 1)
        r_ref[2 + k] = jnp.where(low, a, b)
    for ref, a, e in ((lo_ref, 0, 0), (hi_ref, n - 2, n - 1)):
        ref[0, 0:2, :] = r_ref[0, a : a + 2, :]
        ref[0, 2:4, :] = r_ref[1, a : a + 2, :]
        for k in range(4):
            ref[0, 4 + k : 5 + k, :] = r_ref[2 + k, e : e + 1, :]


def corners(from_left, from_right, lo, hi):
    _, n, _ = from_left.shape
    T = lo.shape[0] - 1
    row = jax.ShapeDtypeStruct(lo.shape, F32)
    return pl.pallas_call(
        functools.partial(corner_kernel, n),
        grid=(1,),
        in_specs=[
            pl.BlockSpec((2, n, 128), lambda g: (0, 0, 0)),
            pl.BlockSpec((2, n, 128), lambda g: (0, 0, 0)),
            pl.BlockSpec(memory_space=pl.ANY),
            pl.BlockSpec(memory_space=pl.ANY),
        ],
        out_specs=[
            pl.BlockSpec((6, n, 128), lambda g: (0, 0, 0)),
            pl.BlockSpec((1, 8, 128), lambda g: (T, 0, 0)),
            pl.BlockSpec((1, 8, 128), lambda g: (T, 0, 0)),
        ],
        out_shape=[jax.ShapeDtypeStruct((6, n, 128), F32), row, row],
        input_output_aliases={2: 1, 3: 2},
        compiler_params=pltpu.CompilerParams(vmem_limit_bytes=8 * MIB),
        cost_estimate=pl.CostEstimate(flops=0, bytes_accessed=40 * n * 128, transcendentals=0),
        name="corners",
    )(from_left, from_right, lo, hi)


def coefficients(f0, f1, free, heated):
    v = jnp.exp2(HALF_LOG2E * heated)
    w = RELAX_FACTOR * free
    a = w * reciprocal(DRAG_COEFF + 4.0 * v)
    return 1.0 - w, a * v, a * f0, a * f1


def under(row, last_vector):
    _, sub = iotas()
    return jnp.where(sub == 0, row, pltpu.roll(last_vector, 1, 0))


def over(row, first_vector):
    _, sub = iotas()
    return jnp.where(sub == 7, row, pltpu.roll(first_vector, 7, 0))


def put(todo):
    for ref, c, i, value in todo:
        ref[c, i] = value


def halo_rows(ref, S, low, high, get):
    todo = []
    for c in range(2):
        for q in range(2):
            todo.append((ref, c, q, under(low(2 * c + q), get(c, S - 2 + q))))
            todo.append((ref, c, S + 2 + q, over(high(2 * c + q), get(c, q))))
    return todo


def halo_coefficients(cos, S, low, high, get):
    below = coefficients(*[under(low(4 + m), get(m, S - 1)) for m in range(4)])
    above = coefficients(*[over(high(4 + m), get(m, 0)) for m in range(4)])
    return [(cos, m, 0, below[m]) for m in range(4)] + [(cos, m, S + 1, above[m]) for m in range(4)]


def strip_kernel(n, lo_ref, hi_ref, r_ref, own_ref, yh1, yh2, xs, ws, r1s, cos):
    S = n // 8
    T = lo_ref.shape[0] - 1
    lane, _ = iotas()
    slot = lane & 3
    outer = (slot == 0) | (slot == 3)
    sign = jnp.where(slot == 1, -0.25, 0.25)

    def low(k):
        return lo_ref[T, k : k + 1, :]

    def high(k):
        return hi_ref[T, k : k + 1, :]

    def get(m, i):
        return r_ref[2 + m, pl.ds(i, 8, stride=S), :]

    def collect(ref):
        parts = [
            jnp.where(lane >> 2 == t, pltpu.roll(ref[t], (4 * t + 2) & 127, 1), 0.0) for t in range(T)
        ]
        while len(parts) > 1:
            parts = [p + q for p, q in zip(parts[::2], parts[1::2])]
        return parts[0]

    own_lo, own_hi = collect(lo_ref), collect(hi_ref)
    both_lo = jnp.where(outer, lo_ref[T], own_lo)
    both_hi = jnp.where(outer, hi_ref[T], own_hi)

    def load(start, m):
        todo = []
        for i in [start + j for j in range(m)]:
            for c in range(2):
                r = r_ref[c, pl.ds(i, 8, stride=S), :]
                todo.append((xs, c, i + 2, r))
                todo.append((ws, c, i + 2, jnp.where(outer, r, own_ref[c, pl.ds(i, 8, stride=S), :])))
            co = coefficients(*[get(q, i) for q in range(4)])
            todo += [(cos, q, i + 1, co[q]) for q in range(4)]
        put(todo)

    over_rows(0, S, load)
    def row_low(k):
        return both_lo[k : k + 1, :]

    def row_high(k):
        return both_hi[k : k + 1, :]

    def get_r(c, i):
        return r_ref[c, pl.ds(i, 8, stride=S), :]

    def get_w(c, i):
        return jnp.where(outer, get_r(c, i), own_ref[c, pl.ds(i, 8, stride=S), :])

    put(
        halo_rows(xs, S, low, high, get_r)
        + halo_rows(ws, S, row_low, row_high, get_w)
        + halo_coefficients(cos, S, low, high, get)
    )

    def relax(start, m):
        r = [[xs[c, start + 1 + j] for c in range(2)] for j in range(m + 2)]
        w = [[ws[c, start + 1 + j] for c in range(2)] for j in range(m + 2)]
        todo = []
        for j in range(m):
            i = start + j
            for c in range(2):
                q = 0.25 * (w[j + 2][1 - c] - w[j][1 - c])
                around = (
                    r[j][c] + r[j + 2][c] + pltpu.roll(w[j + 1][c] + q, 127, 1) + pltpu.roll(w[j + 1][c] - q, 1, 1)
                )
                todo.append((yh1, c, i + 1, r[j + 1][c] + sign * (r[j + 2][1 - c] - r[j][1 - c])))
                new = cos[0, i + 1] * r[j + 1][c] + cos[2 + c, i + 1] + cos[1, i + 1] * around
                todo.append((r1s, c, i + 1, new))
        put(todo)

    over_rows(-1, S + 1, relax, 17)

    def edges(start, m):
        r = [[r1s[c, start + j] for c in range(2)] for j in range(m + 2)]
        put(
            [
                (yh2, c, start + j, r[j + 1][c] + sign * (r[j + 2][1 - c] - r[j][1 - c]))
                for j in range(m)
                for c in range(2)
            ]
        )

    over_rows(0, S, edges, 16)


def strips(lo, hi, r, pk):
    n = r.shape[1]
    S = n // 8
    whole = lambda shape: pl.BlockSpec(shape, lambda g: (0,) * len(shape))
    return pl.pallas_call(
        functools.partial(strip_kernel, n),
        grid=(1,),
        in_specs=[whole(lo.shape), whole(hi.shape), whole(r.shape), whole((2, n, 128))],
        out_specs=[whole((2, S + 2, 8, 128)), whole((2, S, 8, 128))],
        out_shape=[
            jax.ShapeDtypeStruct((2, S + 2, 8, 128), F32),
            jax.ShapeDtypeStruct((2, S, 8, 128), F32),
        ],
        scratch_shapes=[
            pltpu.VMEM((2, S + 4, 8, 128), F32),
            pltpu.VMEM((2, S + 4, 8, 128), F32),
            pltpu.VMEM((2, S + 2, 8, 128), F32),
            pltpu.VMEM((4, S + 2, 8, 128), F32),
        ],
        compiler_params=pltpu.CompilerParams(vmem_limit_bytes=8 * MIB),
        cost_estimate=pl.CostEstimate(flops=60 * n * 128, bytes_accessed=60 * n * 128, transcendentals=n * 128),
        name="strips",
    )(lo, hi, r, pk)


def sweep_kernel(tb, n, v_ref, f_ref, p_ref, h_ref, lo_ref, hi_ref, yh1, yh2, out_ref, xs, v1s, cos):
    S = n // 8
    step = pl.program_id(0)
    lane, _ = iotas()
    first, last = lane == 0, lane == 127

    def layer(u, _):
        t = step * tb + u
        shift = (126 - 4 * t) & 127

        def low(k):
            return lo_ref[t, k : k + 1, :]

        def high(k):
            return hi_ref[t, k : k + 1, :]

        def get(m, i):
            rows = pl.ds(i, 8, stride=S)
            if m < 2:
                return f_ref[m, u, rows, :]
            return 1.0 - p_ref[u, rows, :].astype(F32) if m == 2 else h_ref[u, rows, :]

        def load(start, m):
            todo = []
            for i in [start + j for j in range(m)]:
                todo += [(xs, c, i + 2, v_ref[c, u, pl.ds(i, 8, stride=S), :]) for c in range(2)]
                co = coefficients(*[get(q, i) for q in range(4)])
                todo += [(cos, q, i + 1, co[q]) for q in range(4)]
            put(todo)

        def sweep(src, off, yh, start, m):
            x = [[src[c, start + off + j] for c in range(2)] for j in range(m + 2)]
            done = []
            for j in range(m):
                i = start + j
                prev, here, after = x[j], x[j + 1], x[j + 2]
                q = [0.25 * (after[c] - prev[c]) for c in range(2)]
                k, g = cos[0, i + 1], cos[1, i + 1]
                for c in range(2):
                    edge = pltpu.roll(yh[c, i + off], shift, 1)
                    up = jnp.where(first, edge, here[c] + q[1 - c])
                    down = jnp.where(last, edge, here[c] - q[1 - c])
                    around = prev[c] + after[c] + (pltpu.roll(up, 127, 1) + pltpu.roll(down, 1, 1))
                    done.append((c, i, k * here[c] + cos[2 + c, i + 1] + g * around))
            return done

        def first_sweep(start, m):
            put([(v1s, c, i + 1, value) for c, i, value in sweep(xs, 1, yh1, start, m)])

        def second_sweep(start, m):
            for c, i, value in sweep(v1s, 0, yh2, start, m):
                out_ref[c, u, pl.ds(i, 8, stride=S), :] = value

        put(
            halo_rows(xs, S, low, high, lambda c, i: v_ref[c, u, pl.ds(i, 8, stride=S), :])
            + halo_coefficients(cos, S, low, high, get)
        )
        over_rows(0, S, load, 16)
        over_rows(-1, S + 1, first_sweep, 17)
        over_rows(0, S, second_sweep, 16)
        return 0

    lax.fori_loop(0, tb, layer, 0)


def sweeps(v, f, pinned, heated, lo, hi, yh1, yh2):
    _, T, n, _ = v.shape
    S = n // 8
    tb = 2
    whole = lambda shape: pl.BlockSpec(shape, lambda t: (0,) * len(shape))
    return pl.pallas_call(
        functools.partial(sweep_kernel, tb, n),
        grid=(T // tb,),
        in_specs=[
            pl.BlockSpec((2, tb, n, 128), lambda t: (0, t, 0, 0)),
            pl.BlockSpec((2, tb, n, 128), lambda t: (0, t, 0, 0)),
            pl.BlockSpec((tb, n, 128), lambda t: (t, 0, 0)),
            pl.BlockSpec((tb, n, 128), lambda t: (t, 0, 0)),
            whole((T + 1, 8, 128)),
            whole((T + 1, 8, 128)),
            whole((2, S + 2, 8, 128)),
            whole((2, S, 8, 128)),
        ],
        out_specs=pl.BlockSpec((2, tb, n, 128), lambda t: (0, t, 0, 0)),
        out_shape=jax.ShapeDtypeStruct((2, T, n, 128), F32),
        scratch_shapes=[
            pltpu.VMEM((2, S + 4, 8, 128), F32),
            pltpu.VMEM((2, S + 2, 8, 128), F32),
            pltpu.VMEM((4, S + 2, 8, 128), F32),
        ],
        compiler_params=pltpu.CompilerParams(vmem_limit_bytes=57 * MIB),
        cost_estimate=pl.CostEstimate(
            flops=60 * T * n * 128, bytes_accessed=32 * T * n * 128, transcendentals=T * n * 128
        ),
        name="sweeps",
    )(v, f, pinned, heated, lo, hi, yh1, yh2)


def shifted(up_going, down_going, axis):
    count = lax.axis_size(axis)
    up = [(i, i + 1) for i in range(count - 1)]
    down = [(j, i) for i, j in up]
    return lax.ppermute(up_going, axis, up), lax.ppermute(down_going, axis, down)


def local(prior, d, v, f, pinned):
    seg, pq = moments(d, prior)
    J = lax.axis_size("wid")
    pqs = [pq] + [lax.ppermute(pq, "wid", [(i, (i + s) % J) for i in range(J)]) for s in range(1, J)]
    pk, lo7, hi7 = pack(v, f, pinned)
    heated, right, left, lo, hi = heat(d, pqs, seg, prior, pk, lo7, hi7)
    from_left, from_right = shifted(right, left, "len")
    r, lo, hi = corners(from_left, from_right, lo, hi)
    from_below, from_above = shifted(hi, lo, "wid")
    yh1, yh2 = strips(from_below, from_above, r, pk)
    flow = sweeps(v, f, pinned, heated, from_below, from_above, yh1, yh2)
    return heated, flow


def solution(mesh):
    in_specs = (
        P(None, "wid", "len"),
        P(None, "len"),
        P(None, None, "wid", "len"),
        P(None, None, "wid", "len"),
        P(None, "wid", "len"),
    )
    out_specs = (P(None, "wid", "len"), P(None, None, "wid", "len"))
    return jax.shard_map(local, mesh=mesh, in_specs=in_specs, out_specs=out_specs, check_vma=False)
```

```python
import functools

import jax
import jax.numpy as jnp
from jax import lax
from jax.experimental import pallas as pl
from jax.experimental.pallas import tpu as pltpu
from jax.sharding import PartitionSpec as P

DRAG_COEFF = 0.5
RELAX_FACTOR = 0.8
HALF_LOG2E = -0.7213475204444817
F32 = jnp.float32
MIB = 1 << 20


def decay(d):
    x = 1.0 / d
    one_less = jnp.sqrt(x + 0.25 * x * x) - 0.5 * x
    r = 1.0 - one_less
    return r, (1.0 - r) / (1.0 + r)


def power(r, n):
    out = None
    while n:
        if n & 1:
            out = r if out is None else out * r
        n >>= 1
        if n:
            r = r * r
    return out


def sublane_powers(r, shape):
    s = lax.broadcasted_iota(jnp.int32, shape, 0)
    r2 = r * r
    r4 = r2 * r2
    one = jnp.ones(shape, F32)
    return (
        jnp.where((s & 1) != 0, r, one)
        * jnp.where((s & 2) != 0, r2, one)
        * jnp.where((s & 4) != 0, r4, one)
    )


def reciprocal(x):
    y = pl.reciprocal(x, approx=True)
    return y * (2.0 - x * y)


def batches(lo, hi, most=11):
    parts = -(-(hi - lo) // most)
    cuts = [lo + (hi - lo) * k // parts for k in range(parts + 1)]
    return [range(a, b) for a, b in zip(cuts, cuts[1:])]


def over_rows(first, stop, body, most=8):
    count = stop - first
    m = max(k for k in range(1, most + 1) if count % k == 0)

    def step(k, _):
        body(first + k * m, m)
        return 0

    lax.fori_loop(0, count // m, step, 0)


def iotas():
    lane = lax.broadcasted_iota(jnp.int32, (8, 128), 1)
    sub = lax.broadcasted_iota(jnp.int32, (8, 128), 0)
    return lane, sub


def moments_kernel(tb, n, d_ref, f_ref, seg_ref, pq_ref):
    S = n // 8
    base = pl.program_id(0) * tb
    G = 4
    for g in range(tb // G):
        rs = []
        for u in range(G):
            r, _ = decay(d_ref[pl.ds(base + g * G + u, 1), :])
            rs.append(jnp.broadcast_to(r, (8, 128)))
        fwd = [f_ref[g * G + u, pl.ds(0, 8, stride=S), :] for u in range(G)]
        bwd, weight = list(fwd), list(rs)
        for i in range(1, S):
            for u in range(G):
                x = f_ref[g * G + u, pl.ds(i, 8, stride=S), :]
                fwd[u] = fwd[u] * rs[u] + x
                bwd[u] = bwd[u] + weight[u] * x
                weight[u] = weight[u] * rs[u]
        for u in range(G):
            k = g * G + u
            seg_ref[0, k] = fwd[u]
            seg_ref[1, k] = bwd[u]
            rS = power(rs[u], S)
            up = sublane_powers(rS, (8, 128))
            s = lax.broadcasted_iota(jnp.int32, (8, 128), 0)
            rS2 = rS * rS
            one = jnp.ones((8, 128), F32)
            down = (
                jnp.where((s & 1) == 0, rS, one)
                * jnp.where((s & 2) == 0, rS2, one)
                * jnp.where((s & 4) == 0, rS2 * rS2, one)
            )
            pq_ref[0, k : k + 1, :] = jnp.sum(fwd[u] * down, axis=0, keepdims=True)
            pq_ref[1, k : k + 1, :] = jnp.sum(bwd[u] * up, axis=0, keepdims=True)


def moments(d, prior):
    T, n, _ = prior.shape
    tb = 8
    return pl.pallas_call(
        functools.partial(moments_kernel, tb, n),
        grid=(T // tb,),
        in_specs=[
            pl.BlockSpec((T, 128), lambda t: (0, 0)),
            pl.BlockSpec((tb, n, 128), lambda t: (t, 0, 0)),
        ],
        out_specs=[
            pl.BlockSpec((2, tb, 8, 128), lambda t: (0, t, 0, 0)),
            pl.BlockSpec((2, tb, 128), lambda t: (0, t, 0)),
        ],
        out_shape=[
            jax.ShapeDtypeStruct((2, T, 8, 128), F32),
            jax.ShapeDtypeStruct((2, T, 128), F32),
        ],
        compiler_params=pltpu.CompilerParams(vmem_limit_bytes=57 * MIB),
        cost_estimate=pl.CostEstimate(flops=4 * T * n * 128, bytes_accessed=4 * T * n * 128, transcendentals=0),
        name="moments",
    )(d, prior)


def rows_kernel(T, v_lo, v_hi, f_lo, f_hi, p_lo, p_hi, lo_ref, hi_ref):
    _, sub = iotas()

    def stack(v0, v1, f0, f1, fr):
        out = jnp.where(sub < 2, v0, v1)
        out = jnp.where(sub >= 4, f0, out)
        out = jnp.where(sub >= 5, f1, out)
        out = jnp.where(sub >= 6, fr, out)
        return jnp.where(sub >= 7, 0.0, out)

    for v, f, p, out, shifts in (
        (v_lo, f_lo, p_lo, lo_ref, (0, 2, 4, 5, 6)),
        (v_hi, f_hi, p_hi, hi_ref, (2, 4, 5, 6, 7)),
    ):
        for t in range(T):
            raw = [v[0, t], v[1, t], f[0, t], f[1, t], 1.0 - p[t].astype(F32)]
            out[t] = stack(*[pltpu.roll(x, q, 0) if q else x for x, q in zip(raw, shifts)])


def whole(shape):
    return pl.BlockSpec(shape, lambda t: (0,) * len(shape))


def edge_rows(v, f, pinned):
    _, T, n, _ = v.shape
    row = jax.ShapeDtypeStruct((T, 8, 128), F32)
    end = n // 8 - 1
    four = [pl.BlockSpec((2, T, 8, 128), lambda t, k=k: (0, 0, k, 0)) for k in (0, end)]
    three = [pl.BlockSpec((T, 8, 128), lambda t, k=k: (0, k, 0)) for k in (0, end)]
    return pl.pallas_call(
        functools.partial(rows_kernel, T),
        grid=(1,),
        in_specs=[*four, *four, *three],
        out_specs=[whole((T, 8, 128))] * 2,
        out_shape=[row, row],
        compiler_params=pltpu.CompilerParams(vmem_limit_bytes=57 * MIB),
        cost_estimate=pl.CostEstimate(flops=0, bytes_accessed=48 * T * 8 * 128, transcendentals=0),
        name="edge_rows",
    )(v, v, f, f, pinned, pinned)


def gather_columns(ref, T):
    lane, _ = iotas()
    parts = [jnp.where(lane >> 2 == t, pltpu.roll(ref[t], (4 * t + 2) & 127, 1), 0.0) for t in range(T)]
    while len(parts) > 1:
        parts = [p + q for p, q in zip(parts[::2], parts[1::2])]
    return parts[0]


def pack_kernel(tb, n, T, v_ref, f_ref, p_ref, lo_ref, hi_ref, pk_ref, right_ref, left_ref, fp_ref):
    base = pl.program_id(0) * tb
    lane = lax.broadcasted_iota(jnp.int32, (n, 128), 1)
    group = lane >> 2
    for k in range(5):
        ref, q = (pk_ref, k) if k < 2 else (fp_ref, k - 2)
        acc = ref[q, 0:n, :]
        for u in range(tb):
            if k < 2:
                x = v_ref[k, u]
            elif k < 4:
                x = f_ref[k - 2, u]
            else:
                x = 1.0 - p_ref[u].astype(F32)
            t = base + u
            acc = jnp.where(group == t, pltpu.roll(x, (4 * t + 2) & 127, 1), acc)
        ref[q, 0:n, :] = acc

    @pl.when(pl.program_id(0) == pl.num_programs(0) - 1)
    def _():
        slot = lane & 3
        v0, v1 = pk_ref[0, 0:n, :], pk_ref[1, 0:n, :]
        f0, f1, fr = fp_ref[0], fp_ref[1], fp_ref[2]

        def sel(a, b, c):
            return jnp.where(slot < 1, a, jnp.where(slot == 1, b, c))

        right_ref[0, 0:n, :] = jnp.where(slot < 2, v0, pltpu.roll(v1, 2, 1))
        left_ref[0, 0:n, :] = jnp.where(slot >= 2, v0, pltpu.roll(v1, 126, 1))
        right_ref[1, 0:n, :] = sel(pltpu.roll(f0, 127, 1), f1, pltpu.roll(fr, 1, 1))
        left_ref[1, 0:n, :] = sel(pltpu.roll(f0, 126, 1), pltpu.roll(f1, 127, 1), fr)
        for k, ref in ((0, lo_ref), (1, hi_ref)):
            tile = gather_columns(ref, T)
            for out in (pk_ref, right_ref, left_ref):
                out[k, n : n + 8, :] = tile


def pack(v, f, pinned, lo, hi):
    _, T, n, _ = v.shape
    tb = 4
    out = jax.ShapeDtypeStruct((2, n + 8, 128), F32)
    return pl.pallas_call(
        functools.partial(pack_kernel, tb, n, T),
        grid=(T // tb,),
        in_specs=[
            pl.BlockSpec((2, tb, n, 128), lambda t: (0, t, 0, 0)),
            pl.BlockSpec((2, tb, n, 128), lambda t: (0, t, 0, 0)),
            pl.BlockSpec((tb, n, 128), lambda t: (t, 0, 0)),
            whole((T, 8, 128)),
            whole((T, 8, 128)),
        ],
        out_specs=[whole((2, n + 8, 128))] * 3,
        out_shape=[out, out, out],
        scratch_shapes=[pltpu.VMEM((3, n, 128), F32)],
        compiler_params=pltpu.CompilerParams(vmem_limit_bytes=57 * MIB),
        cost_estimate=pl.CostEstimate(flops=5 * T * n * 128, bytes_accessed=20 * T * n * 128, transcendentals=0),
        name="pack_edges",
    )(v, f, pinned, lo, hi)


def heat_kernel(J, tb, n, *refs):
    d_ref, *pq_refs = refs[: J + 1]
    (
        seg_ref, f_ref,
        out_ref, send_ref, row_ref, alls, sums, ys,
    ) = refs[J + 1 :]
    S = n // 8
    step = pl.program_id(0)
    base = step * tb

    @pl.when(step == 0)
    def _():
        j = lax.axis_index("wid")
        for s in range(J):
            alls[lax.rem(j - s + J, J)] = pq_refs[s][...]
        r, _ = decay(d_ref[...])
        rn = power(r, n)
        rN = power(rn, J)
        sp = alls[0, 0]
        for i in range(1, J):
            sp = sp * rn + alls[i, 0]
        sq = alls[J - 1, 1]
        for i in range(J - 2, -1, -1):
            sq = sq * rn + alls[i, 1]
        inv = 1.0 / (1.0 - rN * rN)
        left = (sq + rN * sp) * inv
        right = (sp + rN * sq) * inv
        for i in range(J - 1):
            left = jnp.where(i < j, rn * left + alls[i, 0], left)
        for i in range(J - 1, 0, -1):
            right = jnp.where(i > j, rn * right + alls[i, 1], right)
        sums[0] = left
        sums[1] = right

    _, sub = iotas()
    rs, gain, y, z = [], [], [], []
    for u in range(tb):
        t = base + u
        r, a0 = decay(d_ref[pl.ds(t, 1), :])
        r = jnp.broadcast_to(r, (8, 128))
        a0 = jnp.broadcast_to(a0, (8, 128))
        rS = power(r, S)
        rS2 = rS * rS
        rS4 = rS2 * rS2
        c = jnp.where(sub == 0, sums[0, pl.ds(t, 1), :], pltpu.roll(seg_ref[0, u], 1, 0))
        b = jnp.where(sub == 7, sums[1, pl.ds(t, 1), :], pltpu.roll(seg_ref[1, u], 7, 0))
        for s, q in ((1, rS), (2, rS2), (4, rS4)):
            c = c + q * jnp.where(sub >= s, pltpu.roll(c, s, 0), 0.0)
            b = b + q * jnp.where(sub < 8 - s, pltpu.roll(b, 8 - s, 0), 0.0)
        rs.append(r)
        gain.append(a0)
        y.append(c)
        z.append(b)
    for rows in batches(0, S, 8):
        done = []
        for i in rows:
            for u in range(tb):
                y[u] = y[u] * rs[u] + f_ref[u, pl.ds(i, 8, stride=S), :]
                done.append((u, i, y[u]))
        for u, i, value in done:
            ys[u, i] = value
    for rows in batches(0, S, 8)[::-1]:
        done = []
        for i in rows[::-1]:
            for u in range(tb):
                zr = z[u] * rs[u]
                done.append((u, i, gain[u] * (ys[u, i] + zr)))
                z[u] = zr + f_ref[u, pl.ds(i, 8, stride=S), :]
        for u, i, value in done:
            out_ref[u, pl.ds(i, 8, stride=S), :] = value

    lane_n = lax.broadcasted_iota(jnp.int32, (n, 128), 1)
    group = lane_n >> 2
    acc = send_ref[0:n, :]
    tile = send_ref[n : n + 8, :]
    lane, _ = iotas()
    rows = []
    for u in range(tb):
        t = base + u
        acc = jnp.where(group == t, pltpu.roll(out_ref[u], (4 * t + 2) & 127, 1), acc)
        below = gain[u][0:1] * (sums[0, pl.ds(t, 1), :] + rs[u][0:1] * z[u][0:1])
        above = gain[u][0:1] * (sums[1, pl.ds(t, 1), :] + rs[u][0:1] * y[u][7:8])
        both = jnp.where(sub == 0, below, above)
        rows.append((u, below, above))
        tile = jnp.where(lane >> 2 == t, pltpu.roll(both, (4 * t + 2) & 127, 1), tile)
    send_ref[0:n, :] = acc
    send_ref[n : n + 8, :] = tile
    for u, below, above in rows:
        row_ref[0, pl.ds(base + u, 1), :] = below
        row_ref[1, pl.ds(base + u, 1), :] = above


def heat(d, pqs, seg, prior):
    T, n, _ = prior.shape
    J = len(pqs)
    tb = 4
    return pl.pallas_call(
        functools.partial(heat_kernel, J, tb, n),
        grid=(T // tb,),
        in_specs=[
            whole((T, 128)),
            *[whole((2, T, 128)) for _ in range(J)],
            pl.BlockSpec((2, tb, 8, 128), lambda t: (0, t, 0, 0)),
            pl.BlockSpec((tb, n, 128), lambda t: (t, 0, 0)),
        ],
        out_specs=[
            pl.BlockSpec((tb, n, 128), lambda t: (t, 0, 0)),
            whole((n + 8, 128)),
            whole((2, T, 128)),
        ],
        out_shape=[
            jax.ShapeDtypeStruct((T, n, 128), F32),
            jax.ShapeDtypeStruct((n + 8, 128), F32),
            jax.ShapeDtypeStruct((2, T, 128), F32),
        ],
        scratch_shapes=[
            pltpu.VMEM((J, 2, T, 128), F32),
            pltpu.VMEM((2, T, 128), F32),
            pltpu.VMEM((tb, n // 8, 8, 128), F32),
        ],
        compiler_params=pltpu.CompilerParams(vmem_limit_bytes=57 * MIB),
        cost_estimate=pl.CostEstimate(flops=10 * T * n * 128, bytes_accessed=8 * T * n * 128, transcendentals=0),
        name="heat",
    )(d, *pqs, seg, prior)


def coefficients(f0, f1, free, heated):
    v = jnp.exp2(HALF_LOG2E * heated)
    w = RELAX_FACTOR * free
    a = w * reciprocal(DRAG_COEFF + 4.0 * v)
    return 1.0 - w, a * v, a * f0, a * f1


def under(row, last_vector):
    _, sub = iotas()
    return jnp.where(sub == 0, row, pltpu.roll(last_vector, 1, 0))


def over(row, first_vector):
    _, sub = iotas()
    return jnp.where(sub == 7, row, pltpu.roll(first_vector, 7, 0))


def put(todo):
    for ref, c, i, value in todo:
        ref[c, i] = value


def halo_rows(ref, S, low, high, get):
    todo = []
    for c in range(2):
        for q in range(2):
            todo.append((ref, c, q, under(low(2 * c + q), get(c, S - 2 + q))))
            todo.append((ref, c, S + 2 + q, over(high(2 * c + q), get(c, q))))
    return todo


def halo_coefficients(cos, S, low, high, get):
    below = coefficients(*[under(low(4 + m), get(m, S - 1)) for m in range(4)])
    above = coefficients(*[over(high(4 + m), get(m, 0)) for m in range(4)])
    return [(cos, m, 0, below[m]) for m in range(4)] + [(cos, m, S + 1, above[m]) for m in range(4)]


def strip_kernel(n, own_ref, fl_ref, fr_ref, hl_ref, hr_ref, yh1, yh2, r_ref, edge, xs, ws, r1s, cos):
    S = n // 8
    lane, sub = iotas()
    slot = lane & 3
    outer = (slot == 0) | (slot == 3)
    sign = jnp.where(slot == 1, -0.25, 0.25)

    low_n = lax.broadcasted_iota(jnp.int32, (n, 128), 1) & 3 < 2
    al, ar, bl, br = [ref[k, 0:n, :] for k in range(2) for ref in (fl_ref, fr_ref)]
    r_ref[0] = jnp.where(low_n, al, ar)
    r_ref[1] = jnp.where(low_n, pltpu.roll(al, 126, 1), pltpu.roll(ar, 2, 1))
    for k in range(3):
        a = bl if k == 1 else pltpu.roll(bl, (1 - k) & 127, 1)
        b = br if k == 2 else pltpu.roll(br, (2 - k) & 127, 1)
        r_ref[2 + k] = jnp.where(low_n, a, b)
    r_ref[5] = jnp.where(low_n, hl_ref[0:n, :], hr_ref[0:n, :])
    heat_rows = jnp.where(slot < 2, hl_ref[n : n + 8, :], hr_ref[n : n + 8, :])
    for k in range(2):
        tile = jnp.where(slot < 2, fl_ref[k, n : n + 8, :], fr_ref[k, n : n + 8, :])
        edge[k] = jnp.where(sub == 7, heat_rows[k : k + 1, :], tile)
        edge[2 + k] = jnp.where(outer, tile, own_ref[k, n : n + 8, :])

    def low(k):
        return edge[0, k : k + 1, :]

    def high(k):
        return edge[1, k : k + 1, :]

    def get(m, i):
        return r_ref[2 + m, pl.ds(i, 8, stride=S), :]

    def load(start, m):
        todo = []
        for i in [start + j for j in range(m)]:
            for c in range(2):
                r = r_ref[c, pl.ds(i, 8, stride=S), :]
                todo.append((xs, c, i + 2, r))
                todo.append((ws, c, i + 2, jnp.where(outer, r, own_ref[c, pl.ds(i, 8, stride=S), :])))
            co = coefficients(*[get(q, i) for q in range(4)])
            todo += [(cos, q, i + 1, co[q]) for q in range(4)]
        put(todo)

    over_rows(0, S, load)
    def row_low(k):
        return edge[2, k : k + 1, :]

    def row_high(k):
        return edge[3, k : k + 1, :]

    def get_r(c, i):
        return r_ref[c, pl.ds(i, 8, stride=S), :]

    def get_w(c, i):
        return jnp.where(outer, get_r(c, i), own_ref[c, pl.ds(i, 8, stride=S), :])

    put(
        halo_rows(xs, S, low, high, get_r)
        + halo_rows(ws, S, row_low, row_high, get_w)
        + halo_coefficients(cos, S, low, high, get)
    )

    def relax(start, m):
        r = [[xs[c, start + 1 + j] for c in range(2)] for j in range(m + 2)]
        w = [[ws[c, start + 1 + j] for c in range(2)] for j in range(m + 2)]
        todo = []
        for j in range(m):
            i = start + j
            for c in range(2):
                q = 0.25 * (w[j + 2][1 - c] - w[j][1 - c])
                around = (
                    r[j][c] + r[j + 2][c] + pltpu.roll(w[j + 1][c] + q, 127, 1) + pltpu.roll(w[j + 1][c] - q, 1, 1)
                )
                todo.append((yh1, c, i + 1, r[j + 1][c] + sign * (r[j + 2][1 - c] - r[j][1 - c])))
                new = cos[0, i + 1] * r[j + 1][c] + cos[2 + c, i + 1] + cos[1, i + 1] * around
                todo.append((r1s, c, i + 1, new))
        put(todo)

    over_rows(-1, S + 1, relax, 17)

    def edges(start, m):
        r = [[r1s[c, start + j] for c in range(2)] for j in range(m + 2)]
        put(
            [
                (yh2, c, start + j, r[j + 1][c] + sign * (r[j + 2][1 - c] - r[j][1 - c]))
                for j in range(m)
                for c in range(2)
            ]
        )

    over_rows(0, S, edges, 16)


def strips(own, fl, fr, hl, hr):
    n = own.shape[1] - 8
    S = n // 8
    return pl.pallas_call(
        functools.partial(strip_kernel, n),
        grid=(1,),
        in_specs=[whole(own.shape), whole(fl.shape), whole(fr.shape), whole(hl.shape), whole(hr.shape)],
        out_specs=[whole((2, S + 2, 8, 128)), whole((2, S, 8, 128))],
        out_shape=[
            jax.ShapeDtypeStruct((2, S + 2, 8, 128), F32),
            jax.ShapeDtypeStruct((2, S, 8, 128), F32),
        ],
        scratch_shapes=[
            pltpu.VMEM((6, n, 128), F32),
            pltpu.VMEM((4, 8, 128), F32),
            pltpu.VMEM((2, S + 4, 8, 128), F32),
            pltpu.VMEM((2, S + 4, 8, 128), F32),
            pltpu.VMEM((2, S + 2, 8, 128), F32),
            pltpu.VMEM((4, S + 2, 8, 128), F32),
        ],
        compiler_params=pltpu.CompilerParams(vmem_limit_bytes=12 * MIB),
        cost_estimate=pl.CostEstimate(flops=60 * n * 128, bytes_accessed=60 * n * 128, transcendentals=n * 128),
        name="strips",
    )(own, fl, fr, hl, hr)


def sweep_kernel(tb, n, v_ref, f_ref, p_ref, h_ref, lo_ref, hi_ref, row_ref, yh1, yh2, out_ref, xs, v1s, cos):
    S = n // 8
    step = pl.program_id(0)
    lane, _ = iotas()
    first, last = lane == 0, lane == 127

    def layer(u, _):
        t = step * tb + u
        shift = (126 - 4 * t) & 127

        def low(k):
            return row_ref[0, pl.ds(t, 1), :] if k == 7 else lo_ref[t, k : k + 1, :]

        def high(k):
            return row_ref[1, pl.ds(t, 1), :] if k == 7 else hi_ref[t, k : k + 1, :]

        def get(m, i):
            rows = pl.ds(i, 8, stride=S)
            if m < 2:
                return f_ref[m, u, rows, :]
            return 1.0 - p_ref[u, rows, :].astype(F32) if m == 2 else h_ref[u, rows, :]

        def load(start, m):
            todo = []
            for i in [start + j for j in range(m)]:
                todo += [(xs, c, i + 2, v_ref[c, u, pl.ds(i, 8, stride=S), :]) for c in range(2)]
                co = coefficients(*[get(q, i) for q in range(4)])
                todo += [(cos, q, i + 1, co[q]) for q in range(4)]
            put(todo)

        def sweep(src, off, yh, start, m, store):
            x = [[src[c, start + off + j] for c in range(2)] for j in range(m + 2)]
            for j in range(m):
                i = start + j
                prev, here, after = x[j], x[j + 1], x[j + 2]
                q = [0.25 * (after[c] - prev[c]) for c in range(2)]
                k, g = cos[0, i + 1], cos[1, i + 1]
                for c in range(2):
                    edge = pltpu.roll(yh[c, i + off], shift, 1)
                    up = jnp.where(first, edge, here[c] + q[1 - c])
                    down = jnp.where(last, edge, here[c] - q[1 - c])
                    around = prev[c] + after[c] + (pltpu.roll(up, 127, 1) + pltpu.roll(down, 1, 1))
                    store(c, i, k * here[c] + cos[2 + c, i + 1] + g * around)

        def keep(c, i, value):
            v1s[c, i + 1] = value

        def give(c, i, value):
            out_ref[c, u, pl.ds(i, 8, stride=S), :] = value

        def first_sweep(start, m):
            sweep(xs, 1, yh1, start, m, keep)

        def second_sweep(start, m):
            sweep(v1s, 0, yh2, start, m, give)

        put(
            halo_rows(xs, S, low, high, lambda c, i: v_ref[c, u, pl.ds(i, 8, stride=S), :])
            + halo_coefficients(cos, S, low, high, get)
        )
        over_rows(0, S, load, 16)
        over_rows(-1, S + 1, first_sweep, 17)
        over_rows(0, S, second_sweep, 16)
        return 0

    lax.fori_loop(0, tb, layer, 0)


def sweeps(v, f, pinned, heated, lo, hi, heated_rows, yh1, yh2):
    _, T, n, _ = v.shape
    S = n // 8
    tb = 2
    return pl.pallas_call(
        functools.partial(sweep_kernel, tb, n),
        grid=(T // tb,),
        in_specs=[
            pl.BlockSpec((2, tb, n, 128), lambda t: (0, t, 0, 0)),
            pl.BlockSpec((2, tb, n, 128), lambda t: (0, t, 0, 0)),
            pl.BlockSpec((tb, n, 128), lambda t: (t, 0, 0)),
            pl.BlockSpec((tb, n, 128), lambda t: (t, 0, 0)),
            whole((T, 8, 128)),
            whole((T, 8, 128)),
            whole((2, T, 128)),
            whole((2, S + 2, 8, 128)),
            whole((2, S, 8, 128)),
        ],
        out_specs=pl.BlockSpec((2, tb, n, 128), lambda t: (0, t, 0, 0)),
        out_shape=jax.ShapeDtypeStruct((2, T, n, 128), F32),
        scratch_shapes=[
            pltpu.VMEM((2, S + 4, 8, 128), F32),
            pltpu.VMEM((2, S + 2, 8, 128), F32),
            pltpu.VMEM((4, S + 2, 8, 128), F32),
        ],
        compiler_params=pltpu.CompilerParams(vmem_limit_bytes=57 * MIB),
        cost_estimate=pl.CostEstimate(
            flops=60 * T * n * 128, bytes_accessed=32 * T * n * 128, transcendentals=T * n * 128
        ),
        name="sweeps",
    )(v, f, pinned, heated, lo, hi, heated_rows, yh1, yh2)


def shifted(up_going, down_going, axis):
    count = lax.axis_size(axis)
    up = [(i, i + 1) for i in range(count - 1)]
    down = [(j, i) for i, j in up]
    return lax.ppermute(up_going, axis, up), lax.ppermute(down_going, axis, down)


def local(prior, d, v, f, pinned):
    J = lax.axis_size("wid")
    lo, hi = edge_rows(v, f, pinned)
    from_below, from_above = shifted(hi, lo, "wid")
    seg, pq = moments(d, prior)
    pqs = [pq] + [lax.ppermute(pq, "wid", [(i, (i + s) % J) for i in range(J)]) for s in range(1, J)]
    own, right, left = pack(v, f, pinned, from_below, from_above)
    from_left, from_right = shifted(right, left, "len")
    heated, columns, heated_rows = heat(d, pqs, seg, prior)
    heat_left, heat_right = shifted(columns, columns, "len")
    yh1, yh2 = strips(own, from_left, from_right, heat_left, heat_right)
    flow = sweeps(v, f, pinned, heated, from_below, from_above, heated_rows, yh1, yh2)
    return heated, flow


def solution(mesh):
    in_specs = (
        P(None, "wid", "len"),
        P(None, "len"),
        P(None, None, "wid", "len"),
        P(None, None, "wid", "len"),
        P(None, "wid", "len"),
    )
    out_specs = (P(None, "wid", "len"), P(None, None, "wid", "len"))
    return jax.shard_map(local, mesh=mesh, in_specs=in_specs, out_specs=out_specs, check_vma=False)
```

```python
import functools

import jax
import jax.numpy as jnp
from jax import lax
from jax.experimental import pallas as pl
from jax.experimental.pallas import tpu as pltpu
from jax.sharding import PartitionSpec as P

DRAG_COEFF = 0.5
RELAX_FACTOR = 0.8
HALF_LOG2E = -0.7213475204444817
F32 = jnp.float32
MIB = 1 << 20


def decay(d):
    x = 1.0 / d
    one_less = jnp.sqrt(x + 0.25 * x * x) - 0.5 * x
    r = 1.0 - one_less
    return r, (1.0 - r) / (1.0 + r)


def power(r, n):
    out = None
    while n:
        if n & 1:
            out = r if out is None else out * r
        n >>= 1
        if n:
            r = r * r
    return out


def sublane_powers(r, shape):
    s = lax.broadcasted_iota(jnp.int32, shape, 0)
    r2 = r * r
    r4 = r2 * r2
    one = jnp.ones(shape, F32)
    return (
        jnp.where((s & 1) != 0, r, one)
        * jnp.where((s & 2) != 0, r2, one)
        * jnp.where((s & 4) != 0, r4, one)
    )


def reciprocal(x):
    y = pl.reciprocal(x, approx=True)
    return y * (2.0 - x * y)


def batches(lo, hi, most=11):
    parts = -(-(hi - lo) // most)
    cuts = [lo + (hi - lo) * k // parts for k in range(parts + 1)]
    return [range(a, b) for a, b in zip(cuts, cuts[1:])]


def over_rows(first, stop, body, most=8):
    count = stop - first
    m = max(k for k in range(1, most + 1) if count % k == 0)

    def step(k, _):
        body(first + k * m, m)
        return 0

    lax.fori_loop(0, count // m, step, 0)


def iotas():
    lane = lax.broadcasted_iota(jnp.int32, (8, 128), 1)
    sub = lax.broadcasted_iota(jnp.int32, (8, 128), 0)
    return lane, sub


def moments_kernel(tb, n, d_ref, f_ref, seg_ref, pq_ref):
    S = n // 8
    base = pl.program_id(0) * tb
    G = 4
    for g in range(tb // G):
        rs = []
        for u in range(G):
            r, _ = decay(d_ref[pl.ds(base + g * G + u, 1), :])
            rs.append(jnp.broadcast_to(r, (8, 128)))
        fwd = [f_ref[g * G + u, pl.ds(0, 8, stride=S), :] for u in range(G)]
        bwd, weight = list(fwd), list(rs)
        for i in range(1, S):
            for u in range(G):
                x = f_ref[g * G + u, pl.ds(i, 8, stride=S), :]
                fwd[u] = fwd[u] * rs[u] + x
                bwd[u] = bwd[u] + weight[u] * x
                weight[u] = weight[u] * rs[u]
        for u in range(G):
            k = g * G + u
            seg_ref[0, k] = fwd[u]
            seg_ref[1, k] = bwd[u]
            rS = power(rs[u], S)
            up = sublane_powers(rS, (8, 128))
            s = lax.broadcasted_iota(jnp.int32, (8, 128), 0)
            rS2 = rS * rS
            one = jnp.ones((8, 128), F32)
            down = (
                jnp.where((s & 1) == 0, rS, one)
                * jnp.where((s & 2) == 0, rS2, one)
                * jnp.where((s & 4) == 0, rS2 * rS2, one)
            )
            pq_ref[0, k : k + 1, :] = jnp.sum(fwd[u] * down, axis=0, keepdims=True)
            pq_ref[1, k : k + 1, :] = jnp.sum(bwd[u] * up, axis=0, keepdims=True)


def moments(d, prior):
    T, n, _ = prior.shape
    tb = 8
    return pl.pallas_call(
        functools.partial(moments_kernel, tb, n),
        grid=(T // tb,),
        in_specs=[
            pl.BlockSpec((T, 128), lambda t: (0, 0)),
            pl.BlockSpec((tb, n, 128), lambda t: (t, 0, 0)),
        ],
        out_specs=[
            pl.BlockSpec((2, tb, 8, 128), lambda t: (0, t, 0, 0)),
            pl.BlockSpec((2, tb, 128), lambda t: (0, t, 0)),
        ],
        out_shape=[
            jax.ShapeDtypeStruct((2, T, 8, 128), F32),
            jax.ShapeDtypeStruct((2, T, 128), F32),
        ],
        compiler_params=pltpu.CompilerParams(vmem_limit_bytes=57 * MIB),
        cost_estimate=pl.CostEstimate(flops=4 * T * n * 128, bytes_accessed=4 * T * n * 128, transcendentals=0),
        name="moments",
    )(d, prior)


def rows_kernel(T, v_lo, v_hi, f_lo, f_hi, p_lo, p_hi, lo_ref, hi_ref):
    _, sub = iotas()

    def stack(v0, v1, f0, f1, fr):
        out = jnp.where(sub < 2, v0, v1)
        out = jnp.where(sub >= 4, f0, out)
        out = jnp.where(sub >= 5, f1, out)
        out = jnp.where(sub >= 6, fr, out)
        return jnp.where(sub >= 7, 0.0, out)

    for v, f, p, out, shifts in (
        (v_lo, f_lo, p_lo, lo_ref, (0, 2, 4, 5, 6)),
        (v_hi, f_hi, p_hi, hi_ref, (2, 4, 5, 6, 7)),
    ):
        for t in range(T):
            raw = [v[0, t], v[1, t], f[0, t], f[1, t], 1.0 - p[t].astype(F32)]
            out[t] = stack(*[pltpu.roll(x, q, 0) if q else x for x, q in zip(raw, shifts)])


def whole(shape):
    return pl.BlockSpec(shape, lambda t: (0,) * len(shape))


def edge_rows(v, f, pinned):
    _, T, n, _ = v.shape
    row = jax.ShapeDtypeStruct((T, 8, 128), F32)
    end = n // 8 - 1
    four = [pl.BlockSpec((2, T, 8, 128), lambda t, k=k: (0, 0, k, 0)) for k in (0, end)]
    three = [pl.BlockSpec((T, 8, 128), lambda t, k=k: (0, k, 0)) for k in (0, end)]
    return pl.pallas_call(
        functools.partial(rows_kernel, T),
        grid=(1,),
        in_specs=[*four, *four, *three],
        out_specs=[whole((T, 8, 128))] * 2,
        out_shape=[row, row],
        compiler_params=pltpu.CompilerParams(vmem_limit_bytes=57 * MIB),
        cost_estimate=pl.CostEstimate(flops=0, bytes_accessed=48 * T * 8 * 128, transcendentals=0),
        name="edge_rows",
    )(v, v, f, f, pinned, pinned)


def gather_columns(ref, T):
    lane, _ = iotas()
    parts = [jnp.where(lane >> 2 == t, pltpu.roll(ref[t], (4 * t + 2) & 127, 1), 0.0) for t in range(T)]
    while len(parts) > 1:
        parts = [p + q for p, q in zip(parts[::2], parts[1::2])]
    return parts[0]


def pack_kernel(tb, n, T, v_ref, f_ref, p_ref, lo_ref, hi_ref, after_ref, pk_ref, right_ref, left_ref, fp_ref):
    base = pl.program_id(0) * tb
    lane = lax.broadcasted_iota(jnp.int32, (n, 128), 1)
    group = lane >> 2
    for k in range(5):
        ref, q = (pk_ref, k) if k < 2 else (fp_ref, k - 2)
        acc = ref[q, 0:n, :]
        for u in range(tb):
            if k < 2:
                x = v_ref[k, u]
            elif k < 4:
                x = f_ref[k - 2, u]
            else:
                x = 1.0 - p_ref[u].astype(F32)
            t = base + u
            acc = jnp.where(group == t, pltpu.roll(x, (4 * t + 2) & 127, 1), acc)
        ref[q, 0:n, :] = acc

    @pl.when(pl.program_id(0) == pl.num_programs(0) - 1)
    def _():
        slot = lane & 3
        v0, v1 = pk_ref[0, 0:n, :], pk_ref[1, 0:n, :]
        f0, f1, fr = fp_ref[0], fp_ref[1], fp_ref[2]

        def sel(a, b, c):
            return jnp.where(slot < 1, a, jnp.where(slot == 1, b, c))

        right_ref[0, 0:n, :] = jnp.where(slot < 2, v0, pltpu.roll(v1, 2, 1))
        left_ref[0, 0:n, :] = jnp.where(slot >= 2, v0, pltpu.roll(v1, 126, 1))
        right_ref[1, 0:n, :] = sel(pltpu.roll(f0, 127, 1), f1, pltpu.roll(fr, 1, 1))
        left_ref[1, 0:n, :] = sel(pltpu.roll(f0, 126, 1), pltpu.roll(f1, 127, 1), fr)
        for k, ref in ((0, lo_ref), (1, hi_ref)):
            tile = gather_columns(ref, T)
            for out in (pk_ref, right_ref, left_ref):
                out[k, n : n + 8, :] = tile


def pack(v, f, pinned, lo, hi, after):
    _, T, n, _ = v.shape
    tb = 4
    out = jax.ShapeDtypeStruct((2, n + 8, 128), F32)
    return pl.pallas_call(
        functools.partial(pack_kernel, tb, n, T),
        grid=(T // tb,),
        in_specs=[
            pl.BlockSpec((2, tb, n, 128), lambda t: (0, t, 0, 0)),
            pl.BlockSpec((2, tb, n, 128), lambda t: (0, t, 0, 0)),
            pl.BlockSpec((tb, n, 128), lambda t: (t, 0, 0)),
            whole((T, 8, 128)),
            whole((T, 8, 128)),
            pl.BlockSpec(memory_space=pl.ANY),
        ],
        out_specs=[whole((2, n + 8, 128))] * 3,
        out_shape=[out, out, out],
        scratch_shapes=[pltpu.VMEM((3, n, 128), F32)],
        compiler_params=pltpu.CompilerParams(vmem_limit_bytes=57 * MIB),
        cost_estimate=pl.CostEstimate(flops=5 * T * n * 128, bytes_accessed=20 * T * n * 128, transcendentals=0),
        name="pack_edges",
    )(v, f, pinned, lo, hi, after)


def heat_kernel(J, tb, n, *refs):
    d_ref, *pq_refs = refs[: J + 1]
    (
        seg_ref, f_ref,
        out_ref, send_ref, row_ref, alls, sums, ys,
    ) = refs[J + 1 :]
    S = n // 8
    step = pl.program_id(0)
    base = step * tb

    @pl.when(step == 0)
    def _():
        j = lax.axis_index("wid")
        for s in range(J):
            alls[lax.rem(j - s + J, J)] = pq_refs[s][...]
        r, _ = decay(d_ref[...])
        rn = power(r, n)
        rN = power(rn, J)
        sp = alls[0, 0]
        for i in range(1, J):
            sp = sp * rn + alls[i, 0]
        sq = alls[J - 1, 1]
        for i in range(J - 2, -1, -1):
            sq = sq * rn + alls[i, 1]
        inv = 1.0 / (1.0 - rN * rN)
        left = (sq + rN * sp) * inv
        right = (sp + rN * sq) * inv
        for i in range(J - 1):
            left = jnp.where(i < j, rn * left + alls[i, 0], left)
        for i in range(J - 1, 0, -1):
            right = jnp.where(i > j, rn * right + alls[i, 1], right)
        sums[0] = left
        sums[1] = right

    _, sub = iotas()
    rs, gain, y, z = [], [], [], []
    for u in range(tb):
        t = base + u
        r, a0 = decay(d_ref[pl.ds(t, 1), :])
        r = jnp.broadcast_to(r, (8, 128))
        a0 = jnp.broadcast_to(a0, (8, 128))
        rS = power(r, S)
        rS2 = rS * rS
        rS4 = rS2 * rS2
        c = jnp.where(sub == 0, sums[0, pl.ds(t, 1), :], pltpu.roll(seg_ref[0, u], 1, 0))
        b = jnp.where(sub == 7, sums[1, pl.ds(t, 1), :], pltpu.roll(seg_ref[1, u], 7, 0))
        for s, q in ((1, rS), (2, rS2), (4, rS4)):
            c = c + q * jnp.where(sub >= s, pltpu.roll(c, s, 0), 0.0)
            b = b + q * jnp.where(sub < 8 - s, pltpu.roll(b, 8 - s, 0), 0.0)
        rs.append(r)
        gain.append(a0)
        y.append(c)
        z.append(b)
    for rows in batches(0, S, 8):
        done = []
        for i in rows:
            for u in range(tb):
                y[u] = y[u] * rs[u] + f_ref[u, pl.ds(i, 8, stride=S), :]
                done.append((u, i, y[u]))
        for u, i, value in done:
            ys[u, i] = value
    for rows in batches(0, S, 8)[::-1]:
        done = []
        for i in rows[::-1]:
            for u in range(tb):
                zr = z[u] * rs[u]
                done.append((u, i, gain[u] * (ys[u, i] + zr)))
                z[u] = zr + f_ref[u, pl.ds(i, 8, stride=S), :]
        for u, i, value in done:
            out_ref[u, pl.ds(i, 8, stride=S), :] = value

    lane_n = lax.broadcasted_iota(jnp.int32, (n, 128), 1)
    group = lane_n >> 2
    acc = send_ref[0:n, :]
    tile = send_ref[n : n + 8, :]
    lane, _ = iotas()
    rows = []
    for u in range(tb):
        t = base + u
        acc = jnp.where(group == t, pltpu.roll(out_ref[u], (4 * t + 2) & 127, 1), acc)
        below = gain[u][0:1] * (sums[0, pl.ds(t, 1), :] + rs[u][0:1] * z[u][0:1])
        above = gain[u][0:1] * (sums[1, pl.ds(t, 1), :] + rs[u][0:1] * y[u][7:8])
        both = jnp.where(sub == 0, below, above)
        rows.append((u, below, above))
        tile = jnp.where(lane >> 2 == t, pltpu.roll(both, (4 * t + 2) & 127, 1), tile)
    send_ref[0:n, :] = acc
    send_ref[n : n + 8, :] = tile
    for u, below, above in rows:
        row_ref[0, pl.ds(base + u, 1), :] = below
        row_ref[1, pl.ds(base + u, 1), :] = above


def heat(d, pqs, seg, prior):
    T, n, _ = prior.shape
    J = len(pqs)
    tb = 4
    return pl.pallas_call(
        functools.partial(heat_kernel, J, tb, n),
        grid=(T // tb,),
        in_specs=[
            whole((T, 128)),
            *[whole((2, T, 128)) for _ in range(J)],
            pl.BlockSpec((2, tb, 8, 128), lambda t: (0, t, 0, 0)),
            pl.BlockSpec((tb, n, 128), lambda t: (t, 0, 0)),
        ],
        out_specs=[
            pl.BlockSpec((tb, n, 128), lambda t: (t, 0, 0)),
            whole((n + 8, 128)),
            whole((2, T, 128)),
        ],
        out_shape=[
            jax.ShapeDtypeStruct((T, n, 128), F32),
            jax.ShapeDtypeStruct((n + 8, 128), F32),
            jax.ShapeDtypeStruct((2, T, 128), F32),
        ],
        scratch_shapes=[
            pltpu.VMEM((J, 2, T, 128), F32),
            pltpu.VMEM((2, T, 128), F32),
            pltpu.VMEM((tb, n // 8, 8, 128), F32),
        ],
        compiler_params=pltpu.CompilerParams(vmem_limit_bytes=57 * MIB),
        cost_estimate=pl.CostEstimate(flops=10 * T * n * 128, bytes_accessed=8 * T * n * 128, transcendentals=0),
        name="heat",
    )(d, *pqs, seg, prior)


def coefficients(f0, f1, free, heated):
    v = jnp.exp2(HALF_LOG2E * heated)
    w = RELAX_FACTOR * free
    a = w * reciprocal(DRAG_COEFF + 4.0 * v)
    return 1.0 - w, a * v, a * f0, a * f1


def under(row, last_vector):
    _, sub = iotas()
    return jnp.where(sub == 0, row, pltpu.roll(last_vector, 1, 0))


def over(row, first_vector):
    _, sub = iotas()
    return jnp.where(sub == 7, row, pltpu.roll(first_vector, 7, 0))


def put(todo):
    for ref, c, i, value in todo:
        ref[c, i] = value


def halo_rows(ref, S, low, high, get):
    todo = []
    for c in range(2):
        for q in range(2):
            todo.append((ref, c, q, under(low(2 * c + q), get(c, S - 2 + q))))
            todo.append((ref, c, S + 2 + q, over(high(2 * c + q), get(c, q))))
    return todo


def halo_coefficients(cos, S, low, high, get):
    below = coefficients(*[under(low(4 + m), get(m, S - 1)) for m in range(4)])
    above = coefficients(*[over(high(4 + m), get(m, 0)) for m in range(4)])
    return [(cos, m, 0, below[m]) for m in range(4)] + [(cos, m, S + 1, above[m]) for m in range(4)]


def strip_kernel(n, own_ref, fl_ref, fr_ref, hl_ref, hr_ref, yh1, yh2, r_ref, edge, xs, ws, r1s, cos):
    S = n // 8
    lane, sub = iotas()
    slot = lane & 3
    outer = (slot == 0) | (slot == 3)
    sign = jnp.where(slot == 1, -0.25, 0.25)

    low_n = lax.broadcasted_iota(jnp.int32, (n, 128), 1) & 3 < 2
    al, ar, bl, br = [ref[k, 0:n, :] for k in range(2) for ref in (fl_ref, fr_ref)]
    r_ref[0] = jnp.where(low_n, al, ar)
    r_ref[1] = jnp.where(low_n, pltpu.roll(al, 126, 1), pltpu.roll(ar, 2, 1))
    for k in range(3):
        a = bl if k == 1 else pltpu.roll(bl, (1 - k) & 127, 1)
        b = br if k == 2 else pltpu.roll(br, (2 - k) & 127, 1)
        r_ref[2 + k] = jnp.where(low_n, a, b)
    r_ref[5] = jnp.where(low_n, hl_ref[0:n, :], hr_ref[0:n, :])
    heat_rows = jnp.where(slot < 2, hl_ref[n : n + 8, :], hr_ref[n : n + 8, :])
    for k in range(2):
        tile = jnp.where(slot < 2, fl_ref[k, n : n + 8, :], fr_ref[k, n : n + 8, :])
        edge[k] = jnp.where(sub == 7, heat_rows[k : k + 1, :], tile)
        edge[2 + k] = jnp.where(outer, tile, own_ref[k, n : n + 8, :])

    def low(k):
        return edge[0, k : k + 1, :]

    def high(k):
        return edge[1, k : k + 1, :]

    def get(m, i):
        return r_ref[2 + m, pl.ds(i, 8, stride=S), :]

    def load(start, m):
        todo = []
        for i in [start + j for j in range(m)]:
            for c in range(2):
                r = r_ref[c, pl.ds(i, 8, stride=S), :]
                todo.append((xs, c, i + 2, r))
                todo.append((ws, c, i + 2, jnp.where(outer, r, own_ref[c, pl.ds(i, 8, stride=S), :])))
            co = coefficients(*[get(q, i) for q in range(4)])
            todo += [(cos, q, i + 1, co[q]) for q in range(4)]
        put(todo)

    over_rows(0, S, load)
    def row_low(k):
        return edge[2, k : k + 1, :]

    def row_high(k):
        return edge[3, k : k + 1, :]

    def get_r(c, i):
        return r_ref[c, pl.ds(i, 8, stride=S), :]

    def get_w(c, i):
        return jnp.where(outer, get_r(c, i), own_ref[c, pl.ds(i, 8, stride=S), :])

    put(
        halo_rows(xs, S, low, high, get_r)
        + halo_rows(ws, S, row_low, row_high, get_w)
        + halo_coefficients(cos, S, low, high, get)
    )

    def relax(start, m):
        r = [[xs[c, start + 1 + j] for c in range(2)] for j in range(m + 2)]
        w = [[ws[c, start + 1 + j] for c in range(2)] for j in range(m + 2)]
        todo = []
        for j in range(m):
            i = start + j
            for c in range(2):
                q = 0.25 * (w[j + 2][1 - c] - w[j][1 - c])
                around = (
                    r[j][c] + r[j + 2][c] + pltpu.roll(w[j + 1][c] + q, 127, 1) + pltpu.roll(w[j + 1][c] - q, 1, 1)
                )
                todo.append((yh1, c, i + 1, r[j + 1][c] + sign * (r[j + 2][1 - c] - r[j][1 - c])))
                new = cos[0, i + 1] * r[j + 1][c] + cos[2 + c, i + 1] + cos[1, i + 1] * around
                todo.append((r1s, c, i + 1, new))
        put(todo)

    over_rows(-1, S + 1, relax, 17)

    def edges(start, m):
        r = [[r1s[c, start + j] for c in range(2)] for j in range(m + 2)]
        put(
            [
                (yh2, c, start + j, r[j + 1][c] + sign * (r[j + 2][1 - c] - r[j][1 - c]))
                for j in range(m)
                for c in range(2)
            ]
        )

    over_rows(0, S, edges, 16)


def strips(own, fl, fr, hl, hr):
    n = own.shape[1] - 8
    S = n // 8
    return pl.pallas_call(
        functools.partial(strip_kernel, n),
        grid=(1,),
        in_specs=[whole(own.shape), whole(fl.shape), whole(fr.shape), whole(hl.shape), whole(hr.shape)],
        out_specs=[whole((2, S + 2, 8, 128)), whole((2, S, 8, 128))],
        out_shape=[
            jax.ShapeDtypeStruct((2, S + 2, 8, 128), F32),
            jax.ShapeDtypeStruct((2, S, 8, 128), F32),
        ],
        scratch_shapes=[
            pltpu.VMEM((6, n, 128), F32),
            pltpu.VMEM((4, 8, 128), F32),
            pltpu.VMEM((2, S + 4, 8, 128), F32),
            pltpu.VMEM((2, S + 4, 8, 128), F32),
            pltpu.VMEM((2, S + 2, 8, 128), F32),
            pltpu.VMEM((4, S + 2, 8, 128), F32),
        ],
        compiler_params=pltpu.CompilerParams(vmem_limit_bytes=12 * MIB),
        cost_estimate=pl.CostEstimate(flops=60 * n * 128, bytes_accessed=60 * n * 128, transcendentals=n * 128),
        name="strips",
    )(own, fl, fr, hl, hr)


def sweep_kernel(tb, n, v_ref, f_ref, p_ref, h_ref, lo_ref, hi_ref, row_ref, yh1, yh2, out_ref, xs, v1s, cos):
    S = n // 8
    step = pl.program_id(0)
    lane, _ = iotas()
    first, last = lane == 0, lane == 127

    def layer(u, _):
        t = step * tb + u
        shift = (126 - 4 * t) & 127

        def low(k):
            return row_ref[0, pl.ds(t, 1), :] if k == 7 else lo_ref[t, k : k + 1, :]

        def high(k):
            return row_ref[1, pl.ds(t, 1), :] if k == 7 else hi_ref[t, k : k + 1, :]

        def get(m, i):
            rows = pl.ds(i, 8, stride=S)
            if m < 2:
                return f_ref[m, u, rows, :]
            return 1.0 - p_ref[u, rows, :].astype(F32) if m == 2 else h_ref[u, rows, :]

        def load(start, m):
            todo = []
            for i in [start + j for j in range(m)]:
                todo += [(xs, c, i + 2, v_ref[c, u, pl.ds(i, 8, stride=S), :]) for c in range(2)]
                co = coefficients(*[get(q, i) for q in range(4)])
                todo += [(cos, q, i + 1, co[q]) for q in range(4)]
            put(todo)

        def sweep(src, off, yh, start, m, store):
            x = [[src[c, start + off + j] for c in range(2)] for j in range(m + 2)]
            for j in range(m):
                i = start + j
                prev, here, after = x[j], x[j + 1], x[j + 2]
                q = [0.25 * (after[c] - prev[c]) for c in range(2)]
                k, g = cos[0, i + 1], cos[1, i + 1]
                for c in range(2):
                    edge = pltpu.roll(yh[c, i + off], shift, 1)
                    up = jnp.where(first, edge, here[c] + q[1 - c])
                    down = jnp.where(last, edge, here[c] - q[1 - c])
                    around = prev[c] + after[c] + (pltpu.roll(up, 127, 1) + pltpu.roll(down, 1, 1))
                    store(c, i, k * here[c] + cos[2 + c, i + 1] + g * around)

        def keep(c, i, value):
            v1s[c, i + 1] = value

        def give(c, i, value):
            out_ref[c, u, pl.ds(i, 8, stride=S), :] = value

        def first_sweep(start, m):
            sweep(xs, 1, yh1, start, m, keep)

        def second_sweep(start, m):
            sweep(v1s, 0, yh2, start, m, give)

        put(
            halo_rows(xs, S, low, high, lambda c, i: v_ref[c, u, pl.ds(i, 8, stride=S), :])
            + halo_coefficients(cos, S, low, high, get)
        )
        over_rows(0, S, load, 16)
        over_rows(-1, S + 1, first_sweep, 17)
        over_rows(0, S, second_sweep, 16)
        return 0

    lax.fori_loop(0, tb, layer, 0)


def sweeps(v, f, pinned, heated, lo, hi, heated_rows, yh1, yh2):
    _, T, n, _ = v.shape
    S = n // 8
    tb = 4
    return pl.pallas_call(
        functools.partial(sweep_kernel, tb, n),
        grid=(T // tb,),
        in_specs=[
            pl.BlockSpec((2, tb, n, 128), lambda t: (0, t, 0, 0)),
            pl.BlockSpec((2, tb, n, 128), lambda t: (0, t, 0, 0)),
            pl.BlockSpec((tb, n, 128), lambda t: (t, 0, 0)),
            pl.BlockSpec((tb, n, 128), lambda t: (t, 0, 0)),
            whole((T, 8, 128)),
            whole((T, 8, 128)),
            whole((2, T, 128)),
            whole((2, S + 2, 8, 128)),
            whole((2, S, 8, 128)),
        ],
        out_specs=pl.BlockSpec((2, tb, n, 128), lambda t: (0, t, 0, 0)),
        out_shape=jax.ShapeDtypeStruct((2, T, n, 128), F32),
        scratch_shapes=[
            pltpu.VMEM((2, S + 4, 8, 128), F32),
            pltpu.VMEM((2, S + 2, 8, 128), F32),
            pltpu.VMEM((4, S + 2, 8, 128), F32),
        ],
        compiler_params=pltpu.CompilerParams(vmem_limit_bytes=57 * MIB),
        cost_estimate=pl.CostEstimate(
            flops=60 * T * n * 128, bytes_accessed=32 * T * n * 128, transcendentals=T * n * 128
        ),
        name="sweeps",
    )(v, f, pinned, heated, lo, hi, heated_rows, yh1, yh2)


def shifted(up_going, down_going, axis):
    count = lax.axis_size(axis)
    up = [(i, i + 1) for i in range(count - 1)]
    down = [(j, i) for i, j in up]
    return lax.ppermute(up_going, axis, up), lax.ppermute(down_going, axis, down)


def local(prior, d, v, f, pinned):
    J = lax.axis_size("wid")
    lo, hi = edge_rows(v, f, pinned)
    from_below, from_above = shifted(hi, lo, "wid")
    seg, pq = moments(d, prior)
    pqs = [pq] + [lax.ppermute(pq, "wid", [(i, (i + s) % J) for i in range(J)]) for s in range(1, J)]
    own, right, left = pack(v, f, pinned, from_below, from_above, pq)
    right, left, *pqs = lax.optimization_barrier((right, left, *pqs))
    from_left, from_right = shifted(right, left, "len")
    heated, columns, heated_rows = heat(d, pqs, seg, prior)
    heat_left, heat_right = shifted(columns, columns, "len")
    yh1, yh2 = strips(own, from_left, from_right, heat_left, heat_right)
    flow = sweeps(v, f, pinned, heated, from_below, from_above, heated_rows, yh1, yh2)
    return heated, flow


def solution(mesh):
    in_specs = (
        P(None, "wid", "len"),
        P(None, "len"),
        P(None, None, "wid", "len"),
        P(None, None, "wid", "len"),
        P(None, "wid", "len"),
    )
    out_specs = (P(None, "wid", "len"), P(None, None, "wid", "len"))
    return jax.shard_map(local, mesh=mesh, in_specs=in_specs, out_specs=out_specs, check_vma=False)
```

```python
import functools

import jax
import jax.numpy as jnp
from jax import lax
from jax.experimental import pallas as pl
from jax.experimental.pallas import tpu as pltpu
from jax.sharding import PartitionSpec as P

DRAG_COEFF = 0.5
RELAX_FACTOR = 0.8
HALF_LOG2E = -0.7213475204444817
F32 = jnp.float32
MIB = 1 << 20


def decay(d):
    x = 1.0 / d
    one_less = jnp.sqrt(x + 0.25 * x * x) - 0.5 * x
    r = 1.0 - one_less
    return r, (1.0 - r) / (1.0 + r)


def power(r, n):
    out = None
    while n:
        if n & 1:
            out = r if out is None else out * r
        n >>= 1
        if n:
            r = r * r
    return out


def sublane_powers(r, shape):
    s = lax.broadcasted_iota(jnp.int32, shape, 0)
    r2 = r * r
    r4 = r2 * r2
    one = jnp.ones(shape, F32)
    return (
        jnp.where((s & 1) != 0, r, one)
        * jnp.where((s & 2) != 0, r2, one)
        * jnp.where((s & 4) != 0, r4, one)
    )


def reciprocal(x):
    y = pl.reciprocal(x, approx=True)
    return y * (2.0 - x * y)


def batches(lo, hi, most=11):
    parts = -(-(hi - lo) // most)
    cuts = [lo + (hi - lo) * k // parts for k in range(parts + 1)]
    return [range(a, b) for a, b in zip(cuts, cuts[1:])]


def over_rows(first, stop, body, most=8):
    count = stop - first
    m = max(k for k in range(1, most + 1) if count % k == 0)

    def step(k, _):
        body(first + k * m, m)
        return 0

    lax.fori_loop(0, count // m, step, 0)


def iotas():
    lane = lax.broadcasted_iota(jnp.int32, (8, 128), 1)
    sub = lax.broadcasted_iota(jnp.int32, (8, 128), 0)
    return lane, sub


def moments_kernel(tb, n, d_ref, f_ref, seg_ref, pq_ref):
    S = n // 8
    base = pl.program_id(0) * tb
    G = 4
    for g in range(tb // G):
        rs = []
        for u in range(G):
            r, _ = decay(d_ref[pl.ds(base + g * G + u, 1), :])
            rs.append(jnp.broadcast_to(r, (8, 128)))
        fwd = [f_ref[g * G + u, pl.ds(0, 8, stride=S), :] for u in range(G)]
        bwd, weight = list(fwd), list(rs)
        for i in range(1, S):
            for u in range(G):
                x = f_ref[g * G + u, pl.ds(i, 8, stride=S), :]
                fwd[u] = fwd[u] * rs[u] + x
                bwd[u] = bwd[u] + weight[u] * x
                weight[u] = weight[u] * rs[u]
        for u in range(G):
            k = g * G + u
            seg_ref[0, k] = fwd[u]
            seg_ref[1, k] = bwd[u]
            rS = power(rs[u], S)
            up = sublane_powers(rS, (8, 128))
            s = lax.broadcasted_iota(jnp.int32, (8, 128), 0)
            rS2 = rS * rS
            one = jnp.ones((8, 128), F32)
            down = (
                jnp.where((s & 1) == 0, rS, one)
                * jnp.where((s & 2) == 0, rS2, one)
                * jnp.where((s & 4) == 0, rS2 * rS2, one)
            )
            pq_ref[0, k : k + 1, :] = jnp.sum(fwd[u] * down, axis=0, keepdims=True)
            pq_ref[1, k : k + 1, :] = jnp.sum(bwd[u] * up, axis=0, keepdims=True)


def moments(d, prior):
    T, n, _ = prior.shape
    tb = 8
    return pl.pallas_call(
        functools.partial(moments_kernel, tb, n),
        grid=(T // tb,),
        in_specs=[
            pl.BlockSpec((T, 128), lambda t: (0, 0)),
            pl.BlockSpec((tb, n, 128), lambda t: (t, 0, 0)),
        ],
        out_specs=[
            pl.BlockSpec((2, tb, 8, 128), lambda t: (0, t, 0, 0)),
            pl.BlockSpec((2, tb, 128), lambda t: (0, t, 0)),
        ],
        out_shape=[
            jax.ShapeDtypeStruct((2, T, 8, 128), F32),
            jax.ShapeDtypeStruct((2, T, 128), F32),
        ],
        compiler_params=pltpu.CompilerParams(vmem_limit_bytes=57 * MIB),
        cost_estimate=pl.CostEstimate(flops=4 * T * n * 128, bytes_accessed=4 * T * n * 128, transcendentals=0),
        name="moments",
    )(d, prior)


def rows_kernel(T, v_lo, v_hi, f_lo, f_hi, p_lo, p_hi, lo_ref, hi_ref):
    _, sub = iotas()

    def stack(v0, v1, f0, f1, fr):
        out = jnp.where(sub < 2, v0, v1)
        out = jnp.where(sub >= 4, f0, out)
        out = jnp.where(sub >= 5, f1, out)
        out = jnp.where(sub >= 6, fr, out)
        return jnp.where(sub >= 7, 0.0, out)

    for v, f, p, out, shifts in (
        (v_lo, f_lo, p_lo, lo_ref, (0, 2, 4, 5, 6)),
        (v_hi, f_hi, p_hi, hi_ref, (2, 4, 5, 6, 7)),
    ):
        for t in range(T):
            raw = [v[0, t], v[1, t], f[0, t], f[1, t], 1.0 - p[t].astype(F32)]
            out[t] = stack(*[pltpu.roll(x, q, 0) if q else x for x, q in zip(raw, shifts)])


def whole(shape):
    return pl.BlockSpec(shape, lambda t: (0,) * len(shape))


def edge_rows(v, f, pinned):
    _, T, n, _ = v.shape
    row = jax.ShapeDtypeStruct((T, 8, 128), F32)
    end = n // 8 - 1
    four = [pl.BlockSpec((2, T, 8, 128), lambda t, k=k: (0, 0, k, 0)) for k in (0, end)]
    three = [pl.BlockSpec((T, 8, 128), lambda t, k=k: (0, k, 0)) for k in (0, end)]
    return pl.pallas_call(
        functools.partial(rows_kernel, T),
        grid=(1,),
        in_specs=[*four, *four, *three],
        out_specs=[whole((T, 8, 128))] * 2,
        out_shape=[row, row],
        compiler_params=pltpu.CompilerParams(vmem_limit_bytes=57 * MIB),
        cost_estimate=pl.CostEstimate(flops=0, bytes_accessed=48 * T * 8 * 128, transcendentals=0),
        name="edge_rows",
    )(v, v, f, f, pinned, pinned)


def gather_columns(ref, T):
    lane, _ = iotas()
    parts = [jnp.where(lane >> 2 == t, pltpu.roll(ref[t], (4 * t + 2) & 127, 1), 0.0) for t in range(T)]
    while len(parts) > 1:
        parts = [p + q for p, q in zip(parts[::2], parts[1::2])]
    return parts[0]


def pack_kernel(tb, n, T, v_ref, f_ref, p_ref, lo_ref, hi_ref, after_ref, pk_ref, right_ref, left_ref, fp_ref):
    base = pl.program_id(0) * tb
    lane = lax.broadcasted_iota(jnp.int32, (n, 128), 1)
    group = lane >> 2
    for k in range(5):
        ref, q = (pk_ref, k) if k < 2 else (fp_ref, k - 2)
        acc = ref[q, 0:n, :]
        for u in range(tb):
            if k < 2:
                x = v_ref[k, u]
            elif k < 4:
                x = f_ref[k - 2, u]
            else:
                x = 1.0 - p_ref[u].astype(F32)
            t = base + u
            acc = jnp.where(group == t, pltpu.roll(x, (4 * t + 2) & 127, 1), acc)
        ref[q, 0:n, :] = acc

    @pl.when(pl.program_id(0) == pl.num_programs(0) - 1)
    def _():
        slot = lane & 3
        v0, v1 = pk_ref[0, 0:n, :], pk_ref[1, 0:n, :]
        f0, f1, fr = fp_ref[0], fp_ref[1], fp_ref[2]

        def sel(a, b, c):
            return jnp.where(slot < 1, a, jnp.where(slot == 1, b, c))

        right_ref[0, 0:n, :] = jnp.where(slot < 2, v0, pltpu.roll(v1, 2, 1))
        left_ref[0, 0:n, :] = jnp.where(slot >= 2, v0, pltpu.roll(v1, 126, 1))
        right_ref[1, 0:n, :] = sel(pltpu.roll(f0, 127, 1), f1, pltpu.roll(fr, 1, 1))
        left_ref[1, 0:n, :] = sel(pltpu.roll(f0, 126, 1), pltpu.roll(f1, 127, 1), fr)
        for k, ref in ((0, lo_ref), (1, hi_ref)):
            tile = gather_columns(ref, T)
            for out in (pk_ref, right_ref, left_ref):
                out[k, n : n + 8, :] = tile


def pack(v, f, pinned, lo, hi, after):
    _, T, n, _ = v.shape
    tb = 4
    out = jax.ShapeDtypeStruct((2, n + 8, 128), F32)
    return pl.pallas_call(
        functools.partial(pack_kernel, tb, n, T),
        grid=(T // tb,),
        in_specs=[
            pl.BlockSpec((2, tb, n, 128), lambda t: (0, t, 0, 0)),
            pl.BlockSpec((2, tb, n, 128), lambda t: (0, t, 0, 0)),
            pl.BlockSpec((tb, n, 128), lambda t: (t, 0, 0)),
            whole((T, 8, 128)),
            whole((T, 8, 128)),
            pl.BlockSpec(memory_space=pl.ANY),
        ],
        out_specs=[whole((2, n + 8, 128))] * 3,
        out_shape=[out, out, out],
        scratch_shapes=[pltpu.VMEM((3, n, 128), F32)],
        compiler_params=pltpu.CompilerParams(vmem_limit_bytes=57 * MIB),
        cost_estimate=pl.CostEstimate(flops=5 * T * n * 128, bytes_accessed=20 * T * n * 128, transcendentals=0),
        name="pack_edges",
    )(v, f, pinned, lo, hi, after)


def heat_kernel(J, tb, n, *refs):
    d_ref, *pq_refs = refs[: J + 1]
    (
        seg_ref, f_ref,
        out_ref, send_ref, row_ref, alls, sums, ys,
    ) = refs[J + 1 :]
    S = n // 8
    step = pl.program_id(0)
    base = step * tb

    @pl.when(step == 0)
    def _():
        j = lax.axis_index("wid")
        for s in range(J):
            alls[lax.rem(j - s + J, J)] = pq_refs[s][...]
        r, _ = decay(d_ref[...])
        rn = power(r, n)
        rN = power(rn, J)
        sp = alls[0, 0]
        for i in range(1, J):
            sp = sp * rn + alls[i, 0]
        sq = alls[J - 1, 1]
        for i in range(J - 2, -1, -1):
            sq = sq * rn + alls[i, 1]
        inv = 1.0 / (1.0 - rN * rN)
        left = (sq + rN * sp) * inv
        right = (sp + rN * sq) * inv
        for i in range(J - 1):
            left = jnp.where(i < j, rn * left + alls[i, 0], left)
        for i in range(J - 1, 0, -1):
            right = jnp.where(i > j, rn * right + alls[i, 1], right)
        sums[0] = left
        sums[1] = right

    _, sub = iotas()
    rs, gain, y, z = [], [], [], []
    for u in range(tb):
        t = base + u
        r, a0 = decay(d_ref[pl.ds(t, 1), :])
        r = jnp.broadcast_to(r, (8, 128))
        a0 = jnp.broadcast_to(a0, (8, 128))
        rS = power(r, S)
        rS2 = rS * rS
        rS4 = rS2 * rS2
        c = jnp.where(sub == 0, sums[0, pl.ds(t, 1), :], pltpu.roll(seg_ref[0, u], 1, 0))
        b = jnp.where(sub == 7, sums[1, pl.ds(t, 1), :], pltpu.roll(seg_ref[1, u], 7, 0))
        for s, q in ((1, rS), (2, rS2), (4, rS4)):
            c = c + q * jnp.where(sub >= s, pltpu.roll(c, s, 0), 0.0)
            b = b + q * jnp.where(sub < 8 - s, pltpu.roll(b, 8 - s, 0), 0.0)
        rs.append(r)
        gain.append(a0)
        y.append(c)
        z.append(b)
    for rows in batches(0, S, 8):
        done = []
        for i in rows:
            for u in range(tb):
                y[u] = y[u] * rs[u] + f_ref[u, pl.ds(i, 8, stride=S), :]
                done.append((u, i, y[u]))
        for u, i, value in done:
            ys[u, i] = value
    for rows in batches(0, S, 8)[::-1]:
        done = []
        for i in rows[::-1]:
            for u in range(tb):
                zr = z[u] * rs[u]
                done.append((u, i, gain[u] * (ys[u, i] + zr)))
                z[u] = zr + f_ref[u, pl.ds(i, 8, stride=S), :]
        for u, i, value in done:
            out_ref[u, pl.ds(i, 8, stride=S), :] = value

    lane_n = lax.broadcasted_iota(jnp.int32, (n, 128), 1)
    group = lane_n >> 2
    acc = send_ref[0:n, :]
    tile = send_ref[n : n + 8, :]
    lane, _ = iotas()
    rows = []
    for u in range(tb):
        t = base + u
        acc = jnp.where(group == t, pltpu.roll(out_ref[u], (4 * t + 2) & 127, 1), acc)
        below = gain[u][0:1] * (sums[0, pl.ds(t, 1), :] + rs[u][0:1] * z[u][0:1])
        above = gain[u][0:1] * (sums[1, pl.ds(t, 1), :] + rs[u][0:1] * y[u][7:8])
        both = jnp.where(sub == 0, below, above)
        rows.append((u, below, above))
        tile = jnp.where(lane >> 2 == t, pltpu.roll(both, (4 * t + 2) & 127, 1), tile)
    send_ref[0:n, :] = acc
    send_ref[n : n + 8, :] = tile
    for u, below, above in rows:
        row_ref[0, pl.ds(base + u, 1), :] = below
        row_ref[1, pl.ds(base + u, 1), :] = above


def heat(d, pqs, seg, prior):
    T, n, _ = prior.shape
    J = len(pqs)
    tb = 4
    return pl.pallas_call(
        functools.partial(heat_kernel, J, tb, n),
        grid=(T // tb,),
        in_specs=[
            whole((T, 128)),
            *[whole((2, T, 128)) for _ in range(J)],
            pl.BlockSpec((2, tb, 8, 128), lambda t: (0, t, 0, 0)),
            pl.BlockSpec((tb, n, 128), lambda t: (t, 0, 0)),
        ],
        out_specs=[
            pl.BlockSpec((tb, n, 128), lambda t: (t, 0, 0)),
            whole((n + 8, 128)),
            whole((2, T, 128)),
        ],
        out_shape=[
            jax.ShapeDtypeStruct((T, n, 128), F32),
            jax.ShapeDtypeStruct((n + 8, 128), F32),
            jax.ShapeDtypeStruct((2, T, 128), F32),
        ],
        scratch_shapes=[
            pltpu.VMEM((J, 2, T, 128), F32),
            pltpu.VMEM((2, T, 128), F32),
            pltpu.VMEM((tb, n // 8, 8, 128), F32),
        ],
        compiler_params=pltpu.CompilerParams(vmem_limit_bytes=57 * MIB),
        cost_estimate=pl.CostEstimate(flops=10 * T * n * 128, bytes_accessed=8 * T * n * 128, transcendentals=0),
        name="heat",
    )(d, *pqs, seg, prior)


def coefficients(f0, f1, free, heated):
    v = jnp.exp2(HALF_LOG2E * heated)
    w = RELAX_FACTOR * free
    a = w * reciprocal(DRAG_COEFF + 4.0 * v)
    return 1.0 - w, a * v, a * f0, a * f1


def under(row, last_vector):
    _, sub = iotas()
    return jnp.where(sub == 0, row, pltpu.roll(last_vector, 1, 0))


def over(row, first_vector):
    _, sub = iotas()
    return jnp.where(sub == 7, row, pltpu.roll(first_vector, 7, 0))


def put(todo):
    for ref, c, i, value in todo:
        ref[c, i] = value


def halo_rows(ref, S, low, high, get):
    todo = []
    for c in range(2):
        for q in range(2):
            todo.append((ref, c, q, under(low(2 * c + q), get(c, S - 2 + q))))
            todo.append((ref, c, S + 2 + q, over(high(2 * c + q), get(c, q))))
    return todo


def halo_coefficients(cos, S, low, high, get):
    below = coefficients(*[under(low(4 + m), get(m, S - 1)) for m in range(4)])
    above = coefficients(*[over(high(4 + m), get(m, 0)) for m in range(4)])
    return [(cos, m, 0, below[m]) for m in range(4)] + [(cos, m, S + 1, above[m]) for m in range(4)]


def strip_kernel(n, own_ref, fl_ref, fr_ref, hl_ref, hr_ref, yh1, yh2, r_ref, edge, xs, ws, r1s, cos):
    S = n // 8
    lane, sub = iotas()
    slot = lane & 3
    outer = (slot == 0) | (slot == 3)
    sign = jnp.where(slot == 1, -0.25, 0.25)

    low_n = lax.broadcasted_iota(jnp.int32, (n, 128), 1) & 3 < 2
    al, ar, bl, br = [ref[k, 0:n, :] for k in range(2) for ref in (fl_ref, fr_ref)]
    r_ref[0] = jnp.where(low_n, al, ar)
    r_ref[1] = jnp.where(low_n, pltpu.roll(al, 126, 1), pltpu.roll(ar, 2, 1))
    for k in range(3):
        a = bl if k == 1 else pltpu.roll(bl, (1 - k) & 127, 1)
        b = br if k == 2 else pltpu.roll(br, (2 - k) & 127, 1)
        r_ref[2 + k] = jnp.where(low_n, a, b)
    r_ref[5] = jnp.where(low_n, hl_ref[0:n, :], hr_ref[0:n, :])
    heat_rows = jnp.where(slot < 2, hl_ref[n : n + 8, :], hr_ref[n : n + 8, :])
    for k in range(2):
        tile = jnp.where(slot < 2, fl_ref[k, n : n + 8, :], fr_ref[k, n : n + 8, :])
        edge[k] = jnp.where(sub == 7, heat_rows[k : k + 1, :], tile)
        edge[2 + k] = jnp.where(outer, tile, own_ref[k, n : n + 8, :])

    def low(k):
        return edge[0, k : k + 1, :]

    def high(k):
        return edge[1, k : k + 1, :]

    def get(m, i):
        return r_ref[2 + m, pl.ds(i, 8, stride=S), :]

    def load(start, m):
        todo = []
        for i in [start + j for j in range(m)]:
            for c in range(2):
                r = r_ref[c, pl.ds(i, 8, stride=S), :]
                todo.append((xs, c, i + 2, r))
                todo.append((ws, c, i + 2, jnp.where(outer, r, own_ref[c, pl.ds(i, 8, stride=S), :])))
            co = coefficients(*[get(q, i) for q in range(4)])
            todo += [(cos, q, i + 1, co[q]) for q in range(4)]
        put(todo)

    over_rows(0, S, load)
    def row_low(k):
        return edge[2, k : k + 1, :]

    def row_high(k):
        return edge[3, k : k + 1, :]

    def get_r(c, i):
        return r_ref[c, pl.ds(i, 8, stride=S), :]

    def get_w(c, i):
        return jnp.where(outer, get_r(c, i), own_ref[c, pl.ds(i, 8, stride=S), :])

    put(
        halo_rows(xs, S, low, high, get_r)
        + halo_rows(ws, S, row_low, row_high, get_w)
        + halo_coefficients(cos, S, low, high, get)
    )

    def relax(start, m):
        r = [[xs[c, start + 1 + j] for c in range(2)] for j in range(m + 2)]
        w = [[ws[c, start + 1 + j] for c in range(2)] for j in range(m + 2)]
        todo = []
        for j in range(m):
            i = start + j
            for c in range(2):
                q = 0.25 * (w[j + 2][1 - c] - w[j][1 - c])
                around = (
                    r[j][c] + r[j + 2][c] + pltpu.roll(w[j + 1][c] + q, 127, 1) + pltpu.roll(w[j + 1][c] - q, 1, 1)
                )
                todo.append((yh1, c, i + 1, r[j + 1][c] + sign * (r[j + 2][1 - c] - r[j][1 - c])))
                new = cos[0, i + 1] * r[j + 1][c] + cos[2 + c, i + 1] + cos[1, i + 1] * around
                todo.append((r1s, c, i + 1, new))
        put(todo)

    over_rows(-1, S + 1, relax, 17)

    def edges(start, m):
        r = [[r1s[c, start + j] for c in range(2)] for j in range(m + 2)]
        put(
            [
                (yh2, c, start + j, r[j + 1][c] + sign * (r[j + 2][1 - c] - r[j][1 - c]))
                for j in range(m)
                for c in range(2)
            ]
        )

    over_rows(0, S, edges, 16)


def strips(own, fl, fr, hl, hr):
    n = own.shape[1] - 8
    S = n // 8
    return pl.pallas_call(
        functools.partial(strip_kernel, n),
        grid=(1,),
        in_specs=[whole(own.shape), whole(fl.shape), whole(fr.shape), whole(hl.shape), whole(hr.shape)],
        out_specs=[whole((2, S + 2, 8, 128)), whole((2, S, 8, 128))],
        out_shape=[
            jax.ShapeDtypeStruct((2, S + 2, 8, 128), F32),
            jax.ShapeDtypeStruct((2, S, 8, 128), F32),
        ],
        scratch_shapes=[
            pltpu.VMEM((6, n, 128), F32),
            pltpu.VMEM((4, 8, 128), F32),
            pltpu.VMEM((2, S + 4, 8, 128), F32),
            pltpu.VMEM((2, S + 4, 8, 128), F32),
            pltpu.VMEM((2, S + 2, 8, 128), F32),
            pltpu.VMEM((4, S + 2, 8, 128), F32),
        ],
        compiler_params=pltpu.CompilerParams(vmem_limit_bytes=57 * MIB),
        cost_estimate=pl.CostEstimate(flops=60 * n * 128, bytes_accessed=60 * n * 128, transcendentals=n * 128),
        name="strips",
    )(own, fl, fr, hl, hr)


def sweep_kernel(tb, n, v_ref, f_ref, p_ref, h_ref, lo_ref, hi_ref, row_ref, yh1, yh2, out_ref, xs, v1s, cos):
    S = n // 8
    step = pl.program_id(0)
    lane, _ = iotas()
    first, last = lane == 0, lane == 127

    def layer(u, _):
        t = step * tb + u
        shift = (126 - 4 * t) & 127

        def low(k):
            return row_ref[0, pl.ds(t, 1), :] if k == 7 else lo_ref[t, k : k + 1, :]

        def high(k):
            return row_ref[1, pl.ds(t, 1), :] if k == 7 else hi_ref[t, k : k + 1, :]

        def get(m, i):
            rows = pl.ds(i, 8, stride=S)
            if m < 2:
                return f_ref[m, u, rows, :]
            return 1.0 - p_ref[u, rows, :].astype(F32) if m == 2 else h_ref[u, rows, :]

        def load(start, m):
            todo = []
            for i in [start + j for j in range(m)]:
                todo += [(xs, c, i + 2, v_ref[c, u, pl.ds(i, 8, stride=S), :]) for c in range(2)]
                co = coefficients(*[get(q, i) for q in range(4)])
                todo += [(cos, q, i + 1, co[q]) for q in range(4)]
            put(todo)

        def sweep(src, off, yh, start, m, store):
            x = [[src[c, start + off + j] for c in range(2)] for j in range(m + 2)]
            for j in range(m):
                i = start + j
                prev, here, after = x[j], x[j + 1], x[j + 2]
                q = [0.25 * (after[c] - prev[c]) for c in range(2)]
                k, g = cos[0, i + 1], cos[1, i + 1]
                for c in range(2):
                    edge = pltpu.roll(yh[c, i + off], shift, 1)
                    up = jnp.where(first, edge, here[c] + q[1 - c])
                    down = jnp.where(last, edge, here[c] - q[1 - c])
                    around = prev[c] + after[c] + (pltpu.roll(up, 127, 1) + pltpu.roll(down, 1, 1))
                    store(c, i, k * here[c] + cos[2 + c, i + 1] + g * around)

        def keep(c, i, value):
            v1s[c, i + 1] = value

        def give(c, i, value):
            out_ref[c, u, pl.ds(i, 8, stride=S), :] = value

        def first_sweep(start, m):
            sweep(xs, 1, yh1, start, m, keep)

        def second_sweep(start, m):
            sweep(v1s, 0, yh2, start, m, give)

        put(
            halo_rows(xs, S, low, high, lambda c, i: v_ref[c, u, pl.ds(i, 8, stride=S), :])
            + halo_coefficients(cos, S, low, high, get)
        )
        over_rows(0, S, load, 8)
        over_rows(-1, S + 1, first_sweep, 17)
        over_rows(0, S, second_sweep, 8)
        return 0

    lax.fori_loop(0, tb, layer, 0)


def sweeps(v, f, pinned, heated, lo, hi, heated_rows, yh1, yh2):
    _, T, n, _ = v.shape
    S = n // 8
    tb = 4
    return pl.pallas_call(
        functools.partial(sweep_kernel, tb, n),
        grid=(T // tb,),
        in_specs=[
            pl.BlockSpec((2, tb, n, 128), lambda t: (0, t, 0, 0)),
            pl.BlockSpec((2, tb, n, 128), lambda t: (0, t, 0, 0)),
            pl.BlockSpec((tb, n, 128), lambda t: (t, 0, 0)),
            pl.BlockSpec((tb, n, 128), lambda t: (t, 0, 0)),
            whole((T, 8, 128)),
            whole((T, 8, 128)),
            whole((2, T, 128)),
            whole((2, S + 2, 8, 128)),
            whole((2, S, 8, 128)),
        ],
        out_specs=pl.BlockSpec((2, tb, n, 128), lambda t: (0, t, 0, 0)),
        out_shape=jax.ShapeDtypeStruct((2, T, n, 128), F32),
        scratch_shapes=[
            pltpu.VMEM((2, S + 4, 8, 128), F32),
            pltpu.VMEM((2, S + 2, 8, 128), F32),
            pltpu.VMEM((4, S + 2, 8, 128), F32),
        ],
        compiler_params=pltpu.CompilerParams(vmem_limit_bytes=57 * MIB),
        cost_estimate=pl.CostEstimate(
            flops=60 * T * n * 128, bytes_accessed=32 * T * n * 128, transcendentals=T * n * 128
        ),
        name="sweeps",
    )(v, f, pinned, heated, lo, hi, heated_rows, yh1, yh2)


def shifted(up_going, down_going, axis):
    count = lax.axis_size(axis)
    up = [(i, i + 1) for i in range(count - 1)]
    down = [(j, i) for i, j in up]
    return lax.ppermute(up_going, axis, up), lax.ppermute(down_going, axis, down)


def local(prior, d, v, f, pinned):
    J = lax.axis_size("wid")
    lo, hi = edge_rows(v, f, pinned)
    from_below, from_above = shifted(hi, lo, "wid")
    seg, pq = moments(d, prior)
    pqs = [pq] + [lax.ppermute(pq, "wid", [(i, (i + s) % J) for i in range(J)]) for s in range(1, J)]
    own, right, left = pack(v, f, pinned, from_below, from_above, pq)
    right, left, *pqs = lax.optimization_barrier((right, left, *pqs))
    from_left, from_right = shifted(right, left, "len")
    heated, columns, heated_rows = heat(d, pqs, seg, prior)
    heat_left, heat_right = shifted(columns, columns, "len")
    yh1, yh2 = strips(own, from_left, from_right, heat_left, heat_right)
    flow = sweeps(v, f, pinned, heated, from_below, from_above, heated_rows, yh1, yh2)
    return heated, flow


def solution(mesh):
    in_specs = (
        P(None, "wid", "len"),
        P(None, "len"),
        P(None, None, "wid", "len"),
        P(None, None, "wid", "len"),
        P(None, "wid", "len"),
    )
    out_specs = (P(None, "wid", "len"), P(None, None, "wid", "len"))
    return jax.shard_map(local, mesh=mesh, in_specs=in_specs, out_specs=out_specs, check_vma=False)
```

```python
import functools

import jax
import jax.numpy as jnp
from jax import lax
from jax.experimental import pallas as pl
from jax.experimental.pallas import tpu as pltpu
from jax.sharding import PartitionSpec as P

DRAG_COEFF = 0.5
RELAX_FACTOR = 0.8
HALF_LOG2E = -0.7213475204444817
F32 = jnp.float32
MIB = 1 << 20


def decay(d):
    x = 1.0 / d
    one_less = jnp.sqrt(x + 0.25 * x * x) - 0.5 * x
    r = 1.0 - one_less
    return r, (1.0 - r) / (1.0 + r)


def power(r, n):
    out = None
    while n:
        if n & 1:
            out = r if out is None else out * r
        n >>= 1
        if n:
            r = r * r
    return out


def sublane_powers(r, shape):
    s = lax.broadcasted_iota(jnp.int32, shape, 0)
    r2 = r * r
    r4 = r2 * r2
    one = jnp.ones(shape, F32)
    return (
        jnp.where((s & 1) != 0, r, one)
        * jnp.where((s & 2) != 0, r2, one)
        * jnp.where((s & 4) != 0, r4, one)
    )


def reciprocal(x):
    y = pl.reciprocal(x, approx=True)
    return y * (2.0 - x * y)


def batches(lo, hi, most=11):
    parts = -(-(hi - lo) // most)
    cuts = [lo + (hi - lo) * k // parts for k in range(parts + 1)]
    return [range(a, b) for a, b in zip(cuts, cuts[1:])]


def over_rows(first, stop, body, most=8):
    count = stop - first
    m = max(k for k in range(1, most + 1) if count % k == 0)

    def step(k, _):
        body(first + k * m, m)
        return 0

    lax.fori_loop(0, count // m, step, 0)


def iotas():
    lane = lax.broadcasted_iota(jnp.int32, (8, 128), 1)
    sub = lax.broadcasted_iota(jnp.int32, (8, 128), 0)
    return lane, sub


def moments_kernel(tb, n, d_ref, f_ref, seg_ref, pq_ref):
    S = n // 8
    base = pl.program_id(0) * tb
    G = 4
    for g in range(tb // G):
        rs = []
        for u in range(G):
            r, _ = decay(d_ref[pl.ds(base + g * G + u, 1), :])
            rs.append(jnp.broadcast_to(r, (8, 128)))
        fwd = [f_ref[g * G + u, pl.ds(0, 8, stride=S), :] for u in range(G)]
        bwd, weight = list(fwd), list(rs)
        for i in range(1, S):
            for u in range(G):
                x = f_ref[g * G + u, pl.ds(i, 8, stride=S), :]
                fwd[u] = fwd[u] * rs[u] + x
                bwd[u] = bwd[u] + weight[u] * x
                weight[u] = weight[u] * rs[u]
        for u in range(G):
            k = g * G + u
            seg_ref[0, k] = fwd[u]
            seg_ref[1, k] = bwd[u]
            rS = power(rs[u], S)
            up = sublane_powers(rS, (8, 128))
            s = lax.broadcasted_iota(jnp.int32, (8, 128), 0)
            rS2 = rS * rS
            one = jnp.ones((8, 128), F32)
            down = (
                jnp.where((s & 1) == 0, rS, one)
                * jnp.where((s & 2) == 0, rS2, one)
                * jnp.where((s & 4) == 0, rS2 * rS2, one)
            )
            pq_ref[0, k : k + 1, :] = jnp.sum(fwd[u] * down, axis=0, keepdims=True)
            pq_ref[1, k : k + 1, :] = jnp.sum(bwd[u] * up, axis=0, keepdims=True)


def moments(d, prior):
    T, n, _ = prior.shape
    tb = 8
    return pl.pallas_call(
        functools.partial(moments_kernel, tb, n),
        grid=(T // tb,),
        in_specs=[
            pl.BlockSpec((T, 128), lambda t: (0, 0)),
            pl.BlockSpec((tb, n, 128), lambda t: (t, 0, 0)),
        ],
        out_specs=[
            pl.BlockSpec((2, tb, 8, 128), lambda t: (0, t, 0, 0)),
            pl.BlockSpec((2, tb, 128), lambda t: (0, t, 0)),
        ],
        out_shape=[
            jax.ShapeDtypeStruct((2, T, 8, 128), F32),
            jax.ShapeDtypeStruct((2, T, 128), F32),
        ],
        compiler_params=pltpu.CompilerParams(vmem_limit_bytes=57 * MIB),
        cost_estimate=pl.CostEstimate(flops=4 * T * n * 128, bytes_accessed=4 * T * n * 128, transcendentals=0),
        name="moments",
    )(d, prior)


def rows_kernel(T, v_lo, v_hi, f_lo, f_hi, p_lo, p_hi, lo_ref, hi_ref):
    _, sub = iotas()

    def stack(v0, v1, f0, f1, fr):
        out = jnp.where(sub < 2, v0, v1)
        out = jnp.where(sub >= 4, f0, out)
        out = jnp.where(sub >= 5, f1, out)
        out = jnp.where(sub >= 6, fr, out)
        return jnp.where(sub >= 7, 0.0, out)

    for v, f, p, out, shifts in (
        (v_lo, f_lo, p_lo, lo_ref, (0, 2, 4, 5, 6)),
        (v_hi, f_hi, p_hi, hi_ref, (2, 4, 5, 6, 7)),
    ):
        for t in range(T):
            raw = [v[0, t], v[1, t], f[0, t], f[1, t], 1.0 - p[t].astype(F32)]
            out[t] = stack(*[pltpu.roll(x, q, 0) if q else x for x, q in zip(raw, shifts)])


def whole(shape):
    return pl.BlockSpec(shape, lambda t: (0,) * len(shape))


def edge_rows(v, f, pinned):
    _, T, n, _ = v.shape
    row = jax.ShapeDtypeStruct((T, 8, 128), F32)
    end = n // 8 - 1
    four = [pl.BlockSpec((2, T, 8, 128), lambda t, k=k: (0, 0, k, 0)) for k in (0, end)]
    three = [pl.BlockSpec((T, 8, 128), lambda t, k=k: (0, k, 0)) for k in (0, end)]
    return pl.pallas_call(
        functools.partial(rows_kernel, T),
        grid=(1,),
        in_specs=[*four, *four, *three],
        out_specs=[whole((T, 8, 128))] * 2,
        out_shape=[row, row],
        compiler_params=pltpu.CompilerParams(vmem_limit_bytes=57 * MIB),
        cost_estimate=pl.CostEstimate(flops=0, bytes_accessed=48 * T * 8 * 128, transcendentals=0),
        name="edge_rows",
    )(v, v, f, f, pinned, pinned)


def gather_columns(ref, T):
    lane, _ = iotas()
    parts = [jnp.where(lane >> 2 == t, pltpu.roll(ref[t], (4 * t + 2) & 127, 1), 0.0) for t in range(T)]
    while len(parts) > 1:
        parts = [p + q for p, q in zip(parts[::2], parts[1::2])]
    return parts[0]


def pack_kernel(tb, n, T, v_ref, f_ref, p_ref, lo_ref, hi_ref, after_ref, pk_ref, right_ref, left_ref, fp_ref):
    base = pl.program_id(0) * tb
    lane = lax.broadcasted_iota(jnp.int32, (n, 128), 1)
    group = lane >> 2
    for k in range(5):
        ref, q = (pk_ref, k) if k < 2 else (fp_ref, k - 2)
        acc = ref[q, 0:n, :]
        for u in range(tb):
            if k < 2:
                x = v_ref[k, u]
            elif k < 4:
                x = f_ref[k - 2, u]
            else:
                x = 1.0 - p_ref[u].astype(F32)
            t = base + u
            acc = jnp.where(group == t, pltpu.roll(x, (4 * t + 2) & 127, 1), acc)
        ref[q, 0:n, :] = acc

    @pl.when(pl.program_id(0) == pl.num_programs(0) - 1)
    def _():
        slot = lane & 3
        v0, v1 = pk_ref[0, 0:n, :], pk_ref[1, 0:n, :]
        f0, f1, fr = fp_ref[0], fp_ref[1], fp_ref[2]

        def sel(a, b, c):
            return jnp.where(slot < 1, a, jnp.where(slot == 1, b, c))

        right_ref[0, 0:n, :] = jnp.where(slot < 2, v0, pltpu.roll(v1, 2, 1))
        left_ref[0, 0:n, :] = jnp.where(slot >= 2, v0, pltpu.roll(v1, 126, 1))
        right_ref[1, 0:n, :] = sel(pltpu.roll(f0, 127, 1), f1, pltpu.roll(fr, 1, 1))
        left_ref[1, 0:n, :] = sel(pltpu.roll(f0, 126, 1), pltpu.roll(f1, 127, 1), fr)
        for k, ref in ((0, lo_ref), (1, hi_ref)):
            tile = gather_columns(ref, T)
            for out in (pk_ref, right_ref, left_ref):
                out[k, n : n + 8, :] = tile


def pack(v, f, pinned, lo, hi, after):
    _, T, n, _ = v.shape
    tb = 4
    out = jax.ShapeDtypeStruct((2, n + 8, 128), F32)
    return pl.pallas_call(
        functools.partial(pack_kernel, tb, n, T),
        grid=(T // tb,),
        in_specs=[
            pl.BlockSpec((2, tb, n, 128), lambda t: (0, t, 0, 0)),
            pl.BlockSpec((2, tb, n, 128), lambda t: (0, t, 0, 0)),
            pl.BlockSpec((tb, n, 128), lambda t: (t, 0, 0)),
            whole((T, 8, 128)),
            whole((T, 8, 128)),
            pl.BlockSpec(memory_space=pl.ANY),
        ],
        out_specs=[whole((2, n + 8, 128))] * 3,
        out_shape=[out, out, out],
        scratch_shapes=[pltpu.VMEM((3, n, 128), F32)],
        compiler_params=pltpu.CompilerParams(vmem_limit_bytes=57 * MIB),
        cost_estimate=pl.CostEstimate(flops=5 * T * n * 128, bytes_accessed=20 * T * n * 128, transcendentals=0),
        name="pack_edges",
    )(v, f, pinned, lo, hi, after)


def heat_kernel(J, tb, n, *refs):
    d_ref, *pq_refs = refs[: J + 1]
    (
        seg_ref, f_ref,
        out_ref, send_ref, row_ref, alls, sums, ys,
    ) = refs[J + 1 :]
    S = n // 8
    step = pl.program_id(0)
    base = step * tb

    @pl.when(step == 0)
    def _():
        j = lax.axis_index("wid")
        for s in range(J):
            alls[lax.rem(j - s + J, J)] = pq_refs[s][...]
        r, _ = decay(d_ref[...])
        rn = power(r, n)
        rN = power(rn, J)
        sp = alls[0, 0]
        for i in range(1, J):
            sp = sp * rn + alls[i, 0]
        sq = alls[J - 1, 1]
        for i in range(J - 2, -1, -1):
            sq = sq * rn + alls[i, 1]
        inv = 1.0 / (1.0 - rN * rN)
        left = (sq + rN * sp) * inv
        right = (sp + rN * sq) * inv
        for i in range(J - 1):
            left = jnp.where(i < j, rn * left + alls[i, 0], left)
        for i in range(J - 1, 0, -1):
            right = jnp.where(i > j, rn * right + alls[i, 1], right)
        sums[0] = left
        sums[1] = right

    _, sub = iotas()
    rs, gain, y, z = [], [], [], []
    for u in range(tb):
        t = base + u
        r, a0 = decay(d_ref[pl.ds(t, 1), :])
        r = jnp.broadcast_to(r, (8, 128))
        a0 = jnp.broadcast_to(a0, (8, 128))
        rS = power(r, S)
        rS2 = rS * rS
        rS4 = rS2 * rS2
        c = jnp.where(sub == 0, sums[0, pl.ds(t, 1), :], pltpu.roll(seg_ref[0, u], 1, 0))
        b = jnp.where(sub == 7, sums[1, pl.ds(t, 1), :], pltpu.roll(seg_ref[1, u], 7, 0))
        for s, q in ((1, rS), (2, rS2), (4, rS4)):
            c = c + q * jnp.where(sub >= s, pltpu.roll(c, s, 0), 0.0)
            b = b + q * jnp.where(sub < 8 - s, pltpu.roll(b, 8 - s, 0), 0.0)
        rs.append(r)
        gain.append(a0)
        y.append(c)
        z.append(b)
    for rows in batches(0, S, 8):
        done = []
        for i in rows:
            for u in range(tb):
                y[u] = y[u] * rs[u] + f_ref[u, pl.ds(i, 8, stride=S), :]
                done.append((u, i, y[u]))
        for u, i, value in done:
            ys[u, i] = value
    for rows in batches(0, S, 8)[::-1]:
        done = []
        for i in rows[::-1]:
            for u in range(tb):
                zr = z[u] * rs[u]
                done.append((u, i, gain[u] * (ys[u, i] + zr)))
                z[u] = zr + f_ref[u, pl.ds(i, 8, stride=S), :]
        for u, i, value in done:
            out_ref[u, pl.ds(i, 8, stride=S), :] = value

    lane_n = lax.broadcasted_iota(jnp.int32, (n, 128), 1)
    group = lane_n >> 2
    acc = send_ref[0:n, :]
    tile = send_ref[n : n + 8, :]
    lane, _ = iotas()
    rows = []
    for u in range(tb):
        t = base + u
        acc = jnp.where(group == t, pltpu.roll(out_ref[u], (4 * t + 2) & 127, 1), acc)
        below = gain[u][0:1] * (sums[0, pl.ds(t, 1), :] + rs[u][0:1] * z[u][0:1])
        above = gain[u][0:1] * (sums[1, pl.ds(t, 1), :] + rs[u][0:1] * y[u][7:8])
        both = jnp.where(sub == 0, below, above)
        rows.append((u, below, above))
        tile = jnp.where(lane >> 2 == t, pltpu.roll(both, (4 * t + 2) & 127, 1), tile)
    send_ref[0:n, :] = acc
    send_ref[n : n + 8, :] = tile
    for u, below, above in rows:
        row_ref[0, pl.ds(base + u, 1), :] = below
        row_ref[1, pl.ds(base + u, 1), :] = above


def heat(d, pqs, seg, prior):
    T, n, _ = prior.shape
    J = len(pqs)
    tb = 4
    return pl.pallas_call(
        functools.partial(heat_kernel, J, tb, n),
        grid=(T // tb,),
        in_specs=[
            whole((T, 128)),
            *[whole((2, T, 128)) for _ in range(J)],
            pl.BlockSpec((2, tb, 8, 128), lambda t: (0, t, 0, 0)),
            pl.BlockSpec((tb, n, 128), lambda t: (t, 0, 0)),
        ],
        out_specs=[
            pl.BlockSpec((tb, n, 128), lambda t: (t, 0, 0)),
            whole((n + 8, 128)),
            whole((2, T, 128)),
        ],
        out_shape=[
            jax.ShapeDtypeStruct((T, n, 128), F32),
            jax.ShapeDtypeStruct((n + 8, 128), F32),
            jax.ShapeDtypeStruct((2, T, 128), F32),
        ],
        scratch_shapes=[
            pltpu.VMEM((J, 2, T, 128), F32),
            pltpu.VMEM((2, T, 128), F32),
            pltpu.VMEM((tb, n // 8, 8, 128), F32),
        ],
        compiler_params=pltpu.CompilerParams(vmem_limit_bytes=57 * MIB),
        cost_estimate=pl.CostEstimate(flops=10 * T * n * 128, bytes_accessed=8 * T * n * 128, transcendentals=0),
        name="heat",
    )(d, *pqs, seg, prior)


def coefficients(f0, f1, free, heated):
    v = jnp.exp2(HALF_LOG2E * heated)
    w = RELAX_FACTOR * free
    a = w * reciprocal(DRAG_COEFF + 4.0 * v)
    return 1.0 - w, a * v, a * f0, a * f1


def under(row, last_vector):
    _, sub = iotas()
    return jnp.where(sub == 0, row, pltpu.roll(last_vector, 1, 0))


def over(row, first_vector):
    _, sub = iotas()
    return jnp.where(sub == 7, row, pltpu.roll(first_vector, 7, 0))


def put(todo):
    for ref, c, i, value in todo:
        ref[c, i] = value


def halo_rows(ref, S, low, high, get):
    todo = []
    for c in range(2):
        for q in range(2):
            todo.append((ref, c, q, under(low(2 * c + q), get(c, S - 2 + q))))
            todo.append((ref, c, S + 2 + q, over(high(2 * c + q), get(c, q))))
    return todo


def halo_coefficients(cos, S, low, high, get):
    below = coefficients(*[under(low(4 + m), get(m, S - 1)) for m in range(4)])
    above = coefficients(*[over(high(4 + m), get(m, 0)) for m in range(4)])
    return [(cos, m, 0, below[m]) for m in range(4)] + [(cos, m, S + 1, above[m]) for m in range(4)]


def strip_kernel(n, own_ref, fl_ref, fr_ref, hl_ref, hr_ref, yh1, yh2, r_ref, edge, xs, ws, r1s, cos):
    S = n // 8
    lane, sub = iotas()
    slot = lane & 3
    outer = (slot == 0) | (slot == 3)
    sign = jnp.where(slot == 1, -0.25, 0.25)

    low_n = lax.broadcasted_iota(jnp.int32, (n, 128), 1) & 3 < 2
    al, ar, bl, br = [ref[k, 0:n, :] for k in range(2) for ref in (fl_ref, fr_ref)]
    r_ref[0] = jnp.where(low_n, al, ar)
    r_ref[1] = jnp.where(low_n, pltpu.roll(al, 126, 1), pltpu.roll(ar, 2, 1))
    for k in range(3):
        a = bl if k == 1 else pltpu.roll(bl, (1 - k) & 127, 1)
        b = br if k == 2 else pltpu.roll(br, (2 - k) & 127, 1)
        r_ref[2 + k] = jnp.where(low_n, a, b)
    r_ref[5] = jnp.where(low_n, hl_ref[0:n, :], hr_ref[0:n, :])
    heat_rows = jnp.where(slot < 2, hl_ref[n : n + 8, :], hr_ref[n : n + 8, :])
    for k in range(2):
        tile = jnp.where(slot < 2, fl_ref[k, n : n + 8, :], fr_ref[k, n : n + 8, :])
        edge[k] = jnp.where(sub == 7, heat_rows[k : k + 1, :], tile)
        edge[2 + k] = jnp.where(outer, tile, own_ref[k, n : n + 8, :])

    def low(k):
        return edge[0, k : k + 1, :]

    def high(k):
        return edge[1, k : k + 1, :]

    def get(m, i):
        return r_ref[2 + m, pl.ds(i, 8, stride=S), :]

    def load(start, m):
        todo = []
        for i in [start + j for j in range(m)]:
            for c in range(2):
                r = r_ref[c, pl.ds(i, 8, stride=S), :]
                todo.append((xs, c, i + 2, r))
                todo.append((ws, c, i + 2, jnp.where(outer, r, own_ref[c, pl.ds(i, 8, stride=S), :])))
            co = coefficients(*[get(q, i) for q in range(4)])
            todo += [(cos, q, i + 1, co[q]) for q in range(4)]
        put(todo)

    over_rows(0, S, load)
    def row_low(k):
        return edge[2, k : k + 1, :]

    def row_high(k):
        return edge[3, k : k + 1, :]

    def get_r(c, i):
        return r_ref[c, pl.ds(i, 8, stride=S), :]

    def get_w(c, i):
        return jnp.where(outer, get_r(c, i), own_ref[c, pl.ds(i, 8, stride=S), :])

    put(
        halo_rows(xs, S, low, high, get_r)
        + halo_rows(ws, S, row_low, row_high, get_w)
        + halo_coefficients(cos, S, low, high, get)
    )

    def relax(start, m):
        r = [[xs[c, start + 1 + j] for c in range(2)] for j in range(m + 2)]
        w = [[ws[c, start + 1 + j] for c in range(2)] for j in range(m + 2)]
        todo = []
        for j in range(m):
            i = start + j
            for c in range(2):
                q = 0.25 * (w[j + 2][1 - c] - w[j][1 - c])
                around = (
                    r[j][c] + r[j + 2][c] + pltpu.roll(w[j + 1][c] + q, 127, 1) + pltpu.roll(w[j + 1][c] - q, 1, 1)
                )
                todo.append((yh1, c, i + 1, r[j + 1][c] + sign * (r[j + 2][1 - c] - r[j][1 - c])))
                new = cos[0, i + 1] * r[j + 1][c] + cos[2 + c, i + 1] + cos[1, i + 1] * around
                todo.append((r1s, c, i + 1, new))
        put(todo)

    over_rows(-1, S + 1, relax, 17)

    def edges(start, m):
        r = [[r1s[c, start + j] for c in range(2)] for j in range(m + 2)]
        put(
            [
                (yh2, c, start + j, r[j + 1][c] + sign * (r[j + 2][1 - c] - r[j][1 - c]))
                for j in range(m)
                for c in range(2)
            ]
        )

    over_rows(0, S, edges, 16)


def strips(own, fl, fr, hl, hr):
    n = own.shape[1] - 8
    S = n // 8
    return pl.pallas_call(
        functools.partial(strip_kernel, n),
        grid=(1,),
        in_specs=[whole(own.shape), whole(fl.shape), whole(fr.shape), whole(hl.shape), whole(hr.shape)],
        out_specs=[whole((2, S + 2, 8, 128)), whole((2, S, 8, 128))],
        out_shape=[
            jax.ShapeDtypeStruct((2, S + 2, 8, 128), F32),
            jax.ShapeDtypeStruct((2, S, 8, 128), F32),
        ],
        scratch_shapes=[
            pltpu.VMEM((6, n, 128), F32),
            pltpu.VMEM((4, 8, 128), F32),
            pltpu.VMEM((2, S + 4, 8, 128), F32),
            pltpu.VMEM((2, S + 4, 8, 128), F32),
            pltpu.VMEM((2, S + 2, 8, 128), F32),
            pltpu.VMEM((4, S + 2, 8, 128), F32),
        ],
        compiler_params=pltpu.CompilerParams(vmem_limit_bytes=12 * MIB),
        cost_estimate=pl.CostEstimate(flops=60 * n * 128, bytes_accessed=60 * n * 128, transcendentals=n * 128),
        name="strips",
    )(own, fl, fr, hl, hr)


def sweep_kernel(tb, n, v_ref, f_ref, p_ref, h_ref, lo_ref, hi_ref, row_ref, yh1, yh2, out_ref, xs, v1s, cos):
    S = n // 8
    step = pl.program_id(0)
    lane, _ = iotas()
    first, last = lane == 0, lane == 127

    def layer(u, _):
        t = step * tb + u
        shift = (126 - 4 * t) & 127

        def low(k):
            return row_ref[0, pl.ds(t, 1), :] if k == 7 else lo_ref[t, k : k + 1, :]

        def high(k):
            return row_ref[1, pl.ds(t, 1), :] if k == 7 else hi_ref[t, k : k + 1, :]

        def get(m, i):
            rows = pl.ds(i, 8, stride=S)
            if m < 2:
                return f_ref[m, u, rows, :]
            return 1.0 - p_ref[u, rows, :].astype(F32) if m == 2 else h_ref[u, rows, :]

        def load(start, m):
            todo = []
            for i in [start + j for j in range(m)]:
                todo += [(xs, c, i + 2, v_ref[c, u, pl.ds(i, 8, stride=S), :]) for c in range(2)]
                co = coefficients(*[get(q, i) for q in range(4)])
                todo += [(cos, q, i + 1, co[q]) for q in range(4)]
            put(todo)

        def sweep(src, off, yh, start, m, store):
            x = [[src[c, start + off + j] for c in range(2)] for j in range(m + 2)]
            for j in range(m):
                i = start + j
                prev, here, after = x[j], x[j + 1], x[j + 2]
                q = [0.25 * (after[c] - prev[c]) for c in range(2)]
                k, g = cos[0, i + 1], cos[1, i + 1]
                for c in range(2):
                    edge = pltpu.roll(yh[c, i + off], shift, 1)
                    up = jnp.where(first, edge, here[c] + q[1 - c])
                    down = jnp.where(last, edge, here[c] - q[1 - c])
                    around = prev[c] + after[c] + (pltpu.roll(up, 127, 1) + pltpu.roll(down, 1, 1))
                    store(c, i, k * here[c] + cos[2 + c, i + 1] + g * around)

        def keep(c, i, value):
            v1s[c, i + 1] = value

        def give(c, i, value):
            out_ref[c, u, pl.ds(i, 8, stride=S), :] = value

        def first_sweep(start, m):
            sweep(xs, 1, yh1, start, m, keep)

        def second_sweep(start, m):
            sweep(v1s, 0, yh2, start, m, give)

        put(
            halo_rows(xs, S, low, high, lambda c, i: v_ref[c, u, pl.ds(i, 8, stride=S), :])
            + halo_coefficients(cos, S, low, high, get)
        )
        over_rows(0, S, load, 32)
        over_rows(-1, S + 1, first_sweep, 17)
        over_rows(0, S, second_sweep, 32)
        return 0

    lax.fori_loop(0, tb, layer, 0)


def sweeps(v, f, pinned, heated, lo, hi, heated_rows, yh1, yh2):
    _, T, n, _ = v.shape
    S = n // 8
    tb = 4
    return pl.pallas_call(
        functools.partial(sweep_kernel, tb, n),
        grid=(T // tb,),
        in_specs=[
            pl.BlockSpec((2, tb, n, 128), lambda t: (0, t, 0, 0)),
            pl.BlockSpec((2, tb, n, 128), lambda t: (0, t, 0, 0)),
            pl.BlockSpec((tb, n, 128), lambda t: (t, 0, 0)),
            pl.BlockSpec((tb, n, 128), lambda t: (t, 0, 0)),
            whole((T, 8, 128)),
            whole((T, 8, 128)),
            whole((2, T, 128)),
            whole((2, S + 2, 8, 128)),
            whole((2, S, 8, 128)),
        ],
        out_specs=pl.BlockSpec((2, tb, n, 128), lambda t: (0, t, 0, 0)),
        out_shape=jax.ShapeDtypeStruct((2, T, n, 128), F32),
        scratch_shapes=[
            pltpu.VMEM((2, S + 4, 8, 128), F32),
            pltpu.VMEM((2, S + 2, 8, 128), F32),
            pltpu.VMEM((4, S + 2, 8, 128), F32),
        ],
        compiler_params=pltpu.CompilerParams(vmem_limit_bytes=57 * MIB),
        cost_estimate=pl.CostEstimate(
            flops=60 * T * n * 128, bytes_accessed=32 * T * n * 128, transcendentals=T * n * 128
        ),
        name="sweeps",
    )(v, f, pinned, heated, lo, hi, heated_rows, yh1, yh2)


def shifted(up_going, down_going, axis):
    count = lax.axis_size(axis)
    up = [(i, i + 1) for i in range(count - 1)]
    down = [(j, i) for i, j in up]
    return lax.ppermute(up_going, axis, up), lax.ppermute(down_going, axis, down)


def local(prior, d, v, f, pinned):
    J = lax.axis_size("wid")
    lo, hi = edge_rows(v, f, pinned)
    from_below, from_above = shifted(hi, lo, "wid")
    seg, pq = moments(d, prior)
    pqs = [pq] + [lax.ppermute(pq, "wid", [(i, (i + s) % J) for i in range(J)]) for s in range(1, J)]
    own, right, left = pack(v, f, pinned, from_below, from_above, pq)
    right, left, *pqs = lax.optimization_barrier((right, left, *pqs))
    from_left, from_right = shifted(right, left, "len")
    heated, columns, heated_rows = heat(d, pqs, seg, prior)
    heat_left, heat_right = shifted(columns, columns, "len")
    yh1, yh2 = strips(own, from_left, from_right, heat_left, heat_right)
    flow = sweeps(v, f, pinned, heated, from_below, from_above, heated_rows, yh1, yh2)
    return heated, flow


def solution(mesh):
    in_specs = (
        P(None, "wid", "len"),
        P(None, "len"),
        P(None, None, "wid", "len"),
        P(None, None, "wid", "len"),
        P(None, "wid", "len"),
    )
    out_specs = (P(None, "wid", "len"), P(None, None, "wid", "len"))
    return jax.shard_map(local, mesh=mesh, in_specs=in_specs, out_specs=out_specs, check_vma=False)
```
